32 devices in a mesh: heads: 2 (over y), seq: 16 (over z, x, core).
Axes of the slice: x: 2, y: 2, z: 4, core: 2. Of those that a mesh axis runs over, the one named last changes fastest.
Arguments:
- inputs: bfloat16 [2, 16, 256, 1024], P(None, 'seq', 'heads'), may hold values from -6 to 6
- cotangent: bfloat16 [2, 16, 256, 1024], P(None, 'seq', 'heads'), may hold values from -6 to 6
- attn_gain: float32 [1024], replicated, may hold values from 0.25 to 1.75
- w_query: bfloat16 [1024, 1024], P(('heads', 'seq')), may hold values from -0.1875 to 0.1875
- w_key: bfloat16 [1024, 512], P(('heads', 'seq')), may hold values from -0.1875 to 0.1875
- w_value: bfloat16 [1024, 512], P(('heads', 'seq')), may hold values from -0.1875 to 0.1875
- w_output: bfloat16 [1024, 1024], P(('heads', 'seq')), may hold values from -1 to 1
- query_gain: float32 [64], replicated, may hold values from 0.25 to 1.75
- key_gain: float32 [64], replicated, may hold values from 0.25 to 1.75
- ffn_gain: float32 [1024], replicated, may hold values from 0.25 to 1.75
- w_gate: bfloat16 [1024, 4608], P(('heads', 'seq')), may hold values from -0.1875 to 0.1875
- w_up: bfloat16 [1024, 4608], P(('heads', 'seq')), may hold values from -0.1875 to 0.1875
- w_down: bfloat16 [4608, 1024], P(('heads', 'seq')), may hold values from -0.09375 to 0.09375
- doc_starts: int32 [2, 3], replicated, may hold values from 0 to 3072, as said below
Outputs:
- block_out: bfloat16 [2, 16, 256, 1024], P(None, 'seq', 'heads')
- grad_inputs: float32 [2, 16, 256, 1024], P(None, 'seq', 'heads')
- grad_attn_gain: float32 [1024], replicated
- grad_w_query: float32 [1024, 1024], P(('heads', 'seq'))
- grad_w_key: float32 [1024, 512], P(('heads', 'seq'))
- grad_w_value: float32 [1024, 512], P(('heads', 'seq'))
- grad_w_output: float32 [1024, 1024], P(('heads', 'seq'))
- grad_query_gain: float32 [64], replicated
- grad_key_gain: float32 [64], replicated
- grad_ffn_gain: float32 [1024], replicated
- grad_w_gate: float32 [1024, 4608], P(('heads', 'seq'))
- grad_w_up: float32 [1024, 4608], P(('heads', 'seq'))
- grad_w_down: float32 [4608, 1024], P(('heads', 'seq'))
The draws below stay inside these ranges and needn't reach their ends.
Inputs may be any that keep to these rules, and one draw needn't show every extreme that they name: `doc_starts`: each row holds the 3 document starts of one micro-batch, ascending, multiples of 1024, the first 0. In one micro-batch, drawn from the seed, all are 0 (one document spans the whole sequence); in every other one they are distinct and the last is the largest value allowed.
All inputs are finite; a program needn't handle non-finite values.
Results may differ from the reference program's by a relative error of at most 0.023.
Values may be sent and summed in bfloat16 or wider, within the bound.
No kernel may reach another device: no remote copies, remote signals or barrier semaphores. Data moves between devices by JAX's collectives and lax.ppermute only.
A program may use at most 192 MiB of HBM per device.

```python
import jax
import jax.numpy as jnp
from jax import lax

D = 1024
QHEADS = 16
KVHEADS = 8
HD = 64
FF = 4608
MB = 2
NDOC = 3
DOCMIN = 1024
QW = 1024
KW = 512
BLK = 256
SEQ_BLOCKS = 16
TOKENS = 4096


def draw_doc_starts(key, part):
    key = jax.random.fold_in(key, 7)
    slot_count = TOKENS // DOCMIN
    single = jax.random.randint(jax.random.fold_in(key, 1), (), 0, MB)
    all_rows = []
    for batch_index in range(MB):
        shuffled = jax.random.permutation(jax.random.fold_in(key, 10 + batch_index), slot_count - 2) + 1
        chosen = jnp.sort(shuffled[:NDOC - 2]).astype(jnp.int32)
        row_starts = jnp.concatenate([jnp.zeros((1,), jnp.int32), chosen, jnp.full((1,), slot_count - 1, jnp.int32)]) * DOCMIN
        row_starts = jnp.where(single == batch_index, jnp.zeros_like(row_starts), row_starts)
        all_rows.append(row_starts)
    return jnp.stack(all_rows).astype(jnp.int32)


def levels(key, extent, split, least, high):
    def one(axis_at, shards_of):
        steps = jax.random.uniform(jax.random.fold_in(jax.random.fold_in(key, 6), axis_at), (shards_of,), jnp.float32, least / len(split), high / len(split))
        return jnp.repeat(jnp.exp(steps), extent[axis_at] // shards_of).reshape((-1,) + (1,) * (len(extent) - axis_at - 1))

    loudness = one(*split[0])
    for cut in split[1:]:
        loudness = loudness * one(*cut)
    return loudness


def scatter_about(own_key, dims, spread, most, pieces=(), held_as=jnp.bfloat16):
    loudness = levels(own_key, dims, pieces, -0.22, 0.18) if pieces else 1.0
    entries = jax.random.normal(own_key, dims, jnp.float32) * spread * loudness
    return jnp.minimum(jnp.maximum(entries, -most), most).astype(held_as)


def setup_inputs(seed: int = 0) -> dict:
    arg_keys = jax.random.split(jax.random.key(seed), 15)
    return {
        "inputs": scatter_about(arg_keys[0], (MB, SEQ_BLOCKS, BLK, D), 1.0, 6.0, ((1, 16), (2, 2))),
        "cotangent": scatter_about(arg_keys[1], (MB, SEQ_BLOCKS, BLK, D), 1.0, 6.0, ((1, 16), (2, 2))),
        "attn_gain": jnp.clip(1.0 + 0.15 * jax.random.normal(arg_keys[2], (D,), jnp.float32), 0.25, 1.75),
        "w_query": scatter_about(arg_keys[3], (D, QW), D ** -0.5, 0.1875, ((0, 32),)),
        "w_key": scatter_about(arg_keys[4], (D, KW), D ** -0.5, 0.1875, ((0, 32),)),
        "w_value": scatter_about(arg_keys[5], (D, KW), D ** -0.5, 0.1875, ((0, 32),)),
        "w_output": scatter_about(arg_keys[6], (QW, D), (QW // 32) ** -0.5, 1.0, ((0, 32),)),
        "query_gain": jnp.clip(1.0 + 0.15 * jax.random.normal(arg_keys[7], (HD,), jnp.float32), 0.25, 1.75),
        "key_gain": jnp.clip(1.0 + 0.15 * jax.random.normal(arg_keys[8], (HD,), jnp.float32), 0.25, 1.75),
        "ffn_gain": jnp.clip(1.0 + 0.15 * jax.random.normal(arg_keys[9], (D,), jnp.float32), 0.25, 1.75),
        "w_gate": scatter_about(arg_keys[10], (D, FF), D ** -0.5, 0.1875, ((0, 32),)),
        "w_up": scatter_about(arg_keys[11], (D, FF), D ** -0.5, 0.1875, ((0, 32),)),
        "w_down": scatter_about(arg_keys[12], (FF, D), FF ** -0.5, 0.09375, ((0, 32),)),
        "doc_starts": draw_doc_starts(jax.random.fold_in(arg_keys[14], 71), 0),
    }


EPS = 1e-05
THETA = 1000000.0
NEG = -1e+30

@jax.custom_vjp
def low(v):
    return lax.optimization_barrier(v.astype(jnp.bfloat16)).astype(jnp.float32)

@jax.custom_vjp
def low_back(v):
    return v

def low_keep(v):
    return (low(v), None)

def low_pass(kept, grad):
    return (grad,)

def back_keep(v):
    return (v, None)

def back_low(kept, grad):
    return (low(grad),)
low.defvjp(low_keep, low_pass)
low_back.defvjp(back_keep, back_low)

def matmul(left_side, right_side):
    return jnp.dot(left_side, right_side, precision=lax.Precision.HIGHEST)

def rms_scale(values):
    return values * lax.rsqrt(lax.optimization_barrier(jnp.mean(values * values, axis=-1, keepdims=True)) + EPS)

def doc_begin(starts, token_pos):
    return lax.optimization_barrier(jnp.max(jnp.where(starts[None, :] <= token_pos[:, None], starts[None, :], 0), axis=1))

def rope_tables(positions, head_width):
    half_width = head_width // 2
    frequency = THETA ** (-(jnp.arange(half_width, dtype=jnp.float32) * 2.0 / head_width))
    angles = positions.astype(jnp.float32)[:, None] * frequency[None, :]
    return (jnp.cos(angles), jnp.sin(angles))

def rotate(values, cos_table, sin_table):
    half_width = values.shape[-1] // 2
    first_half = values[..., :half_width]
    second_half = values[..., half_width:]
    cos_rows = cos_table[:, None, :]
    sin_rows = sin_table[:, None, :]
    return jnp.concatenate([first_half * cos_rows - second_half * sin_rows, second_half * cos_rows + first_half * sin_rows], axis=-1)

def attend(query, key_rows, value_rows, begins):
    count = query.shape[0]
    block_width = min(512, count)
    groups = QHEADS // KVHEADS
    score_scale = HD ** (-0.5)
    grouped = query.reshape(count, KVHEADS, groups, HD)
    key_pos = jnp.arange(count, dtype=jnp.int32)

    def one_block(block_index):
        first_row = (block_index * block_width).astype(jnp.int32)
        query_rows = lax.dynamic_slice_in_dim(grouped, first_row, block_width, 0)
        row_pos = first_row + jnp.arange(block_width, dtype=jnp.int32)
        row_begin = lax.dynamic_slice_in_dim(begins, first_row, block_width, 0)
        scores = jnp.einsum('qkgd,tkd->kgqt', query_rows, key_rows, precision=lax.Precision.HIGHEST) * score_scale
        scores = low_back(scores)
        allowed = (key_pos[None, :] <= row_pos[:, None]) & (begins[None, :] == row_begin[:, None])
        scores = jnp.where(allowed, scores, NEG)
        probabilities = low(jax.nn.softmax(scores, axis=-1))
        return jnp.einsum('kgqt,tkd->qkgd', probabilities, value_rows, precision=lax.Precision.HIGHEST)
    blocks = lax.map(jax.checkpoint(one_block), jnp.arange(count // block_width, dtype=jnp.int32))
    return blocks.reshape(count, QHEADS * HD)

def block_forward(residual_in, starts, attn_gain, w_query, w_key, w_value, w_output, query_gain, key_gain, ffn_gain, w_gate, w_up, w_down):
    count = residual_in.shape[0]
    token_pos = jnp.arange(count, dtype=jnp.int32)
    begins = doc_begin(starts, token_pos)
    cos_table, sin_table = rope_tables(token_pos - begins, HD)
    normed = low(rms_scale(residual_in) * attn_gain)
    query_raw = low_back(matmul(normed, w_query)).reshape(count, QHEADS, HD)
    key_raw = low_back(matmul(normed, w_key)).reshape(count, KVHEADS, HD)
    value_raw = low_back(matmul(normed, w_value)).reshape(count, KVHEADS, HD)
    query = low(rotate(rms_scale(query_raw) * query_gain, cos_table, sin_table))
    key_rows = low(rotate(rms_scale(key_raw) * key_gain, cos_table, sin_table))
    value_rows = low(value_raw)
    attn = low_back(low(attend(query, key_rows, value_rows, begins)))
    middle = residual_in + low_back(matmul(attn, w_output))
    normed_two = low(rms_scale(middle) * ffn_gain)
    gate_proj = low_back(matmul(normed_two, w_gate))
    up_proj = low_back(matmul(normed_two, w_up))
    hidden = low(jax.nn.silu(gate_proj) * up_proj)
    return middle + low_back(matmul(hidden, w_down))

def reference(inputs, cotangent, attn_gain, w_query, w_key, w_value, w_output, query_gain, key_gain, ffn_gain, w_gate, w_up, w_down, doc_starts):
    params = tuple((item_array.astype(jnp.float32) for item_array in (attn_gain, w_query, w_key, w_value, w_output, query_gain, key_gain, ffn_gain, w_gate, w_up, w_down)))
    grad_totals = tuple((jnp.zeros_like(param_array) for param_array in params))
    out_list = []
    input_grads = []
    for batch_index in range(MB):
        starts = doc_starts[batch_index]

        def forward(residual_in, *weight_list):
            return block_forward(residual_in, starts, *weight_list)
        residual_in = inputs[batch_index].reshape(TOKENS, D).astype(jnp.float32)
        result, pullback = jax.vjp(forward, residual_in, *params)
        grad_parts = pullback(cotangent[batch_index].reshape(TOKENS, D).astype(jnp.float32))
        out_list.append(result.astype(jnp.bfloat16))
        input_grads.append(grad_parts[0])
        grad_totals = tuple((total_part + new_part for total_part, new_part in zip(grad_totals, grad_parts[1:])))
    block_out = jnp.stack(out_list).reshape(MB, SEQ_BLOCKS, BLK, D)
    grad_inputs = jnp.stack(input_grads).reshape(MB, SEQ_BLOCKS, BLK, D)
    return (block_out, grad_inputs, grad_totals[0], grad_totals[1], grad_totals[2], grad_totals[3], grad_totals[4], grad_totals[5], grad_totals[6], grad_totals[7], grad_totals[8], grad_totals[9], grad_totals[10])
```

```python
import functools
import math

import jax
import jax.numpy as jnp
from jax import lax
from jax.experimental import pallas as pl
from jax.experimental.pallas import tpu as pltpu
from jax.sharding import Mesh, PartitionSpec as P

EPS = 1e-05
THETA = 1000000.0
LANES = 128
LOG2E = math.log2(math.e)
GROUP = ("heads", "mid")
DATA = ("hi", "lo")
SEQ = ("hi", "mid", "lo")
ALL = ("heads",) + SEQ
BF = jnp.bfloat16
F32 = jnp.float32
VMEM_LIMIT = 48 * 1024 * 1024


def dot_plain(left_side, right_side):
    return jnp.dot(left_side, right_side, preferred_element_type=F32)


def dot_back(left_side, right_side):
    return lax.dot_general(
        left_side, right_side, (((1,), (1,)), ((), ())), preferred_element_type=F32
    )


def dot_outer(left_side, right_side):
    return lax.dot_general(
        left_side, right_side, (((0,), (0,)), ((), ())), preferred_element_type=F32
    )


def rms_inverse(values):
    return lax.rsqrt(jnp.mean(values * values, axis=-1, keepdims=True) + EPS)


def norm_back(values, gain_vec, upstream):
    inverse = rms_inverse(values)
    scaled = upstream * gain_vec
    inner_mean = jnp.mean(scaled * values, axis=-1, keepdims=True)
    grad_values = inverse * scaled - values * inverse * inverse * inverse * inner_mean
    return (grad_values, upstream * values * inverse)


def is_quad():
    return lax.axis_size("heads") == 2 and lax.axis_size("mid") == 2


def swap(part, axis):
    return lax.ppermute(part, axis, [(0, 1), (1, 0)])


def group_gather(part):
    if not is_quad():
        return lax.all_gather(part, GROUP, axis=0, tiled=False)
    half = part.shape[0] // 2
    by_mid = swap(part, "mid")
    by_heads = swap(part, "heads")
    far_low = swap(by_mid[:half], "heads")
    far_high = swap(by_heads[half:], "mid")
    return jnp.stack([part, by_mid, by_heads, jnp.concatenate([far_low, far_high], axis=0)])


def group_sum(parts):
    if not is_quad():
        return lax.psum_scatter(parts, GROUP, scatter_dimension=0, tiled=False).astype(F32)
    half = parts.shape[1] // 2
    far_low = swap(parts[3, :half], "mid")
    far_high = swap(parts[3, half:], "heads")
    for_mid = jnp.concatenate(
        [parts[1, :half], (parts[1, half:].astype(F32) + far_high.astype(F32)).astype(BF)], axis=0
    )
    for_heads = jnp.concatenate(
        [(parts[2, :half].astype(F32) + far_low.astype(F32)).astype(BF), parts[2, half:]], axis=0
    )
    by_mid = swap(for_mid, "mid")
    by_heads = swap(for_heads, "heads")
    return parts[0].astype(F32) + by_mid.astype(F32) + by_heads.astype(F32)


def slot_places():
    head_at = lax.axis_index("heads")
    mid_at = lax.axis_index("mid")
    if is_quad():
        return (
            jnp.stack([head_at, head_at, 1 - head_at, 1 - head_at]),
            jnp.stack([mid_at, 1 - mid_at, mid_at, 1 - mid_at]),
        )
    mids = lax.axis_size("mid")
    slots = jnp.arange(lax.axis_size("heads") * mids, dtype=jnp.int32)
    return (slots // mids, slots % mids)


def all_sum(vector):
    for axis in ("lo", "mid", "heads", "hi"):
        size = lax.axis_size(axis)
        if size & (size - 1):
            vector = lax.psum(vector, axis)
            continue
        step = 1
        while step < size:
            vector = vector + lax.ppermute(vector, axis, [(i, i ^ step) for i in range(size)])
            step *= 2
    return vector


def columns_out(parts):
    return lax.all_to_all(
        parts.transpose(1, 0, 2), GROUP, split_axis=0, concat_axis=0, tiled=True
    )


def gather_data(part):
    return lax.all_gather(part, DATA, axis=0, tiled=False)


def natural_rows(gathered):
    heads, mids = lax.axis_size("heads"), lax.axis_size("mid")
    his, los = lax.axis_size("hi"), lax.axis_size("lo")
    rows, cols = gathered.shape[2:]
    parts = gathered.reshape(his, los, heads, mids, rows, cols)
    return parts.transpose(2, 0, 3, 1, 4, 5).reshape(-1, cols)


def scatter_rows(grads):
    heads, mids = lax.axis_size("heads"), lax.axis_size("mid")
    his, los = lax.axis_size("hi"), lax.axis_size("lo")
    cols = grads.shape[1]
    parts = grads.reshape(heads, his, mids, los, -1, cols).transpose(1, 3, 0, 2, 4, 5)
    rows = parts.shape[4]
    summed = lax.psum_scatter(
        parts.reshape(his * los, heads * mids * rows, cols),
        DATA,
        scatter_dimension=0,
        tiled=False,
    )
    return summed.reshape(heads * mids, rows, cols)


def row_moves():
    mids, los = lax.axis_size("mid"), lax.axis_size("lo")
    count = lax.axis_size("hi") * mids * los
    share = count // mids
    moves = []
    for source in range(count):
        owner, rest = source // share, source % share
        moves.append((source, ((rest // los) * mids + owner) * los + rest % los))
    return moves


def rows_out(part):
    return lax.ppermute(part, SEQ, row_moves())


def rows_back(part):
    return lax.ppermute(part, SEQ, [(there, here) for here, there in row_moves()])


def lane_index(shape):
    return lax.broadcasted_iota(jnp.int32, shape, len(shape) - 1)


def half_sums(values, lane, head_size):
    first = jnp.sum(jnp.where(lane < head_size, values, 0.0), axis=-1, keepdims=True)
    second = jnp.sum(jnp.where(lane < head_size, 0.0, values), axis=-1, keepdims=True)
    return jnp.where(lane < head_size, first, second)


def partner(values, lane, head_size):
    quarter = head_size // 2
    return jnp.where(
        lane % head_size < quarter,
        pltpu.roll(values, LANES - quarter, 1),
        pltpu.roll(values, quarter, 1),
    )


def project_kernel(
    head_size, normed_ref, w_ref, cos_ref, sin_ref, qgain_ref, kgain_ref, raw_ref, q_ref, kv_ref
):
    raw = dot_plain(normed_ref[...], w_ref[...])
    raw_ref[...] = raw
    cos, sin = cos_ref[...], sin_ref[...]
    lane = lane_index(cos.shape)
    q_width = q_ref.shape[1]
    for at in range(0, raw.shape[1], LANES):
        part = raw[:, at : at + LANES]
        is_query = at < q_width
        inverse = lax.rsqrt(half_sums(part * part, lane, head_size) / head_size + EPS)
        scaled = part * inverse * (qgain_ref[...] if is_query else kgain_ref[...])
        turned = scaled * cos + partner(scaled, lane, head_size) * sin
        if is_query:
            q_ref[:, at : at + LANES] = turned.astype(BF)
        else:
            out_at = at - q_width
            kv_ref[:, out_at : out_at + LANES] = jnp.where(lane < head_size, turned, part).astype(BF)


def project(normed, w_qkv, cos, sin, query_gain, key_gain, q_width, head_size):
    rows, width = normed.shape
    cols = w_qkv.shape[1]
    tile = 256
    whole = lambda i: (0, 0)
    step = lambda i: (i, 0)
    return pl.pallas_call(
        functools.partial(project_kernel, head_size),
        grid=(rows // tile,),
        in_specs=[
            pl.BlockSpec((tile, width), step),
            pl.BlockSpec((width, cols), whole),
            pl.BlockSpec((tile, LANES), step),
            pl.BlockSpec((tile, LANES), step),
            pl.BlockSpec((1, LANES), whole),
            pl.BlockSpec((1, LANES), whole),
        ],
        out_specs=[
            pl.BlockSpec((tile, cols), step),
            pl.BlockSpec((tile, q_width), step),
            pl.BlockSpec((tile, cols - q_width), step),
        ],
        out_shape=[
            jax.ShapeDtypeStruct((rows, cols), F32),
            jax.ShapeDtypeStruct((rows, q_width), BF),
            jax.ShapeDtypeStruct((rows, cols - q_width), BF),
        ],
        compiler_params=pltpu.CompilerParams(vmem_limit_bytes=VMEM_LIMIT),
    )(normed, w_qkv, cos, sin, query_gain, key_gain)


def unproject_kernel(
    head_size, raw_ref, dq_ref, dkv_ref, cos_ref, sin_ref, qgain_ref, kgain_ref, out_ref, gain_ref
):
    cos, sin = cos_ref[...], sin_ref[...]
    lane = lane_index(cos.shape)
    q_width = dq_ref.shape[1]
    totals = [jnp.zeros((1, LANES), F32), jnp.zeros((1, LANES), F32)]
    for at in range(0, raw_ref.shape[1], LANES):
        part = raw_ref[:, at : at + LANES]
        is_query = at < q_width
        if is_query:
            upstream = dq_ref[:, at : at + LANES]
            gain = qgain_ref[...]
        else:
            upstream = dkv_ref[:, at - q_width : at - q_width + LANES].astype(F32)
            gain = kgain_ref[...]
        turned = upstream * cos - partner(upstream, lane, head_size) * sin
        inverse = lax.rsqrt(half_sums(part * part, lane, head_size) / head_size + EPS)
        scaled = turned * gain
        inner = half_sums(scaled * part, lane, head_size) / head_size
        grad = inverse * scaled - part * inverse * inverse * inverse * inner
        gain_part = jnp.sum(turned * part * inverse, axis=0, keepdims=True)
        if not is_query:
            grad = jnp.where(lane < head_size, grad, upstream)
            gain_part = jnp.where(lane[:1] < head_size, gain_part, 0.0)
        totals[0 if is_query else 1] += gain_part
        out_ref[:, at : at + LANES] = grad.astype(BF)
    gain_ref[0] = jnp.concatenate(totals, axis=0)


def unproject(raw, dq, dkv, cos, sin, query_gain, key_gain, head_size):
    rows, cols = raw.shape
    q_width = dq.shape[1]
    tile = 256
    whole = lambda i: (0, 0)
    step = lambda i: (i, 0)
    return pl.pallas_call(
        functools.partial(unproject_kernel, head_size),
        grid=(rows // tile,),
        in_specs=[
            pl.BlockSpec((tile, cols), step),
            pl.BlockSpec((tile, q_width), step),
            pl.BlockSpec((tile, cols - q_width), step),
            pl.BlockSpec((tile, LANES), step),
            pl.BlockSpec((tile, LANES), step),
            pl.BlockSpec((1, LANES), whole),
            pl.BlockSpec((1, LANES), whole),
        ],
        out_specs=[
            pl.BlockSpec((tile, cols), step),
            pl.BlockSpec((1, 2, LANES), lambda i: (i, 0, 0)),
        ],
        out_shape=[
            jax.ShapeDtypeStruct((rows, cols), BF),
            jax.ShapeDtypeStruct((rows // tile, 2, LANES), F32),
        ],
        compiler_params=pltpu.CompilerParams(vmem_limit_bytes=VMEM_LIMIT),
    )(raw, dq, dkv, cos, sin, query_gain, key_gain)


def unit_base(unit, places):
    los, span, block = places
    return (unit // los) * span + (unit % los) * block


def attend_kernel(
    head_size,
    places,
    code_ref,
    q_ref,
    kv_ref,
    row_ref,
    key_ref,
    exact_ref,
    low_ref,
    lse_ref,
    qs_ref,
    acc_ref,
    sum_ref,
):
    batch, part = pl.program_id(0), pl.program_id(2)
    count = row_ref.shape[1]
    share = kv_ref.shape[0]
    factor = LOG2E * head_size**-0.5
    lane = lane_index((count, LANES))

    @pl.when(part == 0)
    def _():
        both = q_ref[:, 0].reshape(count, LANES).astype(F32)
        qs_ref[0] = jnp.where(lane < head_size, both, 0.0).astype(BF)
        qs_ref[1] = jnp.where(lane < head_size, pltpu.roll(both, head_size, 1), 0.0).astype(BF)
        acc_ref[...] = jnp.zeros_like(acc_ref)
        sum_ref[...] = jnp.zeros_like(sum_ref)

    def one(at, masked):
        keys = kv_ref[at, :, 0].reshape(count, LANES)
        if masked:
            key_pos = key_ref[...] + unit_base(part * share + at, places)
            allowed = (key_pos <= row_ref[0, :, 0:1]) & (key_pos >= row_ref[0, :, 1:2])
        for head in range(2):
            exps = jnp.exp2(dot_back(qs_ref[head], keys) * factor)
            if masked:
                exps = jnp.where(allowed, exps, 0.0)
            partial = exps[:, :LANES]
            for lane_at in range(LANES, count, LANES):
                partial = partial + exps[:, lane_at : lane_at + LANES]
            sum_ref[head] += partial
            acc_ref[head] += dot_plain(exps.astype(BF), keys)

    def step(at, carry):
        code = code_ref[batch, part * share + at]

        @pl.when(code == 1)
        def _():
            one(at, False)

        @pl.when(code == 2)
        def _():
            one(at, True)

        return carry

    lax.fori_loop(0, share, step, 0)

    @pl.when(part == pl.num_programs(2) - 1)
    def _():
        results = []
        for head in range(2):
            total = jnp.sum(sum_ref[head], axis=-1, keepdims=True)
            results.append(acc_ref[head] / total)
            wide = jnp.broadcast_to(jnp.log2(total), (count, LANES))
            lse_ref[0, 0, head] = wide.T[:8]
        joined = jnp.where(lane < head_size, pltpu.roll(results[0], head_size, 1), results[1])
        joined = joined.reshape(exact_ref.shape[0], -1, LANES)
        exact_ref[:, 0] = joined
        low_ref[:, 0] = joined.astype(BF)


def attend(codes, query, kv_all, row_info, key_pos, places, head_size):
    slots, batches, rows, q_width = query.shape
    units = kv_all.shape[0]
    share = math.gcd(units, 8)
    count = slots * rows
    pairs = q_width // LANES
    pick = lambda b, p, u, codes: (0, b, 0, p)
    return pl.pallas_call(
        functools.partial(attend_kernel, head_size, places),
        grid_spec=pltpu.PrefetchScalarGridSpec(
            num_scalar_prefetch=1,
            grid=(batches, pairs, units // share),
            in_specs=[
                pl.BlockSpec((slots, 1, rows, LANES), pick),
                pl.BlockSpec(
                    (share, slots, 1, rows, LANES), lambda b, p, u, codes: (u, 0, b, 0, p)
                ),
                pl.BlockSpec((1, count, 2), lambda b, p, u, codes: (b, 0, 0)),
                pl.BlockSpec((1, count), lambda b, p, u, codes: (0, 0)),
            ],
            out_specs=[
                pl.BlockSpec((slots, 1, rows, LANES), pick),
                pl.BlockSpec((slots, 1, rows, LANES), pick),
                pl.BlockSpec((1, 1, 2, 8, count), lambda b, p, u, codes: (b, p, 0, 0, 0)),
            ],
            scratch_shapes=[
                pltpu.VMEM((2, count, LANES), BF),
                pltpu.VMEM((2, count, LANES), F32),
                pltpu.VMEM((2, count, LANES), F32),
            ],
        ),
        out_shape=[
            jax.ShapeDtypeStruct(query.shape, F32),
            jax.ShapeDtypeStruct(query.shape, BF),
            jax.ShapeDtypeStruct((batches, pairs, 2, 8, count), F32),
        ],
        compiler_params=pltpu.CompilerParams(vmem_limit_bytes=VMEM_LIMIT),
    )(codes, query, kv_all, row_info, key_pos)


def attend_back_kernel(
    head_size,
    places,
    code_ref,
    q_ref,
    up_ref,
    exact_ref,
    lse_ref,
    kv_ref,
    row_ref,
    key_ref,
    dq_ref,
    dkv_ref,
    qs_ref,
    us_ref,
    acc_ref,
    delta_ref,
):
    batch, part = pl.program_id(0), pl.program_id(2)
    count = row_ref.shape[2]
    share = kv_ref.shape[0]
    scale = head_size**-0.5
    factor = LOG2E * scale
    lane = lane_index((count, LANES))

    @pl.when(part == 0)
    def _():
        both = q_ref[:, 0].reshape(count, LANES).astype(F32)
        qs_ref[0] = jnp.where(lane < head_size, both, 0.0).astype(BF)
        qs_ref[1] = jnp.where(lane < head_size, pltpu.roll(both, head_size, 1), 0.0).astype(BF)
        upper = up_ref[:, 0].reshape(count, LANES).astype(F32)
        us_ref[0] = jnp.where(lane < head_size, 0.0, pltpu.roll(upper, head_size, 1)).astype(BF)
        us_ref[1] = jnp.where(lane < head_size, 0.0, upper).astype(BF)
        products = upper * exact_ref[:, 0].reshape(count, LANES)
        for head in range(2):
            inside = (lane < head_size) if head == 0 else (lane >= head_size)
            total = jnp.sum(jnp.where(inside, products, 0.0), axis=-1, keepdims=True)
            delta_ref[head] = jnp.broadcast_to(total, (count, LANES)).T[:8]
        acc_ref[...] = jnp.zeros_like(acc_ref)

    def one(at, masked):
        keys = kv_ref[at, :, 0].reshape(count, LANES)
        if masked:
            key_pos = key_ref[...] + unit_base(part * share + at, places)
            allowed = (key_pos <= row_ref[0, 0:1]) & (key_pos >= row_ref[0, 1:2])
        grad_kv = jnp.zeros((count, LANES), F32)
        for head in range(2):
            scores = dot_back(keys, qs_ref[head]) * factor
            probs = jnp.exp2(scores - lse_ref[0, 0, head, 0:1])
            if masked:
                probs = jnp.where(allowed, probs, 0.0)
            grads = dot_back(keys, us_ref[head])
            grads = (probs * (grads - delta_ref[head, 0:1])).astype(BF)
            grad_kv += dot_plain(probs.astype(BF), us_ref[head])
            grad_kv += dot_plain(grads, qs_ref[head]) * scale
            acc_ref[head] += dot_outer(grads, keys)
        dkv_ref[at, :, 0] = grad_kv.astype(BF).reshape(dkv_ref.shape[1], -1, LANES)

    def step(at, carry):
        code = code_ref[batch, part * share + at]

        @pl.when(code == 0)
        def _():
            dkv_ref[at, :, 0] = jnp.zeros((dkv_ref.shape[1],) + dkv_ref.shape[3:], BF)

        @pl.when(code == 1)
        def _():
            one(at, False)

        @pl.when(code == 2)
        def _():
            one(at, True)

        return carry

    lax.fori_loop(0, share, step, 0)

    @pl.when(part == pl.num_programs(2) - 1)
    def _():
        joined = jnp.where(lane < head_size, acc_ref[0], pltpu.roll(acc_ref[1], head_size, 1))
        dq_ref[:, 0] = (joined * scale).reshape(dq_ref.shape[0], -1, LANES)


def attend_back(codes, query, upstream, exact, lse, kv_all, row_info, key_pos, places, head_size):
    slots, batches, rows, q_width = query.shape
    units = kv_all.shape[0]
    share = math.gcd(units, 8)
    count = slots * rows
    pairs = q_width // LANES
    pick = lambda b, p, u, codes: (0, b, 0, p)
    pick_kv = lambda b, p, u, codes: (u, 0, b, 0, p)
    return pl.pallas_call(
        functools.partial(attend_back_kernel, head_size, places),
        grid_spec=pltpu.PrefetchScalarGridSpec(
            num_scalar_prefetch=1,
            grid=(batches, pairs, units // share),
            in_specs=[
                pl.BlockSpec((slots, 1, rows, LANES), pick),
                pl.BlockSpec((slots, 1, rows, LANES), pick),
                pl.BlockSpec((slots, 1, rows, LANES), pick),
                pl.BlockSpec((1, 1, 2, 8, count), lambda b, p, u, codes: (b, p, 0, 0, 0)),
                pl.BlockSpec((share, slots, 1, rows, LANES), pick_kv),
                pl.BlockSpec((1, 2, count), lambda b, p, u, codes: (b, 0, 0)),
                pl.BlockSpec((count, 1), lambda b, p, u, codes: (0, 0)),
            ],
            out_specs=[
                pl.BlockSpec((slots, 1, rows, LANES), pick),
                pl.BlockSpec((share, slots, 1, rows, LANES), pick_kv),
            ],
            scratch_shapes=[
                pltpu.VMEM((2, count, LANES), BF),
                pltpu.VMEM((2, count, LANES), BF),
                pltpu.VMEM((2, count, LANES), F32),
                pltpu.VMEM((2, 8, count), F32),
            ],
        ),
        out_shape=[
            jax.ShapeDtypeStruct(query.shape, F32),
            jax.ShapeDtypeStruct(kv_all.shape, BF),
        ],
        compiler_params=pltpu.CompilerParams(vmem_limit_bytes=VMEM_LIMIT),
    )(codes, query, upstream, exact, lse, kv_all, row_info, key_pos)


def per_device(
    inputs,
    cotangent,
    attn_gain,
    w_query,
    w_key,
    w_value,
    w_output,
    query_gain,
    key_gain,
    ffn_gain,
    w_gate,
    w_up,
    w_down,
    doc_starts,
):
    heads, mids = lax.axis_size("heads"), lax.axis_size("mid")
    his, los = lax.axis_size("hi"), lax.axis_size("lo")
    slots, units = heads * mids, his * los
    batches, _, rows, width = inputs.shape
    block = rows * heads
    count = slots * rows
    head_size = query_gain.shape[0]
    w_rows = w_query.shape[0]
    q_width = w_query.shape[1] // slots
    pairs = w_key.shape[1] // head_size // slots
    ff_width = w_gate.shape[1] // slots

    by_slot = lambda w: w.reshape(w_rows, slots, -1)
    kv_cols = jnp.stack(
        [
            w_key.reshape(w_rows, slots, pairs, head_size),
            w_value.reshape(w_rows, slots, pairs, head_size),
        ],
        axis=3,
    )
    qkv_part = columns_out(
        jnp.concatenate([by_slot(w_query), kv_cols.reshape(w_rows, slots, -1)], axis=2)
    )
    w_qkv = natural_rows(gather_data(qkv_part))
    own_in = inputs[:, 0]
    in_all = group_gather(own_in)
    own_cot = cotangent[:, 0]
    cot_all = group_gather(own_cot)
    wo_part = rows_out(w_output)
    gate_up_part = columns_out(jnp.concatenate([by_slot(w_gate), by_slot(w_up)], axis=2))
    wd_part = rows_out(w_down)

    head_at, mid_at = slot_places()
    row_at = jnp.arange(rows, dtype=jnp.int32)
    hi_at, lo_at = lax.axis_index("hi"), lax.axis_index("lo")

    def positions(hi, lo):
        blocks = (hi * mids + mid_at) * los + lo
        return (blocks * block + head_at * rows)[:, None] + row_at[None, :]

    row_pos = positions(hi_at, lo_at).reshape(count)
    first_pos = positions(0, 0).reshape(count)
    places = (los, mids * los * block, block)
    unit_at = unit_base(jnp.arange(units, dtype=jnp.int32), places)
    starts = doc_starts[:, None, :]
    row_begin = jnp.max(jnp.where(starts <= row_pos[None, :, None], starts, 0), axis=2)
    row_both = jnp.broadcast_to(row_pos[None], (batches, count))
    key_low, key_high = (unit_at + jnp.min(first_pos))[None], (unit_at + jnp.max(first_pos))[None]
    begin_low, begin_high = (
        jnp.min(row_begin, axis=1)[:, None],
        jnp.max(row_begin, axis=1)[:, None],
    )
    none = (key_low > jnp.max(row_pos)) | (key_high < begin_low)
    full = (key_high <= jnp.min(row_pos)) & (key_low >= begin_high)
    codes = jnp.where(none, 0, jnp.where(full, 1, 2)).astype(jnp.int32)
    info_cols = jnp.stack([row_both, row_begin], axis=2)
    info_rows = jnp.stack([row_both, row_begin], axis=1)

    half = head_size // 2
    frequency = THETA ** (-(jnp.arange(half, dtype=F32) * 2.0 / head_size))
    turn_pos = (row_both - row_begin).reshape(batches, slots, rows).transpose(1, 0, 2)
    angles = turn_pos.reshape(-1).astype(F32)[:, None] * frequency[None, :]
    cos, sin = jnp.cos(angles), jnp.sin(angles)
    cos = jnp.concatenate([cos] * 4, axis=1)
    sin = jnp.concatenate([-sin, sin, -sin, sin], axis=1)
    q_gain = jnp.concatenate([query_gain, query_gain])[None]
    k_gain = jnp.concatenate([key_gain, key_gain])[None]

    in_wide = in_all.reshape(-1, width).astype(F32)
    in_unit = in_wide * rms_inverse(in_wide)
    normed = (in_unit * attn_gain).astype(BF)
    raw, query, kv = project(normed, w_qkv, cos, sin, q_gain, k_gain, q_width, head_size)
    query = query.reshape(slots, batches, rows, q_width)
    kv_all = gather_data(kv.reshape(slots, batches, rows, -1))
    wo_use = gather_data(wo_part).reshape(-1, width)
    w_gate_up = natural_rows(gather_data(gate_up_part))
    wg_use, wu_use = w_gate_up[:, :ff_width], w_gate_up[:, ff_width:]
    wd_use = gather_data(wd_part).reshape(-1, width)
    exact, attn, lse = attend(
        codes, query, kv_all, info_cols, first_pos[None], places, head_size
    )
    attn = attn.reshape(-1, q_width)
    by_slots = lambda total: total.astype(BF).reshape(slots, batches * rows, width)
    middle = own_in.reshape(-1, width).astype(F32) + group_sum(by_slots(dot_plain(attn, wo_use)))

    normed_two = (middle * rms_inverse(middle) * ffn_gain).astype(BF)
    normed_two_all = group_gather(normed_two).reshape(-1, width)
    cot_rows = cot_all.reshape(-1, width)
    gate = dot_plain(normed_two_all, wg_use)
    upper = dot_plain(normed_two_all, wu_use)
    grad_hidden = dot_back(cot_rows, wd_use)
    sigmoid = jax.nn.sigmoid(gate)
    silu = gate * sigmoid
    hidden = (silu * upper).astype(BF)
    grad_gate = (grad_hidden * upper * sigmoid * (1.0 + gate * (1.0 - sigmoid))).astype(BF)
    grad_upper = (grad_hidden * silu).astype(BF)
    grad_two = group_sum(by_slots(dot_back(grad_gate, wg_use) + dot_back(grad_upper, wu_use)))
    grad_gate_up = jnp.concatenate(
        [dot_outer(normed_two_all, grad_gate), dot_outer(normed_two_all, grad_upper)], axis=1
    )
    gate_up_sum = scatter_rows(grad_gate_up.astype(BF))
    down_sum = lax.psum_scatter(
        dot_outer(hidden, cot_rows).astype(BF), DATA, scatter_dimension=0, tiled=True
    )
    block_out = (middle + group_sum(by_slots(dot_plain(hidden, wd_use)))).astype(BF)
    grad_mid_part, ffn_gain_part = norm_back(middle, ffn_gain, grad_two)
    grad_middle = own_cot.reshape(-1, width).astype(F32) + grad_mid_part

    grad_mid_all = group_gather(grad_middle.astype(BF)).reshape(-1, width)
    grad_attn = dot_back(grad_mid_all, wo_use).astype(BF).reshape(query.shape)
    dq, dkv = attend_back(
        codes,
        query,
        grad_attn,
        exact,
        lse,
        kv_all,
        info_rows,
        first_pos[:, None],
        places,
        head_size,
    )
    dkv_mine = lax.psum_scatter(dkv, DATA, scatter_dimension=0, tiled=False)
    grad_output = dot_outer(attn, grad_mid_all)
    output_sum = lax.psum_scatter(grad_output.astype(BF), DATA, scatter_dimension=0, tiled=True)
    grad_raw, head_gains = unproject(
        raw,
        dq.reshape(-1, q_width),
        dkv_mine.reshape(raw.shape[0], -1),
        cos,
        sin,
        q_gain,
        k_gain,
        head_size,
    )
    grad_normed_low = dot_back(grad_raw, w_qkv).astype(BF)
    grad_qkv = dot_outer(normed, grad_raw)
    qkv_sum = scatter_rows(grad_qkv.astype(BF))
    grad_normed = group_sum(grad_normed_low.reshape(slots, batches * rows, width))
    grad_in_part, _ = norm_back(own_in.reshape(-1, width).astype(F32), attn_gain, grad_normed)
    grad_inputs = grad_middle + grad_in_part
    attn_gain_part = jnp.sum(grad_normed_low.astype(F32) * in_unit, axis=0)

    qkv_cols = columns_out(qkv_sum.transpose(1, 0, 2)).transpose(1, 0, 2).astype(F32)
    gate_up_cols = columns_out(gate_up_sum.transpose(1, 0, 2)).transpose(1, 0, 2).astype(F32)
    kv_sums = qkv_cols[:, :, q_width:].reshape(w_rows, slots, pairs, 2, head_size)
    head_sums = jnp.sum(head_gains, axis=0).reshape(2, 2, head_size).sum(axis=1)
    gains = all_sum(
        jnp.concatenate(
            [attn_gain_part, jnp.sum(ffn_gain_part, axis=0), head_sums[0], head_sums[1]]
        )
    )
    return (
        block_out.reshape(batches, 1, rows, width),
        grad_inputs.reshape(batches, 1, rows, width),
        gains[:width],
        qkv_cols[:, :, :q_width].reshape(w_rows, -1),
        kv_sums[:, :, :, 0].reshape(w_rows, -1),
        kv_sums[:, :, :, 1].reshape(w_rows, -1),
        rows_back(output_sum).astype(F32),
        gains[2 * width : 2 * width + head_size],
        gains[2 * width + head_size :],
        gains[width : 2 * width],
        gate_up_cols[:, :, :ff_width].reshape(w_rows, -1),
        gate_up_cols[:, :, ff_width:].reshape(w_rows, -1),
        rows_back(down_sum).astype(F32),
    )


def solution(mesh):
    heads, seq = mesh.shape["heads"], mesh.shape["seq"]
    rows_spec = P(None, SEQ, "heads", None)
    weight_spec = P(ALL, None)

    def run(*args):
        kv_heads = args[4].shape[1] // args[7].shape[0]
        low = 2 if seq % 2 == 0 else 1
        mid = 2 if seq % (2 * low) == 0 and kv_heads % (2 * heads) == 0 else 1
        split = Mesh(
            mesh.devices.reshape(heads, seq // (mid * low), mid, low), ("heads",) + SEQ
        )
        return jax.shard_map(
            per_device,
            mesh=split,
            in_specs=(
                (rows_spec, rows_spec, P())
                + (weight_spec,) * 4
                + (P(), P(), P())
                + (weight_spec,) * 3
                + (P(),)
            ),
            out_specs=(
                (rows_spec, rows_spec, P())
                + (weight_spec,) * 4
                + (P(), P(), P())
                + (weight_spec,) * 3
            ),
            check_vma=False,
        )(*args)

    return run
```

```python
import functools
import math

import jax
import jax.numpy as jnp
from jax import lax
from jax.experimental import pallas as pl
from jax.experimental.pallas import tpu as pltpu
from jax.sharding import Mesh, PartitionSpec as P

EPS = 1e-05
THETA = 1000000.0
LANES = 128
LOG2E = math.log2(math.e)
GROUP = ("heads", "mid")
DATA = ("hi", "lo")
SEQ = ("hi", "mid", "lo")
ALL = ("heads",) + SEQ
BF = jnp.bfloat16
F32 = jnp.float32
VMEM_LIMIT = 48 * 1024 * 1024
CHEAP = pl.CostEstimate(flops=1, bytes_accessed=1, transcendentals=0)


def dot_plain(left_side, right_side):
    return jnp.dot(left_side, right_side, preferred_element_type=F32)


def dot_back(left_side, right_side):
    return lax.dot_general(
        left_side, right_side, (((1,), (1,)), ((), ())), preferred_element_type=F32
    )


def dot_outer(left_side, right_side):
    return lax.dot_general(
        left_side, right_side, (((0,), (0,)), ((), ())), preferred_element_type=F32
    )


def together(*values):
    return lax.optimization_barrier(values)


def rms_inverse(values):
    return lax.rsqrt(jnp.mean(values * values, axis=-1, keepdims=True) + EPS)


def norm_back(values, gain_vec, upstream):
    inverse = rms_inverse(values)
    scaled = upstream * gain_vec
    inner_mean = jnp.mean(scaled * values, axis=-1, keepdims=True)
    grad_values = inverse * scaled - values * inverse * inverse * inverse * inner_mean
    return (grad_values, upstream * values * inverse)


def is_quad():
    return lax.axis_size("heads") == 2 and lax.axis_size("mid") == 2


def swap(part, axis):
    return lax.ppermute(part, axis, [(0, 1), (1, 0)])


def group_rank():
    return lax.axis_index("heads") * lax.axis_size("mid") + lax.axis_index("mid")


def block_at(parts, index):
    return lax.dynamic_index_in_dim(parts, index, axis=0, keepdims=False)


def in_order(blocks):
    rank = group_rank()
    total = jnp.zeros((4,) + blocks[0].shape, blocks[0].dtype)
    for slot, block in enumerate(blocks):
        total = lax.dynamic_update_index_in_dim(total, block, rank ^ slot, axis=0)
    return total


def group_near(part):
    return swap(part, "mid"), swap(part, "heads")


def group_far(by_mid, by_heads):
    half = by_mid.shape[0] // 2
    return swap(by_mid[:half], "heads"), swap(by_heads[half:], "mid")


def group_joined(part, near, far):
    return in_order([part, *near, jnp.concatenate(far, axis=0)])


def group_gather(part):
    if not is_quad():
        return lax.all_gather(part, GROUP, axis=0, tiled=False)
    near = group_near(part)
    return group_joined(part, near, group_far(*near))


def group_gather_plain(part):
    return lax.all_gather(part, GROUP, axis=0, tiled=False)


def group_sum_plain(parts):
    flat = parts.reshape((-1,) + parts.shape[2:])
    return lax.psum_scatter(flat, GROUP, scatter_dimension=0, tiled=True)


class GroupSum:
    def __init__(self, parts):
        if is_quad():
            rank = group_rank()
            self.parts = [block_at(parts, rank ^ slot) for slot in range(4)]
            half = parts.shape[1] // 2
            far = self.parts[3]
            self.far = (swap(far[:half], "mid"), swap(far[half:], "heads"))
        else:
            self.total = group_sum_plain(parts)

    def second(self, *between):
        if is_quad():
            _, mid, head, _ = self.parts
            half = mid.shape[0] // 2
            far_low, far_high = self.far
            if between:
                far_low, far_high, *between = together(far_low, far_high, *between)
            for_mid = jnp.concatenate([mid[:half], low_sum(mid[half:], far_high)], axis=0)
            for_heads = jnp.concatenate([low_sum(head[:half], far_low), head[half:]], axis=0)
            self.near = (swap(for_mid, "mid"), swap(for_heads, "heads"))
        return between

    def hold(self, *later):
        if is_quad():
            near_mid, near_heads, *later = together(*self.near, *later)
            self.near = (near_mid, near_heads)
        return later

    def done(self):
        if not is_quad():
            return self.total.astype(F32)
        return self.parts[0].astype(F32) + self.near[0].astype(F32) + self.near[1].astype(F32)


def slot_places():
    mids = lax.axis_size("mid")
    slots = jnp.arange(lax.axis_size("heads") * mids, dtype=jnp.int32)
    return (slots // mids, slots % mids)


def all_sum(vector):
    for axis in ("lo", "mid", "heads", "hi"):
        size = lax.axis_size(axis)
        if size & (size - 1):
            vector = lax.psum(vector, axis)
            continue
        step = 1
        while step < size:
            vector = vector + lax.ppermute(vector, axis, [(i, i ^ step) for i in range(size)])
            step *= 2
    return vector


def columns_out(parts):
    return lax.all_to_all(parts, GROUP, split_axis=0, concat_axis=0, tiled=True)


def columns_out_async(parts):
    if not is_quad():
        return columns_out(parts)
    rank = group_rank()
    far = [(0, 3), (1, 2), (2, 1), (3, 0)]
    return in_order(
        [
            block_at(parts, rank),
            swap(block_at(parts, rank ^ 1), "mid"),
            swap(block_at(parts, rank ^ 2), "heads"),
            lax.ppermute(block_at(parts, rank ^ 3), GROUP, far),
        ]
    )


def ring(part, shift):
    size = lax.axis_size("hi")
    return lax.ppermute(part, "hi", [(i, (i + shift) % size) for i in range(size)])


def other_low(part):
    return swap(part, "lo")


def fast_rows(rows):
    return lax.axis_size("lo") == 2 and rows % 16 == 0


def data_ring(part):
    own = [part]
    for _ in range(lax.axis_size("hi") - 1):
        own.append(ring(own[-1], 1))
    return own, [other_low(piece) for piece in own]


def place_index():
    return jnp.stack(
        [lax.axis_index("hi"), lax.axis_index("lo"), lax.axis_index("heads"), lax.axis_index("mid")]
    ).astype(jnp.int32)


def block_row(at_ref, sizes, step, other, source):
    his, los, heads, mids = sizes
    hi = lax.rem(at_ref[0] - step + his, his)
    low = 1 - at_ref[1] if other else at_ref[1]
    if source is None:
        return hi * los + low
    return ((source // mids * his + hi) * mids + source % mids) * los + low


def split_sizes():
    return tuple(lax.axis_size(name) for name in ("hi", "lo", "heads", "mid"))


def place_kernel(sizes, sources, rows, at_ref, *refs):
    his = sizes[0]
    pieces, out_ref, sems = refs[: 2 * his], refs[2 * his], refs[2 * his + 1]
    copies = []
    for step in range(his):
        for other in range(2):
            for source in sources:
                first = block_row(at_ref, sizes, step, other, source) * rows
                piece = pieces[step + other * his]
                copies.append(
                    pltpu.make_async_copy(
                        piece if source is None else piece.at[source],
                        out_ref.at[pl.ds(pl.multiple_of(first, rows), rows)],
                        sems.at[len(copies)],
                    )
                )
    for copy in copies:
        copy.start()
    for copy in copies:
        copy.wait()


def placed(own, other):
    sizes = split_sizes()
    first = own[0]
    rows, cols = first.shape[-2:]
    sources = range(first.shape[0]) if first.ndim == 3 else (None,)
    total = rows * sizes[0] * sizes[1] * len(sources)
    anywhere = pl.BlockSpec(memory_space=pl.ANY)
    return pl.pallas_call(
        functools.partial(place_kernel, sizes, sources, rows),
        in_specs=[pl.BlockSpec(memory_space=pltpu.SMEM)] + [anywhere] * (2 * sizes[0]),
        out_specs=pl.BlockSpec(memory_space=pltpu.VMEM),
        out_shape=jax.ShapeDtypeStruct((total, cols), first.dtype),
        scratch_shapes=[pltpu.SemaphoreType.DMA((2 * sizes[0] * len(sources),))],
        compiler_params=pltpu.CompilerParams(vmem_limit_bytes=VMEM_LIMIT),
        cost_estimate=CHEAP,
    )(place_index(), *own, *other)


def unplace_kernel(sizes, sources, rows, at_ref, full_ref, own_ref, other_ref, sems):
    his = sizes[0]
    copies = []
    for step in range(his):
        for other in range(2):
            for source in sources:
                first = block_row(at_ref, sizes, step, other, source) * rows
                target = (other_ref if other else own_ref).at[step]
                copies.append(
                    pltpu.make_async_copy(
                        full_ref.at[pl.ds(pl.multiple_of(first, rows), rows)],
                        target if source is None else target.at[source],
                        sems.at[len(copies)],
                    )
                )
    for copy in copies:
        copy.start()
    for copy in copies:
        copy.wait()


def unplaced(full, rows, by_source):
    sizes = split_sizes()
    cols = full.shape[1]
    slots = sizes[2] * sizes[3]
    sources = range(slots) if by_source else (None,)
    shape = (sizes[0],) + ((slots,) if by_source else ()) + (rows, cols)
    anywhere = pl.BlockSpec(memory_space=pl.ANY)
    return pl.pallas_call(
        functools.partial(unplace_kernel, sizes, sources, rows),
        in_specs=[pl.BlockSpec(memory_space=pltpu.SMEM), pl.BlockSpec(memory_space=pltpu.VMEM)],
        out_specs=[anywhere, anywhere],
        out_shape=[jax.ShapeDtypeStruct(shape, full.dtype)] * 2,
        scratch_shapes=[pltpu.SemaphoreType.DMA((2 * sizes[0] * len(sources),))],
        compiler_params=pltpu.CompilerParams(vmem_limit_bytes=VMEM_LIMIT),
        cost_estimate=CHEAP,
    )(place_index(), full)


def natural_rows(gathered):
    his, los, heads, mids = split_sizes()
    rows, cols = gathered.shape[2:]
    parts = gathered.reshape(his, los, heads, mids, rows, cols)
    return parts.transpose(2, 0, 3, 1, 4, 5).reshape(-1, cols)


def gather_data(part):
    return lax.all_gather(part, DATA, axis=0, tiled=False)


def gather_rows(part):
    if fast_rows(part.shape[-2]):
        return placed(*data_ring(part))
    return natural_rows(gather_data(part))


def low_sum(*parts):
    total = parts[0].astype(F32)
    for part in parts[1:]:
        total = total + part.astype(F32)
    return total.astype(BF)


def scatter_data(parts):
    return lax.psum_scatter(parts, DATA, scatter_dimension=0, tiled=False)


def scatter_order(grads, rows):
    his, los, heads, mids = split_sizes()
    cols = grads.shape[1]
    parts = grads.reshape(heads, his, mids, los, rows, cols).transpose(1, 3, 0, 2, 4, 5)
    return parts.reshape(his * los, heads * mids * rows, cols)


def scatter_ring(summed):
    moving = None
    for step in range(1, lax.axis_size("hi")):
        part = summed[step]
        moving = ring(part if moving is None else low_sum(part, moving), 1)
    return summed[0] if moving is None else low_sum(summed[0], moving)


def row_moves():
    mids, los = lax.axis_size("mid"), lax.axis_size("lo")
    count = lax.axis_size("hi") * mids * los
    share = count // mids
    moves = []
    for source in range(count):
        owner, rest = source // share, source % share
        moves.append((source, ((rest // los) * mids + owner) * los + rest % los))
    return moves


def rows_out(part):
    return lax.ppermute(part, SEQ, row_moves())


def rows_back(part):
    return lax.ppermute(part, SEQ, [(there, here) for here, there in row_moves()])


def lane_index(shape):
    return lax.broadcasted_iota(jnp.int32, shape, len(shape) - 1)


def half_sums(values, lane, head_size):
    first = jnp.sum(jnp.where(lane < head_size, values, 0.0), axis=-1, keepdims=True)
    second = jnp.sum(jnp.where(lane < head_size, 0.0, values), axis=-1, keepdims=True)
    return jnp.where(lane < head_size, first, second)


def partner(values, lane, head_size):
    quarter = head_size // 2
    return jnp.where(
        lane % head_size < quarter,
        pltpu.roll(values, LANES - quarter, 1),
        pltpu.roll(values, quarter, 1),
    )


def project_kernel(
    head_size, normed_ref, w_ref, cos_ref, sin_ref, qgain_ref, kgain_ref, raw_ref, q_ref, kv_ref
):
    raw = dot_plain(normed_ref[...], w_ref[...])
    raw_ref[...] = raw
    cos, sin = cos_ref[...], sin_ref[...]
    lane = lane_index(cos.shape)
    q_width = q_ref.shape[1]
    for at in range(0, raw.shape[1], LANES):
        part = raw[:, at : at + LANES]
        is_query = at < q_width
        inverse = lax.rsqrt(half_sums(part * part, lane, head_size) / head_size + EPS)
        scaled = part * inverse * (qgain_ref[...] if is_query else kgain_ref[...])
        turned = scaled * cos + partner(scaled, lane, head_size) * sin
        if is_query:
            q_ref[:, at : at + LANES] = turned.astype(BF)
        else:
            out_at = at - q_width
            kv_ref[:, out_at : out_at + LANES] = jnp.where(lane < head_size, turned, part).astype(BF)


def project(normed, w_qkv, cos, sin, query_gain, key_gain, q_width, head_size):
    rows, width = normed.shape
    cols = w_qkv.shape[1]
    tile = 256
    whole = lambda i: (0, 0)
    step = lambda i: (i, 0)
    return pl.pallas_call(
        functools.partial(project_kernel, head_size),
        grid=(rows // tile,),
        in_specs=[
            pl.BlockSpec((tile, width), step),
            pl.BlockSpec((width, cols), whole),
            pl.BlockSpec((tile, LANES), step),
            pl.BlockSpec((tile, LANES), step),
            pl.BlockSpec((1, LANES), whole),
            pl.BlockSpec((1, LANES), whole),
        ],
        out_specs=[
            pl.BlockSpec((tile, cols), step),
            pl.BlockSpec((tile, q_width), step),
            pl.BlockSpec((tile, cols - q_width), step),
        ],
        out_shape=[
            jax.ShapeDtypeStruct((rows, cols), F32),
            jax.ShapeDtypeStruct((rows, q_width), BF),
            jax.ShapeDtypeStruct((rows, cols - q_width), BF),
        ],
        compiler_params=pltpu.CompilerParams(vmem_limit_bytes=VMEM_LIMIT),
        cost_estimate=CHEAP,
    )(normed, w_qkv, cos, sin, query_gain, key_gain)


def unproject_kernel(
    head_size, raw_ref, dq_ref, dkv_ref, cos_ref, sin_ref, qgain_ref, kgain_ref, out_ref, gain_ref
):
    cos, sin = cos_ref[...], sin_ref[...]
    lane = lane_index(cos.shape)
    q_width = dq_ref.shape[1]
    totals = [jnp.zeros((1, LANES), F32), jnp.zeros((1, LANES), F32)]
    for at in range(0, raw_ref.shape[1], LANES):
        part = raw_ref[:, at : at + LANES]
        is_query = at < q_width
        if is_query:
            upstream = dq_ref[:, at : at + LANES]
            gain = qgain_ref[...]
        else:
            upstream = dkv_ref[:, at - q_width : at - q_width + LANES].astype(F32)
            gain = kgain_ref[...]
        turned = upstream * cos - partner(upstream, lane, head_size) * sin
        inverse = lax.rsqrt(half_sums(part * part, lane, head_size) / head_size + EPS)
        scaled = turned * gain
        inner = half_sums(scaled * part, lane, head_size) / head_size
        grad = inverse * scaled - part * inverse * inverse * inverse * inner
        gain_part = jnp.sum(turned * part * inverse, axis=0, keepdims=True)
        if not is_query:
            grad = jnp.where(lane < head_size, grad, upstream)
            gain_part = jnp.where(lane[:1] < head_size, gain_part, 0.0)
        totals[0 if is_query else 1] += gain_part
        out_ref[:, at : at + LANES] = grad.astype(BF)
    gain_ref[0] = jnp.concatenate(totals, axis=0)


def unproject(raw, dq, dkv, cos, sin, query_gain, key_gain, head_size):
    rows, cols = raw.shape
    q_width = dq.shape[1]
    tile = 256
    whole = lambda i: (0, 0)
    step = lambda i: (i, 0)
    return pl.pallas_call(
        functools.partial(unproject_kernel, head_size),
        grid=(rows // tile,),
        in_specs=[
            pl.BlockSpec((tile, cols), step),
            pl.BlockSpec((tile, q_width), step),
            pl.BlockSpec((tile, cols - q_width), step),
            pl.BlockSpec((tile, LANES), step),
            pl.BlockSpec((tile, LANES), step),
            pl.BlockSpec((1, LANES), whole),
            pl.BlockSpec((1, LANES), whole),
        ],
        out_specs=[
            pl.BlockSpec((tile, cols), step),
            pl.BlockSpec((1, 2, LANES), lambda i: (i, 0, 0)),
        ],
        out_shape=[
            jax.ShapeDtypeStruct((rows, cols), BF),
            jax.ShapeDtypeStruct((rows // tile, 2, LANES), F32),
        ],
        compiler_params=pltpu.CompilerParams(vmem_limit_bytes=VMEM_LIMIT),
        cost_estimate=CHEAP,
    )(raw, dq, dkv, cos, sin, query_gain, key_gain)


def head_parts(pair, lane, head_size):
    return (
        jnp.where(lane < head_size, pair, 0.0).astype(BF),
        jnp.where(lane < head_size, pltpu.roll(pair, head_size, 1), 0.0).astype(BF),
    )


def attend_kernel(head_size, lows, first, last, code_ref, base_ref, q_ref, row_ref, key_ref, *refs):
    kv_refs, refs = refs[:lows], refs[lows:]
    if not first:
        (acc_in, sum_in), refs = refs[:2], refs[2:]
    if last:
        exact_ref, low_ref, lse_ref, qs_ref, acc_ref, sum_ref = refs
    else:
        acc_out, sum_out, qs_ref, acc_ref, sum_ref = refs
    batch = pl.program_id(0)
    count = row_ref.shape[1]
    factor = LOG2E * head_size**-0.5
    lane = lane_index((count, LANES))
    some = functools.reduce(jnp.maximum, [code_ref[batch, low] for low in range(lows)]) > 0

    @pl.when(some)
    def _():
        both = q_ref[:, 0].reshape(count, LANES).astype(F32)
        qs_ref[0], qs_ref[1] = head_parts(both, lane, head_size)

    if first:
        acc_ref[...] = jnp.zeros_like(acc_ref)
        sum_ref[...] = jnp.zeros_like(sum_ref)
    else:
        acc_ref[...] = acc_in[0, 0]
        sum_ref[...] = sum_in[0, 0]

    def one(low, masked):
        keys = kv_refs[low][:, 0].reshape(count, LANES)
        if masked:
            key_pos = key_ref[...] + base_ref[low]
            allowed = (key_pos <= row_ref[0, :, 0:1]) & (key_pos >= row_ref[0, :, 1:2])
        for head in range(2):
            exps = jnp.exp2(dot_back(qs_ref[head], keys) * factor)
            if masked:
                exps = jnp.where(allowed, exps, 0.0)
            partial = exps[:, :LANES]
            for lane_at in range(LANES, count, LANES):
                partial = partial + exps[:, lane_at : lane_at + LANES]
            sum_ref[head] += partial
            acc_ref[head] += dot_plain(exps.astype(BF), keys)

    for low in range(lows):
        code = code_ref[batch, low]
        pl.when(code == 1)(functools.partial(one, low, False))
        pl.when(code == 2)(functools.partial(one, low, True))

    if not last:
        acc_out[0, 0] = acc_ref[...]
        sum_out[0, 0] = sum_ref[...]
        return
    results = []
    for head in range(2):
        total = jnp.sum(sum_ref[head], axis=-1, keepdims=True)
        results.append(acc_ref[head] / total)
        wide = jnp.broadcast_to(jnp.log2(total), (count, LANES))
        lse_ref[0, 0, head] = wide.T[:8]
    joined = jnp.where(lane < head_size, pltpu.roll(results[0], head_size, 1), results[1])
    joined = joined.reshape(exact_ref.shape[0], -1, LANES)
    exact_ref[:, 0] = joined
    low_ref[:, 0] = joined.astype(BF)


def attend(codes, bases, query, kvs, row_info, key_pos, state, last, head_size):
    slots, batches, rows, q_width = query.shape
    count = slots * rows
    pairs = q_width // LANES
    pick = lambda b, p, *_: (0, b, 0, p)
    by_pair = lambda b, p, *_: (b, p, 0, 0, 0)
    slab = pl.BlockSpec((slots, 1, rows, LANES), pick)
    wide = pl.BlockSpec((1, 1, 2, count, LANES), by_pair)
    wide_shape = jax.ShapeDtypeStruct((batches, pairs, 2, count, LANES), F32)
    if last:
        out_specs = [slab, slab, pl.BlockSpec((1, 1, 2, 8, count), by_pair)]
        out_shape = [
            jax.ShapeDtypeStruct(query.shape, F32),
            jax.ShapeDtypeStruct(query.shape, BF),
            jax.ShapeDtypeStruct((batches, pairs, 2, 8, count), F32),
        ]
    else:
        out_specs, out_shape = [wide, wide], [wide_shape, wide_shape]
    return pl.pallas_call(
        functools.partial(attend_kernel, head_size, len(kvs), not state, last),
        grid_spec=pltpu.PrefetchScalarGridSpec(
            num_scalar_prefetch=2,
            grid=(batches, pairs),
            in_specs=[
                slab,
                pl.BlockSpec((1, count, 2), lambda b, p, *_: (b, 0, 0)),
                pl.BlockSpec((1, count), lambda b, p, *_: (0, 0)),
            ]
            + [slab] * len(kvs)
            + [wide] * len(state),
            out_specs=out_specs,
            scratch_shapes=[
                pltpu.VMEM((2, count, LANES), BF),
                pltpu.VMEM((2, count, LANES), F32),
                pltpu.VMEM((2, count, LANES), F32),
            ],
        ),
        out_shape=out_shape,
        compiler_params=pltpu.CompilerParams(vmem_limit_bytes=VMEM_LIMIT),
        cost_estimate=CHEAP,
    )(codes, bases, query, row_info, key_pos, *kvs, *state)


def attend_back_kernel(
    head_size,
    lows,
    first,
    last,
    code_ref,
    base_ref,
    q_ref,
    up_ref,
    exact_ref,
    lse_ref,
    row_ref,
    key_ref,
    *refs,
):
    kv_refs, refs = refs[:lows], refs[lows:]
    if not first:
        acc_in, refs = refs[0], refs[1:]
    dkv_refs, refs = refs[:lows], refs[lows:]
    out_ref, qs_ref, us_ref, acc_ref, delta_ref = refs
    batch = pl.program_id(0)
    count = row_ref.shape[2]
    scale = head_size**-0.5
    factor = LOG2E * scale
    lane = lane_index((count, LANES))
    some = functools.reduce(jnp.maximum, [code_ref[batch, low] for low in range(lows)]) > 0

    @pl.when(some)
    def _():
        both = q_ref[:, 0].reshape(count, LANES).astype(F32)
        qs_ref[0], qs_ref[1] = head_parts(both, lane, head_size)
        upper = up_ref[:, 0].reshape(count, LANES).astype(F32)
        us_ref[0] = jnp.where(lane < head_size, 0.0, pltpu.roll(upper, head_size, 1)).astype(BF)
        us_ref[1] = jnp.where(lane < head_size, 0.0, upper).astype(BF)
        products = upper * exact_ref[:, 0].reshape(count, LANES)
        for head in range(2):
            inside = (lane < head_size) if head == 0 else (lane >= head_size)
            total = jnp.sum(jnp.where(inside, products, 0.0), axis=-1, keepdims=True)
            delta_ref[head] = jnp.broadcast_to(total, (count, LANES)).T[:8]

    acc_ref[...] = jnp.zeros_like(acc_ref) if first else acc_in[0, 0]

    def none(low):
        dkv_refs[low][:, 0] = jnp.zeros((kv_refs[low].shape[0],) + kv_refs[low].shape[2:], BF)

    def one(low, masked):
        keys = kv_refs[low][:, 0].reshape(count, LANES)
        if masked:
            key_pos = key_ref[...] + base_ref[low]
            allowed = (key_pos <= row_ref[0, 0:1]) & (key_pos >= row_ref[0, 1:2])
        grad_kv = jnp.zeros((count, LANES), F32)
        for head in range(2):
            scores = dot_back(keys, qs_ref[head]) * factor
            probs = jnp.exp2(scores - lse_ref[0, 0, head, 0:1])
            if masked:
                probs = jnp.where(allowed, probs, 0.0)
            grads = dot_back(keys, us_ref[head])
            grads = (probs * (grads - delta_ref[head, 0:1])).astype(BF)
            grad_kv += dot_plain(probs.astype(BF), us_ref[head])
            grad_kv += dot_plain(grads, qs_ref[head]) * scale
            acc_ref[head] += dot_outer(grads, keys)
        dkv_refs[low][:, 0] = grad_kv.astype(BF).reshape(kv_refs[low].shape[0], -1, LANES)

    for low in range(lows):
        code = code_ref[batch, low]
        pl.when(code == 0)(functools.partial(none, low))
        pl.when(code == 1)(functools.partial(one, low, False))
        pl.when(code == 2)(functools.partial(one, low, True))

    if not last:
        out_ref[0, 0] = acc_ref[...]
        return
    joined = jnp.where(lane < head_size, acc_ref[0], pltpu.roll(acc_ref[1], head_size, 1))
    out_ref[:, 0] = (joined * scale).reshape(out_ref.shape[0], -1, LANES)


def attend_back(codes, bases, query, upstream, exact, lse, kvs, row_info, key_pos, state, last, head_size):
    slots, batches, rows, q_width = query.shape
    count = slots * rows
    pairs = q_width // LANES
    pick = lambda b, p, *_: (0, b, 0, p)
    by_pair = lambda b, p, *_: (b, p, 0, 0, 0)
    slab = pl.BlockSpec((slots, 1, rows, LANES), pick)
    wide = pl.BlockSpec((1, 1, 2, count, LANES), by_pair)
    wide_shape = jax.ShapeDtypeStruct((batches, pairs, 2, count, LANES), F32)
    return pl.pallas_call(
        functools.partial(attend_back_kernel, head_size, len(kvs), not state, last),
        grid_spec=pltpu.PrefetchScalarGridSpec(
            num_scalar_prefetch=2,
            grid=(batches, pairs),
            in_specs=[
                slab,
                slab,
                slab,
                pl.BlockSpec((1, 1, 2, 8, count), by_pair),
                pl.BlockSpec((1, 2, count), lambda b, p, *_: (b, 0, 0)),
                pl.BlockSpec((count, 1), lambda b, p, *_: (0, 0)),
            ]
            + [slab] * len(kvs)
            + [wide] * len(state),
            out_specs=[slab] * len(kvs) + [slab if last else wide],
            scratch_shapes=[
                pltpu.VMEM((2, count, LANES), BF),
                pltpu.VMEM((2, count, LANES), BF),
                pltpu.VMEM((2, count, LANES), F32),
                pltpu.VMEM((2, 8, count), F32),
            ],
        ),
        out_shape=[jax.ShapeDtypeStruct(kvs[0].shape, BF)] * len(kvs)
        + [jax.ShapeDtypeStruct(query.shape, F32) if last else wide_shape],
        compiler_params=pltpu.CompilerParams(vmem_limit_bytes=VMEM_LIMIT),
        cost_estimate=CHEAP,
    )(codes, bases, query, upstream, exact, lse, row_info, key_pos, *kvs, *state)


TILE = 384


def tiled_columns(gate, upper):
    lead = gate.shape[:-1]
    parts = [part.reshape(lead + (-1, 1, TILE)) for part in (gate, upper)]
    return jnp.concatenate(parts, axis=-2).reshape(lead + (-1,))


def untiled_columns(both):
    lead = both.shape[:-1]
    parts = both.reshape(lead + (-1, 2, TILE))
    return [parts[..., index, :].reshape(lead + (-1,)) for index in range(2)]


def block_order():
    his, los, heads, mids = split_sizes()
    return tuple(
        (hi * los + lo, head * mids + mid)
        for head in range(heads)
        for hi in range(his)
        for mid in range(mids)
        for lo in range(los)
    )


def feed_kernel(order, x_ref, cot_ref, w_ref, wd_ref, hid_ref, grad_ref, two_ref, w_all, acc_ref):
    rows = w_ref.shape[2]
    for index, (data, source) in enumerate(order):
        w_all[pl.ds(index * rows, rows)] = w_ref[data, source]
    step = pl.program_id(0)
    count = x_ref.shape[0]
    part = math.gcd(count, 256)

    @pl.when(step == 0)
    def _():
        acc_ref[...] = jnp.zeros_like(acc_ref)

    for first in range(0, count, part):
        at = pl.ds(first, part)
        both = dot_plain(x_ref[at], w_all[...])
        gate, upper = both[:, :TILE], both[:, TILE:]
        grad_hidden = dot_back(cot_ref[at], wd_ref[...])
        sigmoid = jax.nn.sigmoid(gate)
        silu = gate * sigmoid
        hid_ref[at] = (silu * upper).astype(BF)
        grad_gate = (grad_hidden * upper * sigmoid * (1.0 + gate * (1.0 - sigmoid))).astype(BF)
        grad_upper = (grad_hidden * silu).astype(BF)
        grads = jnp.concatenate([grad_gate, grad_upper], axis=1)
        grad_ref[at] = grads
        acc_ref[at] += dot_back(grads, w_all[...])

    @pl.when(step == pl.num_programs(0) - 1)
    def _():
        two_ref[...] = acc_ref[...].astype(BF)


def feed(x, cot, w_both, wd):
    count, width = x.shape
    cols = wd.shape[0]
    whole = lambda i: (0, 0)
    column = lambda i: (0, i)
    return pl.pallas_call(
        functools.partial(feed_kernel, block_order()),
        grid=(cols // TILE,),
        in_specs=[
            pl.BlockSpec((count, width), whole),
            pl.BlockSpec((count, width), whole),
            pl.BlockSpec(w_both.shape[:3] + (2 * TILE,), lambda i: (0, 0, 0, i)),
            pl.BlockSpec((TILE, width), lambda i: (i, 0)),
        ],
        out_specs=[
            pl.BlockSpec((count, TILE), column),
            pl.BlockSpec((count, 2 * TILE), column),
            pl.BlockSpec((count, width), whole),
        ],
        out_shape=[
            jax.ShapeDtypeStruct((count, cols), BF),
            jax.ShapeDtypeStruct((count, 2 * cols), BF),
            jax.ShapeDtypeStruct((count, width), BF),
        ],
        scratch_shapes=[pltpu.VMEM((width, 2 * TILE), BF), pltpu.VMEM((count, width), F32)],
        compiler_params=pltpu.CompilerParams(vmem_limit_bytes=VMEM_LIMIT),
        cost_estimate=CHEAP,
    )(x, cot, w_both, wd)


def gate_grad_kernel(order, x_ref, grad_ref, out_ref, xt_ref):
    rows = out_ref.shape[2]

    @pl.when(pl.program_id(0) == 0)
    def _():
        xt_ref[...] = x_ref[...].T

    result = dot_plain(xt_ref[...], grad_ref[...]).astype(BF)
    for index, (data, source) in enumerate(order):
        out_ref[data, source] = result[index * rows : (index + 1) * rows]


def gate_grads(x, grads, shape):
    count, width = x.shape
    return pl.pallas_call(
        functools.partial(gate_grad_kernel, block_order()),
        grid=(grads.shape[1] // (2 * TILE),),
        in_specs=[
            pl.BlockSpec((count, width), lambda i: (0, 0)),
            pl.BlockSpec((count, 2 * TILE), lambda i: (0, i)),
        ],
        out_specs=pl.BlockSpec(shape[:3] + (2 * TILE,), lambda i: (0, 0, 0, i)),
        out_shape=jax.ShapeDtypeStruct(shape, BF),
        scratch_shapes=[pltpu.VMEM((width, count), BF)],
        compiler_params=pltpu.CompilerParams(vmem_limit_bytes=VMEM_LIMIT),
        cost_estimate=CHEAP,
    )(x, grads)


def down_kernel(hid_ref, cot_ref, wd_ref, grad_ref, out_ref, acc_ref):
    step = pl.program_id(0)
    hidden = hid_ref[...]
    grad_ref[...] = dot_outer(hidden, cot_ref[...]).astype(BF)
    part = dot_plain(hidden, wd_ref[...])

    @pl.when(step == 0)
    def _():
        acc_ref[...] = part

    @pl.when(step > 0)
    def _():
        acc_ref[...] += part

    @pl.when(step == pl.num_programs(0) - 1)
    def _():
        out_ref[...] = acc_ref[...].astype(BF)


def down_grads(hidden, cot, wd):
    count, cols = hidden.shape
    width = wd.shape[1]
    tile = TILE
    whole = lambda i: (0, 0)
    return pl.pallas_call(
        down_kernel,
        grid=(cols // tile,),
        in_specs=[
            pl.BlockSpec((count, tile), lambda i: (0, i)),
            pl.BlockSpec((count, width), whole),
            pl.BlockSpec((tile, width), lambda i: (i, 0)),
        ],
        out_specs=[
            pl.BlockSpec((tile, width), lambda i: (i, 0)),
            pl.BlockSpec((count, width), whole),
        ],
        out_shape=[
            jax.ShapeDtypeStruct((cols, width), BF),
            jax.ShapeDtypeStruct((count, width), BF),
        ],
        scratch_shapes=[pltpu.VMEM((count, width), F32)],
        compiler_params=pltpu.CompilerParams(vmem_limit_bytes=VMEM_LIMIT),
        cost_estimate=CHEAP,
    )(hidden, cot, wd)


def per_device(
    inputs,
    cotangent,
    attn_gain,
    w_query,
    w_key,
    w_value,
    w_output,
    query_gain,
    key_gain,
    ffn_gain,
    w_gate,
    w_up,
    w_down,
    doc_starts,
):
    heads, mids = lax.axis_size("heads"), lax.axis_size("mid")
    his, los = lax.axis_size("hi"), lax.axis_size("lo")
    slots = heads * mids
    batches, _, rows, width = inputs.shape
    block = rows * heads
    count = slots * rows
    head_size = query_gain.shape[0]
    w_rows = w_query.shape[0]
    q_width = w_query.shape[1] // slots
    pairs = w_key.shape[1] // head_size // slots
    ff_width = w_gate.shape[1] // slots

    by_slot = lambda w: w.reshape(w_rows, slots, -1)
    kv_cols = jnp.stack(
        [
            w_key.reshape(w_rows, slots, pairs, head_size),
            w_value.reshape(w_rows, slots, pairs, head_size),
        ],
        axis=3,
    )
    qkv_parts = jnp.concatenate([by_slot(w_query), kv_cols.reshape(w_rows, slots, -1)], axis=2)
    qkv_mine = columns_out(qkv_parts.transpose(1, 0, 2))
    out_rows, down_rows = w_output.shape[0], w_down.shape[0]
    own_in, own_cot = inputs[:, 0], cotangent[:, 0]
    gather_in, row_part = own_in, jnp.concatenate([w_output, w_down], axis=0)
    w_gate_late, w_up_late = w_gate, w_up
    if is_quad():
        qkv_mine, gather_in, row_part = together(qkv_mine, gather_in, row_part)
        in_near = group_near(gather_in)
        row_part = rows_out(row_part)
        *in_near, row_part = together(*in_near, row_part)
        in_far = group_far(*in_near)
        *in_far, w_gate_late, w_up_late = together(*in_far, w_gate, w_up)
        in_all = group_joined(gather_in, in_near, in_far)
    else:
        row_part = rows_out(row_part)
        in_all = group_gather(gather_in)
    w_qkv = natural_rows(gather_data(qkv_mine))
    row_all = gather_data(row_part)
    fast = fast_rows(w_rows) and ff_width % TILE == 0
    if fast:
        gate_up_parts = tiled_columns(by_slot(w_gate_late), by_slot(w_up_late))
    else:
        gate_up_parts = jnp.concatenate([by_slot(w_gate_late), by_slot(w_up_late)], axis=2)
    gate_up_mine = columns_out_async(gate_up_parts.transpose(1, 0, 2))

    head_at, mid_at = slot_places()
    row_at = jnp.arange(rows, dtype=jnp.int32)
    hi_at, lo_at = lax.axis_index("hi"), lax.axis_index("lo")
    first_pos = ((mid_at * los * block + head_at * rows)[:, None] + row_at[None, :]).reshape(count)
    row_pos = first_pos + hi_at * (mids * los * block) + lo_at * block
    lows = [lo_at] if los == 1 else [lo_at, 1 - lo_at]
    starts = doc_starts[:, None, :]
    row_begin = jnp.max(jnp.where(starts <= row_pos[None, :, None], starts, 0), axis=2)
    row_both = jnp.broadcast_to(row_pos[None], (batches, count))
    begin_low, begin_high = (
        jnp.min(row_begin, axis=1)[:, None],
        jnp.max(row_begin, axis=1)[:, None],
    )

    def step_codes(step):
        bases = jnp.stack([(hi_at - step) * (mids * los * block) + low * block for low in lows])
        key_low, key_high = (bases + jnp.min(first_pos))[None], (bases + jnp.max(first_pos))[None]
        none = (key_low > jnp.max(row_pos)) | (key_high < begin_low) | (hi_at < step)
        full = (key_high <= jnp.min(row_pos)) & (key_low >= begin_high)
        return jnp.where(none, 0, jnp.where(full, 1, 2)).astype(jnp.int32), bases.astype(jnp.int32)

    steps = [step_codes(step) for step in range(his)]
    info_cols = jnp.stack([row_both, row_begin], axis=2)
    info_rows = jnp.stack([row_both, row_begin], axis=1)

    half = head_size // 2
    frequency = THETA ** (-(jnp.arange(half, dtype=F32) * 2.0 / head_size))
    turn_pos = (row_both - row_begin).reshape(batches, slots, rows).transpose(1, 0, 2)
    angles = turn_pos.reshape(-1).astype(F32)[:, None] * frequency[None, :]
    cos, sin = jnp.cos(angles), jnp.sin(angles)
    cos = jnp.concatenate([cos] * 4, axis=1)
    sin = jnp.concatenate([-sin, sin, -sin, sin], axis=1)
    q_gain = jnp.concatenate([query_gain, query_gain])[None]
    k_gain = jnp.concatenate([key_gain, key_gain])[None]

    in_wide = in_all.reshape(-1, width).astype(F32)
    in_unit = in_wide * rms_inverse(in_wide)
    normed = (in_unit * attn_gain).astype(BF)
    raw, query, kv = project(normed, w_qkv, cos, sin, q_gain, k_gain, q_width, head_size)
    query = query.reshape(slots, batches, rows, q_width)
    moving = kv.reshape(slots, batches, rows, -1)
    own_cot_late, moving = together(own_cot, moving)
    kv_steps, state = [], ()
    for step in range(his):
        if step:
            moving = lax.ppermute(moving, "hi", [(i, i + 1) for i in range(step - 1, his - 1)])
            moving, *state = together(moving, *state)
        if step == his - 1:
            moving, gate_up_mine = together(moving, gate_up_mine)
            gate_up_all = gather_data(gate_up_mine)
        kv_steps.append([moving] if los == 1 else [moving, other_low(moving)])
        state = attend(
            *steps[step],
            query,
            kv_steps[step],
            info_cols,
            first_pos[None],
            tuple(state),
            step == his - 1,
            head_size,
        )
        state = list(state)
        if not is_quad():
            continue
        if step == 0:
            own_cot_late, *state = together(own_cot_late, *state)
            cot_near = group_near(own_cot_late)
        if step == 1:
            *cot_near, state[0] = together(*cot_near, state[0])
            cot_far = group_far(*cot_near)
        if step == 2:
            *cot_far, row_all, state[0] = together(*cot_far, row_all, state[0])
            wo_part = row_all[:, :out_rows].reshape(-1, width)
            wo_near = group_near(wo_part)
        if step == 3:
            *wo_near, state[1] = together(*wo_near, state[1])
            wo_far = group_far(*wo_near)
    exact, attn, lse = state
    if is_quad():
        cot_all = group_joined(own_cot_late, cot_near, cot_far)
        wo_full = group_joined(wo_part, wo_near, wo_far)
    else:
        cot_all = group_gather(own_cot)
        wo_full = group_gather(row_all[:, :out_rows].reshape(-1, width))
    wo_full = wo_full.reshape(-1, width)
    attn_wide = columns_out_async(attn.reshape(slots, batches * rows, q_width))
    attn_wide = jnp.concatenate([attn_wide[slot] for slot in range(slots)], axis=1)
    attn_wide, wo_full = together(attn_wide, wo_full)
    middle = own_in.reshape(-1, width).astype(F32) + dot_plain(attn_wide, wo_full)

    normed_two = (middle * rms_inverse(middle) * ffn_gain).astype(BF)
    normed_two, cot_all, wd_all = together(normed_two, cot_all, row_all[:, out_rows:])
    normed_two_all = group_gather(normed_two).reshape(-1, width)
    normed_two_all, gate_up_all = together(normed_two_all, gate_up_all)
    cot_rows = cot_all.reshape(-1, width)
    wd_use = wd_all.reshape(-1, width)
    if fast:
        hidden, grads, grad_two = feed(normed_two_all, cot_rows, gate_up_all, wd_use)
        grad_two, grads, hidden = together(grad_two, grads, hidden)
        grad_gate_up = gate_grads(normed_two_all, grads, gate_up_all.shape)
        grad_gate_up = grad_gate_up.reshape(his * los, slots * w_rows, -1)
        grad_down, out_part = down_grads(hidden, cot_rows, wd_use)
    else:
        w_both = natural_rows(gate_up_all)
        both = dot_plain(normed_two_all, w_both)
        gate, upper = both[:, :ff_width], both[:, ff_width:]
        grad_hidden = dot_back(cot_rows, wd_use)
        sigmoid = jax.nn.sigmoid(gate)
        silu = gate * sigmoid
        hidden = (silu * upper).astype(BF)
        grad_gate = grad_hidden * upper * sigmoid * (1.0 + gate * (1.0 - sigmoid))
        grads = jnp.concatenate([grad_gate, grad_hidden * silu], axis=1).astype(BF)
        grad_two = dot_back(grads, w_both).astype(BF)
        grad_gate_up = scatter_order(dot_outer(normed_two_all, grads).astype(BF), w_rows)
        grad_down = dot_outer(hidden, cot_rows).astype(BF)
        out_part = dot_plain(hidden, wd_use).astype(BF)
    in_slots = lambda total: total.reshape(slots, batches * rows, width)
    out_part = in_slots(out_part)
    two_sum = GroupSum(in_slots(grad_two))
    (grad_gate_up,) = two_sum.second(grad_gate_up)
    grad_down, out_part = two_sum.hold(grad_down, out_part)
    grad_two = two_sum.done()
    gate_up_sum = scatter_data(grad_gate_up).reshape(slots, w_rows, -1)
    grad_mid_part, ffn_gain_part = norm_back(middle, ffn_gain, grad_two)
    grad_middle = own_cot.reshape(-1, width).astype(F32) + grad_mid_part

    grad_middle_low = grad_middle.astype(BF)
    grad_attn = dot_back(grad_middle_low, wo_full).astype(BF)
    grad_attn = jnp.stack(
        [grad_attn[:, slot * q_width : (slot + 1) * q_width] for slot in range(slots)]
    )
    grad_attn, grad_middle_low = together(grad_attn, grad_middle_low)
    grad_output = dot_outer(attn_wide, grad_middle_low)
    grad_output = grad_output.astype(BF).reshape(slots, -1, width)
    grad_attn = columns_out_async(grad_attn).reshape(query.shape)
    sums = [GroupSum(grad_output), None]
    state, moving = (), None
    for turn in range(1, his + 1):
        step = his - turn
        *dkv, state_out = attend_back(
            *steps[step],
            query,
            grad_attn,
            exact,
            lse,
            kv_steps[step],
            info_rows,
            first_pos[:, None],
            state,
            turn == his,
            head_size,
        )
        if turn > 1:
            *dkv, moving = together(*dkv, moving)
        if turn == his:
            *dkv, gate_up_sum = together(*dkv, gate_up_sum)
            gate_up_back = columns_out_async(gate_up_sum)
        parts = [dkv[0]] + ([other_low(dkv[1])] if los == 2 else [])
        parts += [moving] if turn > 1 else []
        if turn < his:
            low, state_out = together(low_sum(*parts), state_out)
            moving = lax.ppermute(low, "hi", [(i, i - 1) for i in range(his - turn, his)])
        if turn == 1:
            (state_out,) = sums[0].second(state_out)
        if turn == min(2, his):
            (state_out,) = sums[0].hold(state_out)
            out_part, state_out = together(out_part, state_out)
            sums[1] = GroupSum(out_part)
            output_part = sums[0].done().astype(BF)
            row_grads = jnp.concatenate(
                [
                    output_part.reshape(his * los, out_rows, width),
                    grad_down.reshape(his * los, down_rows, width),
                ],
                axis=1,
            )
            row_sum = scatter_data(row_grads)
        if turn == min(3, his):
            (state_out,) = sums[1].second(state_out)
        state = (state_out,)
    out_sum = sums[1].done()
    dkv_mine = sum(part.astype(F32) for part in parts)
    dq = state[0]
    grad_raw, head_gains = unproject(
        raw,
        dq.reshape(-1, q_width),
        dkv_mine.reshape(raw.shape[0], -1),
        cos,
        sin,
        q_gain,
        k_gain,
        head_size,
    )
    block_out = (middle + out_sum).astype(BF)
    grad_raw, gate_up_back, row_sum = together(grad_raw, gate_up_back, row_sum)
    grad_qkv = dot_outer(normed, grad_raw).astype(BF)
    qkv_sum = scatter_data(scatter_order(grad_qkv, w_rows)).reshape(slots, w_rows, -1)
    row_back = rows_back(row_sum).astype(F32)
    grad_normed_low = dot_back(grad_raw, w_qkv).astype(BF)
    normed_sum = GroupSum(grad_normed_low.reshape(slots, batches * rows, width))
    normed_sum.second()
    grad_normed = normed_sum.done()
    grad_in_part, _ = norm_back(own_in.reshape(-1, width).astype(F32), attn_gain, grad_normed)
    grad_inputs = grad_middle + grad_in_part
    attn_gain_part = jnp.sum(grad_normed_low.astype(F32) * in_unit, axis=0)

    qkv_cols = columns_out(qkv_sum).transpose(1, 0, 2).astype(F32)
    if fast:
        gate_cols, up_cols = untiled_columns(gate_up_back.transpose(1, 0, 2))
    else:
        gate_cols, up_cols = jnp.split(gate_up_back.transpose(1, 0, 2), 2, axis=2)
    kv_sums = qkv_cols[:, :, q_width:].reshape(w_rows, slots, pairs, 2, head_size)
    head_sums = jnp.sum(head_gains, axis=0).reshape(2, 2, head_size).sum(axis=1)
    gains = all_sum(
        jnp.concatenate(
            [attn_gain_part, jnp.sum(ffn_gain_part, axis=0), head_sums[0], head_sums[1]]
        )
    )
    return (
        block_out.reshape(batches, 1, rows, width),
        grad_inputs.reshape(batches, 1, rows, width),
        gains[:width],
        qkv_cols[:, :, :q_width].reshape(w_rows, -1),
        kv_sums[:, :, :, 0].reshape(w_rows, -1),
        kv_sums[:, :, :, 1].reshape(w_rows, -1),
        row_back[:out_rows],
        gains[2 * width : 2 * width + head_size],
        gains[2 * width + head_size :],
        gains[width : 2 * width],
        gate_cols.reshape(w_rows, -1).astype(F32),
        up_cols.reshape(w_rows, -1).astype(F32),
        row_back[out_rows:],
    )


def solution(mesh):
    heads, seq = mesh.shape["heads"], mesh.shape["seq"]
    rows_spec = P(None, SEQ, "heads", None)
    weight_spec = P(ALL, None)

    def run(*args):
        kv_heads = args[4].shape[1] // args[7].shape[0]
        low = 2 if seq % 2 == 0 else 1
        mid = 2 if seq % (2 * low) == 0 and kv_heads % (2 * heads) == 0 else 1
        split = Mesh(
            mesh.devices.reshape(heads, seq // (mid * low), mid, low), ("heads",) + SEQ
        )
        return jax.shard_map(
            per_device,
            mesh=split,
            in_specs=(
                (rows_spec, rows_spec, P())
                + (weight_spec,) * 4
                + (P(), P(), P())
                + (weight_spec,) * 3
                + (P(),)
            ),
            out_specs=(
                (rows_spec, rows_spec, P())
                + (weight_spec,) * 4
                + (P(), P(), P())
                + (weight_spec,) * 3
            ),
            check_vma=False,
        )(*args)

    return run
```

```python
import functools
import math

import jax
import jax.numpy as jnp
from jax import lax
from jax.experimental import pallas as pl
from jax.experimental.pallas import tpu as pltpu
from jax.sharding import Mesh, PartitionSpec as P

EPS = 1e-05
THETA = 1000000.0
LANES = 128
LOG2E = math.log2(math.e)
GROUP = ("heads", "mid")
DATA = ("hi", "lo")
SEQ = ("hi", "mid", "lo")
ALL = ("heads",) + SEQ
BF = jnp.bfloat16
F32 = jnp.float32
VMEM_LIMIT = 48 * 1024 * 1024
CHEAP = pl.CostEstimate(flops=1, bytes_accessed=1, transcendentals=0)
STEP = pl.CostEstimate(flops=1, bytes_accessed=1, transcendentals=0)


def dot_plain(left_side, right_side):
    return jnp.dot(left_side, right_side, preferred_element_type=F32)


def dot_back(left_side, right_side):
    return lax.dot_general(
        left_side, right_side, (((1,), (1,)), ((), ())), preferred_element_type=F32
    )


def dot_outer(left_side, right_side):
    return lax.dot_general(
        left_side, right_side, (((0,), (0,)), ((), ())), preferred_element_type=F32
    )


def together(*values):
    return lax.optimization_barrier(values)


def rms_inverse(values):
    return lax.rsqrt(jnp.mean(values * values, axis=-1, keepdims=True) + EPS)


def norm_back(values, gain_vec, upstream):
    inverse = rms_inverse(values)
    scaled = upstream * gain_vec
    inner_mean = jnp.mean(scaled * values, axis=-1, keepdims=True)
    grad_values = inverse * scaled - values * inverse * inverse * inverse * inner_mean
    return (grad_values, upstream * values * inverse)


def is_quad():
    return lax.axis_size("heads") == 2 and lax.axis_size("mid") == 2


def swap(part, axis):
    return lax.ppermute(part, axis, [(0, 1), (1, 0)])


def group_rank():
    return lax.axis_index("heads") * lax.axis_size("mid") + lax.axis_index("mid")


def block_at(parts, index):
    return lax.dynamic_index_in_dim(parts, index, axis=0, keepdims=False)


def in_order(blocks):
    rank = group_rank()
    total = jnp.zeros((4,) + blocks[0].shape, blocks[0].dtype)
    for slot, block in enumerate(blocks):
        total = lax.dynamic_update_index_in_dim(total, block, rank ^ slot, axis=0)
    return total


def group_near(part):
    return swap(part, "mid"), swap(part, "heads")


def group_far(by_mid, by_heads):
    half = by_mid.shape[0] // 2
    return swap(by_mid[:half], "heads"), swap(by_heads[half:], "mid")


def join_kernel(rank_ref, gain_ref, own_ref, mid_ref, head_ref, low_ref, high_ref, out_ref, *normed_ref):
    source = pl.program_id(0) ^ rank_ref[0]
    half = low_ref.shape[0]
    for slot, ref in enumerate((own_ref, mid_ref, head_ref)):

        @pl.when(source == slot)
        def _(ref=ref):
            out_ref[0] = ref[...]

    @pl.when(source == 3)
    def _():
        out_ref[0, :half] = low_ref[...]
        out_ref[0, half:] = high_ref[...]

    if normed_ref:
        values = out_ref[0].astype(F32)
        normed_ref[0][0] = (values * rms_inverse(values) * gain_ref[...]).astype(BF)


def group_joined(part, near, far, gain=None):
    width = part.shape[-1]
    flat = [block.reshape(-1, width) for block in (part, *near, *far)]
    whole = lambda i, rank: (0, 0)
    shape = (4,) + flat[0].shape
    outs = 1 if gain is None else 2
    out_spec = pl.BlockSpec((1,) + flat[0].shape, lambda i, rank: (i, 0, 0))
    gain_vec = jnp.zeros((1, width), F32) if gain is None else gain[None]
    result = pl.pallas_call(
        join_kernel,
        grid_spec=pltpu.PrefetchScalarGridSpec(
            num_scalar_prefetch=1,
            grid=(4,),
            in_specs=[pl.BlockSpec((1, width), whole)]
            + [pl.BlockSpec(block.shape, whole) for block in flat],
            out_specs=[out_spec] * outs,
        ),
        out_shape=[jax.ShapeDtypeStruct(shape, part.dtype)] * outs,
        compiler_params=pltpu.CompilerParams(vmem_limit_bytes=VMEM_LIMIT),
        cost_estimate=CHEAP,
    )(group_rank()[None].astype(jnp.int32), gain_vec, *flat)
    total = result[0].reshape((4,) + part.shape)
    return total if gain is None else (total, result[1].reshape(total.shape))


def group_gather(part):
    if not is_quad():
        return lax.all_gather(part, GROUP, axis=0, tiled=False)
    near = group_near(part)
    return group_joined(part, near, group_far(*near))


def group_gather_plain(part):
    return lax.all_gather(part, GROUP, axis=0, tiled=False)


def group_sum_plain(parts):
    flat = parts.reshape((-1,) + parts.shape[2:])
    return lax.psum_scatter(flat, GROUP, scatter_dimension=0, tiled=True)


class GroupSum:
    def __init__(self, parts):
        if is_quad():
            rank = group_rank()
            self.parts = [block_at(parts, rank ^ slot) for slot in range(4)]
            half = parts.shape[1] // 2
            far = self.parts[3]
            self.far = (swap(far[:half], "mid"), swap(far[half:], "heads"))
        else:
            self.total = group_sum_plain(parts)

    def second(self, *between):
        if is_quad():
            _, mid, head, _ = self.parts
            half = mid.shape[0] // 2
            far_low, far_high = self.far
            if between:
                far_low, far_high, *between = together(far_low, far_high, *between)
            for_mid = jnp.concatenate([mid[:half], low_sum(mid[half:], far_high)], axis=0)
            for_heads = jnp.concatenate([low_sum(head[:half], far_low), head[half:]], axis=0)
            self.near = (swap(for_mid, "mid"), swap(for_heads, "heads"))
        return between

    def hold(self, *later):
        if is_quad():
            near_mid, near_heads, *later = together(*self.near, *later)
            self.near = (near_mid, near_heads)
        return later

    def done(self):
        if not is_quad():
            return self.total.astype(F32)
        return self.parts[0].astype(F32) + self.near[0].astype(F32) + self.near[1].astype(F32)


def slot_places():
    mids = lax.axis_size("mid")
    slots = jnp.arange(lax.axis_size("heads") * mids, dtype=jnp.int32)
    return (slots // mids, slots % mids)


def sum_stages():
    stages = []
    for axis in ("lo", "mid", "heads", "hi"):
        size, step = lax.axis_size(axis), 1
        while step < size:
            pairs = [(i, i ^ step) for i in range(size)]
            stages.append(functools.partial(lax.ppermute, axis_name=axis, perm=pairs))
            step *= 2
    return stages


def all_sum(vector):
    for axis in ("lo", "mid", "heads", "hi"):
        size = lax.axis_size(axis)
        if size & (size - 1):
            vector = lax.psum(vector, axis)
            continue
        step = 1
        while step < size:
            vector = vector + lax.ppermute(vector, axis, [(i, i ^ step) for i in range(size)])
            step *= 2
    return vector


def columns_out(parts):
    return lax.all_to_all(parts, GROUP, split_axis=0, concat_axis=0, tiled=True)


def columns_out_async(parts):
    if not is_quad():
        return columns_out(parts)
    rank = group_rank()
    far = [(0, 3), (1, 2), (2, 1), (3, 0)]
    return in_order(
        [
            block_at(parts, rank),
            swap(block_at(parts, rank ^ 1), "mid"),
            swap(block_at(parts, rank ^ 2), "heads"),
            lax.ppermute(block_at(parts, rank ^ 3), GROUP, far),
        ]
    )


def ring(part, shift):
    size = lax.axis_size("hi")
    return lax.ppermute(part, "hi", [(i, (i + shift) % size) for i in range(size)])


def other_low(part):
    return swap(part, "lo")


def fast_rows(rows):
    return lax.axis_size("lo") == 2 and rows % 16 == 0


def data_ring(part):
    own = [part]
    for _ in range(lax.axis_size("hi") - 1):
        own.append(ring(own[-1], 1))
    return own, [other_low(piece) for piece in own]


def place_index():
    return jnp.stack(
        [lax.axis_index("hi"), lax.axis_index("lo"), lax.axis_index("heads"), lax.axis_index("mid")]
    ).astype(jnp.int32)


def block_row(at_ref, sizes, step, other, source):
    his, los, heads, mids = sizes
    hi = lax.rem(at_ref[0] - step + his, his)
    low = 1 - at_ref[1] if other else at_ref[1]
    if source is None:
        return hi * los + low
    return ((source // mids * his + hi) * mids + source % mids) * los + low


def split_sizes():
    return tuple(lax.axis_size(name) for name in ("hi", "lo", "heads", "mid"))


def place_kernel(sizes, sources, rows, at_ref, *refs):
    his = sizes[0]
    pieces, out_ref, sems = refs[: 2 * his], refs[2 * his], refs[2 * his + 1]
    copies = []
    for step in range(his):
        for other in range(2):
            for source in sources:
                first = block_row(at_ref, sizes, step, other, source) * rows
                piece = pieces[step + other * his]
                copies.append(
                    pltpu.make_async_copy(
                        piece if source is None else piece.at[source],
                        out_ref.at[pl.ds(pl.multiple_of(first, rows), rows)],
                        sems.at[len(copies)],
                    )
                )
    for copy in copies:
        copy.start()
    for copy in copies:
        copy.wait()


def placed(own, other):
    sizes = split_sizes()
    first = own[0]
    rows, cols = first.shape[-2:]
    sources = range(first.shape[0]) if first.ndim == 3 else (None,)
    total = rows * sizes[0] * sizes[1] * len(sources)
    anywhere = pl.BlockSpec(memory_space=pl.ANY)
    return pl.pallas_call(
        functools.partial(place_kernel, sizes, sources, rows),
        in_specs=[pl.BlockSpec(memory_space=pltpu.SMEM)] + [anywhere] * (2 * sizes[0]),
        out_specs=pl.BlockSpec(memory_space=pltpu.VMEM),
        out_shape=jax.ShapeDtypeStruct((total, cols), first.dtype),
        scratch_shapes=[pltpu.SemaphoreType.DMA((2 * sizes[0] * len(sources),))],
        compiler_params=pltpu.CompilerParams(vmem_limit_bytes=VMEM_LIMIT),
        cost_estimate=CHEAP,
    )(place_index(), *own, *other)


def unplace_kernel(sizes, sources, rows, at_ref, full_ref, own_ref, other_ref, sems):
    his = sizes[0]
    copies = []
    for step in range(his):
        for other in range(2):
            for source in sources:
                first = block_row(at_ref, sizes, step, other, source) * rows
                target = (other_ref if other else own_ref).at[step]
                copies.append(
                    pltpu.make_async_copy(
                        full_ref.at[pl.ds(pl.multiple_of(first, rows), rows)],
                        target if source is None else target.at[source],
                        sems.at[len(copies)],
                    )
                )
    for copy in copies:
        copy.start()
    for copy in copies:
        copy.wait()


def unplaced(full, rows, by_source):
    sizes = split_sizes()
    cols = full.shape[1]
    slots = sizes[2] * sizes[3]
    sources = range(slots) if by_source else (None,)
    shape = (sizes[0],) + ((slots,) if by_source else ()) + (rows, cols)
    anywhere = pl.BlockSpec(memory_space=pl.ANY)
    return pl.pallas_call(
        functools.partial(unplace_kernel, sizes, sources, rows),
        in_specs=[pl.BlockSpec(memory_space=pltpu.SMEM), pl.BlockSpec(memory_space=pltpu.VMEM)],
        out_specs=[anywhere, anywhere],
        out_shape=[jax.ShapeDtypeStruct(shape, full.dtype)] * 2,
        scratch_shapes=[pltpu.SemaphoreType.DMA((2 * sizes[0] * len(sources),))],
        compiler_params=pltpu.CompilerParams(vmem_limit_bytes=VMEM_LIMIT),
        cost_estimate=CHEAP,
    )(place_index(), full)


def natural_rows(gathered):
    his, los, heads, mids = split_sizes()
    rows, cols = gathered.shape[2:]
    parts = gathered.reshape(his, los, heads, mids, rows, cols)
    return parts.transpose(2, 0, 3, 1, 4, 5).reshape(-1, cols)


def gather_data(part):
    return lax.all_gather(part, DATA, axis=0, tiled=False)


def gather_rows(part):
    if fast_rows(part.shape[-2]):
        return placed(*data_ring(part))
    return natural_rows(gather_data(part))


def low_sum(*parts):
    total = parts[0].astype(F32)
    for part in parts[1:]:
        total = total + part.astype(F32)
    return total.astype(BF)


def scatter_data(parts):
    return lax.psum_scatter(parts, DATA, scatter_dimension=0, tiled=False)


def scatter_order(grads, rows):
    his, los, heads, mids = split_sizes()
    cols = grads.shape[1]
    parts = grads.reshape(heads, his, mids, los, rows, cols).transpose(1, 3, 0, 2, 4, 5)
    return parts.reshape(his * los, heads * mids * rows, cols)


def scatter_ring(summed):
    moving = None
    for step in range(1, lax.axis_size("hi")):
        part = summed[step]
        moving = ring(part if moving is None else low_sum(part, moving), 1)
    return summed[0] if moving is None else low_sum(summed[0], moving)


def row_moves():
    mids, los = lax.axis_size("mid"), lax.axis_size("lo")
    count = lax.axis_size("hi") * mids * los
    share = count // mids
    moves = []
    for source in range(count):
        owner, rest = source // share, source % share
        moves.append((source, ((rest // los) * mids + owner) * los + rest % los))
    return moves


def rows_out(part):
    return lax.ppermute(part, SEQ, row_moves())


def rows_back(part):
    return lax.ppermute(part, SEQ, [(there, here) for here, there in row_moves()])


def lane_index(shape):
    return lax.broadcasted_iota(jnp.int32, shape, len(shape) - 1)


def half_sums(values, lane, head_size):
    first = jnp.sum(jnp.where(lane < head_size, values, 0.0), axis=-1, keepdims=True)
    second = jnp.sum(jnp.where(lane < head_size, 0.0, values), axis=-1, keepdims=True)
    return jnp.where(lane < head_size, first, second)


def partner(values, lane, head_size):
    quarter = head_size // 2
    return jnp.where(
        lane % head_size < quarter,
        pltpu.roll(values, LANES - quarter, 1),
        pltpu.roll(values, quarter, 1),
    )


def project_kernel(
    head_size, normed_ref, w_ref, cos_ref, sin_ref, qgain_ref, kgain_ref, raw_ref, q_ref, kv_ref
):
    raw = dot_plain(normed_ref[...], w_ref[...])
    raw_ref[...] = raw
    cos, sin = cos_ref[...], sin_ref[...]
    lane = lane_index(cos.shape)
    q_width = q_ref.shape[1]
    for at in range(0, raw.shape[1], LANES):
        part = raw[:, at : at + LANES]
        is_query = at < q_width
        inverse = lax.rsqrt(half_sums(part * part, lane, head_size) / head_size + EPS)
        scaled = part * inverse * (qgain_ref[...] if is_query else kgain_ref[...])
        turned = scaled * cos + partner(scaled, lane, head_size) * sin
        if is_query:
            q_ref[:, at : at + LANES] = turned.astype(BF)
        else:
            out_at = at - q_width
            kv_ref[:, out_at : out_at + LANES] = jnp.where(lane < head_size, turned, part).astype(BF)


def project(normed, w_qkv, cos, sin, query_gain, key_gain, q_width, head_size):
    rows, width = normed.shape
    cols = w_qkv.shape[1]
    tile = 256
    whole = lambda i: (0, 0)
    step = lambda i: (i, 0)
    return pl.pallas_call(
        functools.partial(project_kernel, head_size),
        grid=(rows // tile,),
        in_specs=[
            pl.BlockSpec((tile, width), step),
            pl.BlockSpec((width, cols), whole),
            pl.BlockSpec((tile, LANES), step),
            pl.BlockSpec((tile, LANES), step),
            pl.BlockSpec((1, LANES), whole),
            pl.BlockSpec((1, LANES), whole),
        ],
        out_specs=[
            pl.BlockSpec((tile, cols), step),
            pl.BlockSpec((tile, q_width), step),
            pl.BlockSpec((tile, cols - q_width), step),
        ],
        out_shape=[
            jax.ShapeDtypeStruct((rows, cols), F32),
            jax.ShapeDtypeStruct((rows, q_width), BF),
            jax.ShapeDtypeStruct((rows, cols - q_width), BF),
        ],
        compiler_params=pltpu.CompilerParams(vmem_limit_bytes=VMEM_LIMIT),
        cost_estimate=CHEAP,
    )(normed, w_qkv, cos, sin, query_gain, key_gain)


def unproject_kernel(
    head_size, raw_ref, dq_ref, dkv_ref, cos_ref, sin_ref, qgain_ref, kgain_ref, out_ref, gain_ref
):
    cos, sin = cos_ref[...], sin_ref[...]
    lane = lane_index(cos.shape)
    q_width = dq_ref.shape[1]
    totals = [jnp.zeros((1, LANES), F32), jnp.zeros((1, LANES), F32)]
    for at in range(0, raw_ref.shape[1], LANES):
        part = raw_ref[:, at : at + LANES]
        is_query = at < q_width
        if is_query:
            upstream = dq_ref[:, at : at + LANES]
            gain = qgain_ref[...]
        else:
            upstream = dkv_ref[:, at - q_width : at - q_width + LANES].astype(F32)
            gain = kgain_ref[...]
        turned = upstream * cos - partner(upstream, lane, head_size) * sin
        inverse = lax.rsqrt(half_sums(part * part, lane, head_size) / head_size + EPS)
        scaled = turned * gain
        inner = half_sums(scaled * part, lane, head_size) / head_size
        grad = inverse * scaled - part * inverse * inverse * inverse * inner
        gain_part = jnp.sum(turned * part * inverse, axis=0, keepdims=True)
        if not is_query:
            grad = jnp.where(lane < head_size, grad, upstream)
            gain_part = jnp.where(lane[:1] < head_size, gain_part, 0.0)
        totals[0 if is_query else 1] += gain_part
        out_ref[:, at : at + LANES] = grad.astype(BF)
    gain_ref[0] = jnp.concatenate(totals, axis=0)


def unproject(raw, dq, dkv, cos, sin, query_gain, key_gain, head_size):
    rows, cols = raw.shape
    q_width = dq.shape[1]
    tile = 256
    whole = lambda i: (0, 0)
    step = lambda i: (i, 0)
    return pl.pallas_call(
        functools.partial(unproject_kernel, head_size),
        grid=(rows // tile,),
        in_specs=[
            pl.BlockSpec((tile, cols), step),
            pl.BlockSpec((tile, q_width), step),
            pl.BlockSpec((tile, cols - q_width), step),
            pl.BlockSpec((tile, LANES), step),
            pl.BlockSpec((tile, LANES), step),
            pl.BlockSpec((1, LANES), whole),
            pl.BlockSpec((1, LANES), whole),
        ],
        out_specs=[
            pl.BlockSpec((tile, cols), step),
            pl.BlockSpec((1, 2, LANES), lambda i: (i, 0, 0)),
        ],
        out_shape=[
            jax.ShapeDtypeStruct((rows, cols), BF),
            jax.ShapeDtypeStruct((rows // tile, 2, LANES), F32),
        ],
        compiler_params=pltpu.CompilerParams(vmem_limit_bytes=VMEM_LIMIT),
        cost_estimate=CHEAP,
    )(raw, dq, dkv, cos, sin, query_gain, key_gain)


def head_parts(pair, lane, head_size):
    return (
        jnp.where(lane < head_size, pair, 0.0).astype(BF),
        jnp.where(lane < head_size, pltpu.roll(pair, head_size, 1), 0.0).astype(BF),
    )


def attend_kernel(head_size, lows, first, last, code_ref, base_ref, q_ref, row_ref, key_ref, *refs):
    kv_refs, refs = refs[:lows], refs[lows:]
    if not first:
        (acc_in, sum_in), refs = refs[:2], refs[2:]
    if last:
        exact_ref, low_ref, lse_ref, qs_ref, acc_ref, sum_ref = refs
    else:
        acc_out, sum_out, qs_ref, acc_ref, sum_ref = refs
    batch = pl.program_id(0)
    count = row_ref.shape[1]
    factor = LOG2E * head_size**-0.5
    lane = lane_index((count, LANES))
    some = functools.reduce(jnp.maximum, [code_ref[batch, low] for low in range(lows)]) > 0

    @pl.when(some)
    def _():
        both = q_ref[:, 0].reshape(count, LANES).astype(F32)
        qs_ref[0], qs_ref[1] = head_parts(both, lane, head_size)

    if first:
        acc_ref[...] = jnp.zeros_like(acc_ref)
        sum_ref[...] = jnp.zeros_like(sum_ref)
    else:
        acc_ref[...] = acc_in[0, 0]
        sum_ref[...] = sum_in[0, 0]

    def one(low, masked):
        keys = kv_refs[low][:, 0].reshape(count, LANES)
        if masked:
            key_pos = key_ref[...] + base_ref[low]
            allowed = (key_pos <= row_ref[0, :, 0:1]) & (key_pos >= row_ref[0, :, 1:2])
        for head in range(2):
            exps = jnp.exp2(dot_back(qs_ref[head], keys) * factor)
            if masked:
                exps = jnp.where(allowed, exps, 0.0)
            partial = exps[:, :LANES]
            for lane_at in range(LANES, count, LANES):
                partial = partial + exps[:, lane_at : lane_at + LANES]
            sum_ref[head] += partial
            acc_ref[head] += dot_plain(exps.astype(BF), keys)

    for low in range(lows):
        code = code_ref[batch, low]
        pl.when(code == 1)(functools.partial(one, low, False))
        pl.when(code == 2)(functools.partial(one, low, True))

    if not last:
        acc_out[0, 0] = acc_ref[...]
        sum_out[0, 0] = sum_ref[...]
        return
    results = []
    for head in range(2):
        total = jnp.sum(sum_ref[head], axis=-1, keepdims=True)
        results.append(acc_ref[head] / total)
        wide = jnp.broadcast_to(jnp.log2(total), (count, LANES))
        lse_ref[0, 0, head] = wide.T[:8]
    joined = jnp.where(lane < head_size, pltpu.roll(results[0], head_size, 1), results[1])
    joined = joined.reshape(exact_ref.shape[0], -1, LANES)
    exact_ref[:, 0] = joined
    low_ref[:, 0] = joined.astype(BF)


def attend(codes, bases, query, kvs, row_info, key_pos, state, last, head_size):
    slots, batches, rows, q_width = query.shape
    count = slots * rows
    pairs = q_width // LANES
    pick = lambda b, p, *_: (0, b, 0, p)
    by_pair = lambda b, p, *_: (b, p, 0, 0, 0)
    slab = pl.BlockSpec((slots, 1, rows, LANES), pick)
    wide = pl.BlockSpec((1, 1, 2, count, LANES), by_pair)
    wide_shape = jax.ShapeDtypeStruct((batches, pairs, 2, count, LANES), F32)
    if last:
        out_specs = [slab, slab, pl.BlockSpec((1, 1, 2, 8, count), by_pair)]
        out_shape = [
            jax.ShapeDtypeStruct(query.shape, F32),
            jax.ShapeDtypeStruct(query.shape, BF),
            jax.ShapeDtypeStruct((batches, pairs, 2, 8, count), F32),
        ]
    else:
        out_specs, out_shape = [wide, wide], [wide_shape, wide_shape]
    return pl.pallas_call(
        functools.partial(attend_kernel, head_size, len(kvs), not state, last),
        grid_spec=pltpu.PrefetchScalarGridSpec(
            num_scalar_prefetch=2,
            grid=(batches, pairs),
            in_specs=[
                slab,
                pl.BlockSpec((1, count, 2), lambda b, p, *_: (b, 0, 0)),
                pl.BlockSpec((1, count), lambda b, p, *_: (0, 0)),
            ]
            + [slab] * len(kvs)
            + [wide] * len(state),
            out_specs=out_specs,
            scratch_shapes=[
                pltpu.VMEM((2, count, LANES), BF),
                pltpu.VMEM((2, count, LANES), F32),
                pltpu.VMEM((2, count, LANES), F32),
            ],
        ),
        out_shape=out_shape,
        compiler_params=pltpu.CompilerParams(vmem_limit_bytes=VMEM_LIMIT),
        cost_estimate=STEP,
    )(codes, bases, query, row_info, key_pos, *kvs, *state)


def attend_back_kernel(
    head_size,
    lows,
    first,
    last,
    code_ref,
    base_ref,
    q_ref,
    up_ref,
    exact_ref,
    lse_ref,
    row_ref,
    key_ref,
    *refs,
):
    kv_refs, refs = refs[:lows], refs[lows:]
    if not first:
        acc_in, refs = refs[0], refs[1:]
    dkv_refs, refs = refs[:lows], refs[lows:]
    out_ref, qs_ref, us_ref, acc_ref, delta_ref = refs
    batch = pl.program_id(0)
    count = row_ref.shape[2]
    scale = head_size**-0.5
    factor = LOG2E * scale
    lane = lane_index((count, LANES))
    some = functools.reduce(jnp.maximum, [code_ref[batch, low] for low in range(lows)]) > 0

    @pl.when(some)
    def _():
        both = q_ref[:, 0].reshape(count, LANES).astype(F32)
        qs_ref[0], qs_ref[1] = head_parts(both, lane, head_size)
        upper = up_ref[:, 0].reshape(count, LANES).astype(F32)
        us_ref[0] = jnp.where(lane < head_size, 0.0, pltpu.roll(upper, head_size, 1)).astype(BF)
        us_ref[1] = jnp.where(lane < head_size, 0.0, upper).astype(BF)
        products = upper * exact_ref[:, 0].reshape(count, LANES)
        for head in range(2):
            inside = (lane < head_size) if head == 0 else (lane >= head_size)
            total = jnp.sum(jnp.where(inside, products, 0.0), axis=-1, keepdims=True)
            delta_ref[head] = jnp.broadcast_to(total, (count, LANES)).T[:8]

    acc_ref[...] = jnp.zeros_like(acc_ref) if first else acc_in[0, 0]

    def none(low):
        dkv_refs[low][:, 0] = jnp.zeros((kv_refs[low].shape[0],) + kv_refs[low].shape[2:], BF)

    def one(low, masked):
        keys = kv_refs[low][:, 0].reshape(count, LANES)
        if masked:
            key_pos = key_ref[...] + base_ref[low]
            allowed = (key_pos <= row_ref[0, 0:1]) & (key_pos >= row_ref[0, 1:2])
        grad_kv = jnp.zeros((count, LANES), F32)
        for head in range(2):
            scores = dot_back(keys, qs_ref[head]) * factor
            probs = jnp.exp2(scores - lse_ref[0, 0, head, 0:1])
            if masked:
                probs = jnp.where(allowed, probs, 0.0)
            grads = dot_back(keys, us_ref[head])
            grads = (probs * (grads - delta_ref[head, 0:1])).astype(BF)
            grad_kv += dot_plain(probs.astype(BF), us_ref[head])
            grad_kv += dot_plain(grads, qs_ref[head]) * scale
            acc_ref[head] += dot_outer(grads, keys)
        dkv_refs[low][:, 0] = grad_kv.astype(BF).reshape(kv_refs[low].shape[0], -1, LANES)

    for low in range(lows):
        code = code_ref[batch, low]
        pl.when(code == 0)(functools.partial(none, low))
        pl.when(code == 1)(functools.partial(one, low, False))
        pl.when(code == 2)(functools.partial(one, low, True))

    if not last:
        out_ref[0, 0] = acc_ref[...]
        return
    joined = jnp.where(lane < head_size, acc_ref[0], pltpu.roll(acc_ref[1], head_size, 1))
    out_ref[:, 0] = (joined * scale).reshape(out_ref.shape[0], -1, LANES)


def attend_back(codes, bases, query, upstream, exact, lse, kvs, row_info, key_pos, state, last, head_size):
    slots, batches, rows, q_width = query.shape
    count = slots * rows
    pairs = q_width // LANES
    pick = lambda b, p, *_: (0, b, 0, p)
    by_pair = lambda b, p, *_: (b, p, 0, 0, 0)
    slab = pl.BlockSpec((slots, 1, rows, LANES), pick)
    wide = pl.BlockSpec((1, 1, 2, count, LANES), by_pair)
    wide_shape = jax.ShapeDtypeStruct((batches, pairs, 2, count, LANES), F32)
    return pl.pallas_call(
        functools.partial(attend_back_kernel, head_size, len(kvs), not state, last),
        grid_spec=pltpu.PrefetchScalarGridSpec(
            num_scalar_prefetch=2,
            grid=(batches, pairs),
            in_specs=[
                slab,
                slab,
                slab,
                pl.BlockSpec((1, 1, 2, 8, count), by_pair),
                pl.BlockSpec((1, 2, count), lambda b, p, *_: (b, 0, 0)),
                pl.BlockSpec((count, 1), lambda b, p, *_: (0, 0)),
            ]
            + [slab] * len(kvs)
            + [wide] * len(state),
            out_specs=[slab] * len(kvs) + [slab if last else wide],
            scratch_shapes=[
                pltpu.VMEM((2, count, LANES), BF),
                pltpu.VMEM((2, count, LANES), BF),
                pltpu.VMEM((2, count, LANES), F32),
                pltpu.VMEM((2, 8, count), F32),
            ],
        ),
        out_shape=[jax.ShapeDtypeStruct(kvs[0].shape, BF)] * len(kvs)
        + [jax.ShapeDtypeStruct(query.shape, F32) if last else wide_shape],
        compiler_params=pltpu.CompilerParams(vmem_limit_bytes=VMEM_LIMIT),
        cost_estimate=STEP,
    )(codes, bases, query, upstream, exact, lse, row_info, key_pos, *kvs, *state)


TILE = 384


def block_order():
    his, los, heads, mids = split_sizes()
    return tuple(
        (hi * los + lo, head * mids + mid)
        for head in range(heads)
        for hi in range(his)
        for mid in range(mids)
        for lo in range(los)
    )


def split_kernel(rank_ref, *refs):
    for slot in range(4):
        gate_ref, up_ref, out_ref = refs[slot], refs[4 + slot], refs[8 + slot]
        for at in range(0, gate_ref.shape[1], TILE):
            out_ref[:, 2 * at : 2 * at + TILE] = gate_ref[:, at : at + TILE]
            out_ref[:, 2 * at + TILE : 2 * at + 2 * TILE] = up_ref[:, at : at + TILE]


def rank_scalar():
    return group_rank()[None].astype(jnp.int32)


def gate_up_blocks(w_gate, w_up):
    rows, cols = w_gate.shape
    part = cols // 4
    picks = [
        pl.BlockSpec((rows, part), lambda i, rank, slot=slot: (0, rank[0] ^ slot)) for slot in range(4)
    ]
    return pl.pallas_call(
        split_kernel,
        grid_spec=pltpu.PrefetchScalarGridSpec(
            num_scalar_prefetch=1,
            grid=(1,),
            in_specs=picks + picks,
            out_specs=[pl.BlockSpec((rows, 2 * part), lambda i, rank: (0, 0))] * 4,
        ),
        out_shape=[jax.ShapeDtypeStruct((rows, 2 * part), w_gate.dtype)] * 4,
        compiler_params=pltpu.CompilerParams(vmem_limit_bytes=VMEM_LIMIT),
        cost_estimate=CHEAP,
    )(rank_scalar(), *[w_gate] * 4, *[w_up] * 4)


def merge_kernel(rank_ref, *refs):
    source = pl.program_id(0) ^ rank_ref[0]
    gate_ref, up_ref = refs[4:]
    for slot in range(4):

        @pl.when(source == slot)
        def _(ref=refs[slot]):
            for at in range(0, gate_ref.shape[1], TILE):
                gate_ref[:, at : at + TILE] = ref[:, 2 * at : 2 * at + TILE].astype(F32)
                up_ref[:, at : at + TILE] = ref[:, 2 * at + TILE : 2 * at + 2 * TILE].astype(F32)


def gate_up_merge(blocks):
    rows, both = blocks[0].shape
    column = pl.BlockSpec((rows, both // 2), lambda i, rank: (0, i))
    return pl.pallas_call(
        merge_kernel,
        grid_spec=pltpu.PrefetchScalarGridSpec(
            num_scalar_prefetch=1,
            grid=(4,),
            in_specs=[pl.BlockSpec((rows, both), lambda i, rank: (0, 0))] * 4,
            out_specs=[column, column],
        ),
        out_shape=[jax.ShapeDtypeStruct((rows, 2 * both), F32)] * 2,
        compiler_params=pltpu.CompilerParams(vmem_limit_bytes=VMEM_LIMIT),
        cost_estimate=CHEAP,
    )(rank_scalar(), *blocks)


def exchange_blocks(blocks):
    far = [(0, 3), (1, 2), (2, 1), (3, 0)]
    return [
        blocks[0],
        swap(blocks[1], "mid"),
        swap(blocks[2], "heads"),
        lax.ppermute(blocks[3], GROUP, far),
    ]


def feed_kernel(order, rank_ref, x_ref, cot_ref, w_ref, wd_ref, hid_ref, grad_ref, two_ref, w_all, acc_ref):
    rows = w_ref.shape[2]
    for index, (data, source) in enumerate(order):
        w_all[pl.ds(index * rows, rows)] = w_ref[data, source ^ rank_ref[0]]
    step = pl.program_id(0)
    count = x_ref.shape[0]
    part = math.gcd(count, 256)

    @pl.when(step == 0)
    def _():
        acc_ref[...] = jnp.zeros_like(acc_ref)

    for first in range(0, count, part):
        at = pl.ds(first, part)
        both = dot_plain(x_ref[at], w_all[...])
        gate, upper = both[:, :TILE], both[:, TILE:]
        grad_hidden = dot_back(cot_ref[at], wd_ref[...])
        sigmoid = jax.nn.sigmoid(gate)
        silu = gate * sigmoid
        hid_ref[at] = (silu * upper).astype(BF)
        grad_gate = (grad_hidden * upper * sigmoid * (1.0 + gate * (1.0 - sigmoid))).astype(BF)
        grad_upper = (grad_hidden * silu).astype(BF)
        grads = jnp.concatenate([grad_gate, grad_upper], axis=1)
        grad_ref[at] = grads
        acc_ref[at] += dot_back(grads, w_all[...])

    @pl.when(step == pl.num_programs(0) - 1)
    def _():
        two_ref[...] = acc_ref[...].astype(BF)


def feed(x, cot, w_both, wd):
    count, width = x.shape
    cols = wd.shape[0]
    whole = lambda i, rank: (0, 0)
    column = lambda i, rank: (0, i)
    return pl.pallas_call(
        functools.partial(feed_kernel, block_order()),
        grid_spec=pltpu.PrefetchScalarGridSpec(
            num_scalar_prefetch=1,
            grid=(cols // TILE,),
            in_specs=[
                pl.BlockSpec((count, width), whole),
                pl.BlockSpec((count, width), whole),
                pl.BlockSpec(w_both.shape[:3] + (2 * TILE,), lambda i, rank: (0, 0, 0, i)),
                pl.BlockSpec((TILE, width), lambda i, rank: (i, 0)),
            ],
            out_specs=[
                pl.BlockSpec((count, TILE), column),
                pl.BlockSpec((count, 2 * TILE), column),
                pl.BlockSpec((count, width), whole),
            ],
            scratch_shapes=[pltpu.VMEM((width, 2 * TILE), BF), pltpu.VMEM((count, width), F32)],
        ),
        out_shape=[
            jax.ShapeDtypeStruct((count, cols), BF),
            jax.ShapeDtypeStruct((count, 2 * cols), BF),
            jax.ShapeDtypeStruct((count, width), BF),
        ],
        compiler_params=pltpu.CompilerParams(vmem_limit_bytes=VMEM_LIMIT),
        cost_estimate=CHEAP,
    )(rank_scalar(), x, cot, w_both, wd)


def gate_grad_kernel(order, rank_ref, x_ref, grad_ref, out_ref, xt_ref):
    rows = out_ref.shape[2]

    @pl.when(pl.program_id(0) == 0)
    def _():
        xt_ref[...] = x_ref[...].T

    result = dot_plain(xt_ref[...], grad_ref[...]).astype(BF)
    for index, (data, source) in enumerate(order):
        out_ref[data, source ^ rank_ref[0]] = result[index * rows : (index + 1) * rows]


def gate_grads(x, grads, shape):
    count, width = x.shape
    return pl.pallas_call(
        functools.partial(gate_grad_kernel, block_order()),
        grid_spec=pltpu.PrefetchScalarGridSpec(
            num_scalar_prefetch=1,
            grid=(grads.shape[1] // (2 * TILE),),
            in_specs=[
                pl.BlockSpec((count, width), lambda i, rank: (0, 0)),
                pl.BlockSpec((count, 2 * TILE), lambda i, rank: (0, i)),
            ],
            out_specs=pl.BlockSpec(shape[:3] + (2 * TILE,), lambda i, rank: (0, 0, 0, i)),
            scratch_shapes=[pltpu.VMEM((width, count), BF)],
        ),
        out_shape=jax.ShapeDtypeStruct(shape, BF),
        compiler_params=pltpu.CompilerParams(vmem_limit_bytes=VMEM_LIMIT),
        cost_estimate=CHEAP,
    )(rank_scalar(), x, grads)


def down_kernel(hid_ref, cot_ref, wd_ref, grad_ref, out_ref, acc_ref):
    step = pl.program_id(0)
    hidden = hid_ref[...]
    grad_ref[...] = dot_outer(hidden, cot_ref[...]).astype(BF)
    part = dot_plain(hidden, wd_ref[...])

    @pl.when(step == 0)
    def _():
        acc_ref[...] = part

    @pl.when(step > 0)
    def _():
        acc_ref[...] += part

    @pl.when(step == pl.num_programs(0) - 1)
    def _():
        out_ref[...] = acc_ref[...].astype(BF)


def down_grads(hidden, cot, wd):
    count, cols = hidden.shape
    width = wd.shape[1]
    tile = TILE
    whole = lambda i: (0, 0)
    return pl.pallas_call(
        down_kernel,
        grid=(cols // tile,),
        in_specs=[
            pl.BlockSpec((count, tile), lambda i: (0, i)),
            pl.BlockSpec((count, width), whole),
            pl.BlockSpec((tile, width), lambda i: (i, 0)),
        ],
        out_specs=[
            pl.BlockSpec((tile, width), lambda i: (i, 0)),
            pl.BlockSpec((count, width), whole),
        ],
        out_shape=[
            jax.ShapeDtypeStruct((cols, width), BF),
            jax.ShapeDtypeStruct((count, width), BF),
        ],
        scratch_shapes=[pltpu.VMEM((count, width), F32)],
        compiler_params=pltpu.CompilerParams(vmem_limit_bytes=VMEM_LIMIT),
        cost_estimate=CHEAP,
    )(hidden, cot, wd)


def per_device(
    inputs,
    cotangent,
    attn_gain,
    w_query,
    w_key,
    w_value,
    w_output,
    query_gain,
    key_gain,
    ffn_gain,
    w_gate,
    w_up,
    w_down,
    doc_starts,
):
    heads, mids = lax.axis_size("heads"), lax.axis_size("mid")
    his, los = lax.axis_size("hi"), lax.axis_size("lo")
    slots = heads * mids
    batches, _, rows, width = inputs.shape
    block = rows * heads
    count = slots * rows
    head_size = query_gain.shape[0]
    w_rows = w_query.shape[0]
    q_width = w_query.shape[1] // slots
    pairs = w_key.shape[1] // head_size // slots
    ff_width = w_gate.shape[1] // slots

    by_slot = lambda w: w.reshape(w_rows, slots, -1)
    kv_cols = jnp.stack(
        [
            w_key.reshape(w_rows, slots, pairs, head_size),
            w_value.reshape(w_rows, slots, pairs, head_size),
        ],
        axis=3,
    )
    qkv_parts = jnp.concatenate([by_slot(w_query), kv_cols.reshape(w_rows, slots, -1)], axis=2)
    qkv_mine = columns_out(qkv_parts.transpose(1, 0, 2))
    out_rows, down_rows = w_output.shape[0], w_down.shape[0]
    own_in, own_cot = inputs[:, 0], cotangent[:, 0]
    row_part = jnp.concatenate([w_output, w_down], axis=0)
    if is_quad():
        qkv_mine, own_in, row_part, doc_starts = together(qkv_mine, own_in, row_part, doc_starts)
        in_near = group_near(own_in)
    row_part = rows_out(row_part)
    qkv_all = gather_data(qkv_mine)
    fast = is_quad() and fast_rows(w_rows) and ff_width % TILE == 0

    head_at, mid_at = slot_places()
    row_at = jnp.arange(rows, dtype=jnp.int32)
    hi_at, lo_at = lax.axis_index("hi"), lax.axis_index("lo")
    first_pos = ((mid_at * los * block + head_at * rows)[:, None] + row_at[None, :]).reshape(count)
    row_pos = first_pos + hi_at * (mids * los * block) + lo_at * block
    lows = [lo_at] if los == 1 else [lo_at, 1 - lo_at]
    starts = doc_starts[:, None, :]
    row_begin = jnp.max(jnp.where(starts <= row_pos[None, :, None], starts, 0), axis=2)
    row_both = jnp.broadcast_to(row_pos[None], (batches, count))
    begin_low, begin_high = (
        jnp.min(row_begin, axis=1)[:, None],
        jnp.max(row_begin, axis=1)[:, None],
    )

    back = hi_at - jnp.arange(his, dtype=jnp.int32)[:, None]
    bases = back * (mids * los * block) + jnp.stack(lows)[None] * block
    key_low, key_high = (bases + jnp.min(first_pos))[:, None], (bases + jnp.max(first_pos))[:, None]
    none = (key_low > jnp.max(row_pos)) | (key_high < begin_low) | (back < 0)[:, None]
    full = (key_high <= jnp.min(row_pos)) & (key_low >= begin_high)
    codes = jnp.where(none, 0, jnp.where(full, 1, 2)).astype(jnp.int32)
    bases = bases.astype(jnp.int32)
    info_cols = jnp.stack([row_both, row_begin], axis=2)
    info_rows = jnp.stack([row_both, row_begin], axis=1)

    half = head_size // 2
    frequency = THETA ** (-(jnp.arange(half, dtype=F32) * 2.0 / head_size))
    turn_pos = (row_both - row_begin).reshape(batches, slots, rows).transpose(1, 0, 2)
    angles = turn_pos.reshape(-1).astype(F32)[:, None] * frequency[None, :]
    cos, sin = jnp.cos(angles), jnp.sin(angles)
    cos = jnp.concatenate([cos] * 4, axis=1)
    sin = jnp.concatenate([-sin, sin, -sin, sin], axis=1)
    q_gain = jnp.concatenate([query_gain, query_gain])[None]
    k_gain = jnp.concatenate([key_gain, key_gain])[None]

    if is_quad():
        *in_near, cos, sin, info_cols, info_rows, codes, bases = together(
            *in_near, cos, sin, info_cols, info_rows, codes, bases
        )
        in_far = group_far(*in_near)
        *in_far, qkv_all, row_part = together(*in_far, qkv_all, row_part)
        in_all, normed = group_joined(own_in, in_near, in_far, attn_gain)
    else:
        in_all = group_gather(own_in)
        in_wide = in_all.astype(F32)
        normed = (in_wide * rms_inverse(in_wide) * attn_gain).astype(BF)
    row_all = gather_data(row_part)
    w_qkv = natural_rows(qkv_all)
    normed = normed.reshape(-1, width)
    raw, query, kv = project(normed, w_qkv, cos, sin, q_gain, k_gain, q_width, head_size)
    query, w_gate, w_up = together(query, w_gate, w_up)
    if fast:
        gate_up_mine = jnp.stack(exchange_blocks(gate_up_blocks(w_gate, w_up)))
    else:
        gate_up_parts = jnp.concatenate([by_slot(w_gate), by_slot(w_up)], axis=2)
        gate_up_mine = columns_out(gate_up_parts.transpose(1, 0, 2))
    query = query.reshape(slots, batches, rows, q_width)
    moving = kv.reshape(slots, batches, rows, -1)
    kv_steps, state = [], ()
    for step in range(his):
        if step:
            moving = lax.ppermute(moving, "hi", [(i, i + 1) for i in range(step - 1, his - 1)])
            moving, *state = together(moving, *state)
        if step == his - 1:
            moving, gate_up_mine = together(moving, gate_up_mine)
            gate_up_all = gather_data(gate_up_mine)
        kv_steps.append([moving] if los == 1 else [moving, other_low(moving)])
        state = attend(
            codes[step],
            bases[step],
            query,
            kv_steps[step],
            info_cols,
            first_pos[None],
            tuple(state),
            step == his - 1,
            head_size,
        )
        state = list(state)
        if not is_quad():
            continue
        if step == 0:
            gate_up_mine, state[0], cot_own = together(gate_up_mine, state[0], own_cot)
            cot_near = group_near(cot_own)
        if step == 1:
            *cot_near, row_all, state[0] = together(*cot_near, row_all, state[0])
            cot_far = group_far(*cot_near)
            wo_part = row_all[:, :out_rows].reshape(-1, width)
            wd_use = row_all[:, out_rows:].reshape(-1, width)
            wo_near = group_near(wo_part)
        if step == 2:
            *cot_far, state[0] = together(*cot_far, state[0])
            *wo_near, wd_use, state[0] = together(*wo_near, wd_use, state[0])
            wo_far = group_far(*wo_near)
            cot_all = group_joined(cot_own, cot_near, cot_far)
        if step == 3:
            *wo_far, cot_all, state[1] = together(*wo_far, cot_all, state[1])
            wo_full = group_joined(wo_part, wo_near, wo_far)
    exact, attn, lse = state
    if not is_quad():
        cot_all = group_gather(own_cot)
        wo_full = group_gather(row_all[:, :out_rows].reshape(-1, width))
        wd_use = row_all[:, out_rows:].reshape(-1, width)
    wo_full = wo_full.reshape(-1, width)
    attn_wide = columns_out_async(attn.reshape(slots, batches * rows, q_width))
    attn_wide = jnp.concatenate([attn_wide[slot] for slot in range(slots)], axis=1)
    middle = own_in.reshape(-1, width).astype(F32) + dot_plain(attn_wide, wo_full)

    normed_two = (middle * rms_inverse(middle) * ffn_gain).astype(BF)
    normed_two_all = group_gather(normed_two).reshape(-1, width)
    normed_two_all, gate_up_all = together(normed_two_all, gate_up_all)
    cot_rows = cot_all.reshape(-1, width)
    if fast:
        hidden, grads, grad_two = feed(normed_two_all, cot_rows, gate_up_all, wd_use)
        grad_two, grads, hidden = together(grad_two, grads, hidden)
        grad_gate_up = gate_grads(normed_two_all, grads, gate_up_all.shape)
        grad_gate_up = grad_gate_up.reshape(his * los, slots * w_rows, -1)
        grad_down, out_part = down_grads(hidden, cot_rows, wd_use)
    else:
        w_both = natural_rows(gate_up_all)
        both = dot_plain(normed_two_all, w_both)
        gate, upper = both[:, :ff_width], both[:, ff_width:]
        grad_hidden = dot_back(cot_rows, wd_use)
        sigmoid = jax.nn.sigmoid(gate)
        silu = gate * sigmoid
        hidden = (silu * upper).astype(BF)
        grad_gate = grad_hidden * upper * sigmoid * (1.0 + gate * (1.0 - sigmoid))
        grads = jnp.concatenate([grad_gate, grad_hidden * silu], axis=1).astype(BF)
        grad_two = dot_back(grads, w_both).astype(BF)
        grad_gate_up = scatter_order(dot_outer(normed_two_all, grads).astype(BF), w_rows)
        grad_down = dot_outer(hidden, cot_rows).astype(BF)
        out_part = dot_plain(hidden, wd_use).astype(BF)
    in_slots = lambda total: total.reshape(slots, batches * rows, width)
    out_part = in_slots(out_part)
    two_sum = GroupSum(in_slots(grad_two))
    (grad_gate_up,) = two_sum.second(grad_gate_up)
    grad_down, out_part = two_sum.hold(grad_down, out_part)
    grad_two = two_sum.done()
    gate_up_sum = scatter_data(grad_gate_up).reshape(slots, w_rows, -1)
    grad_mid_part, _ = norm_back(middle, ffn_gain, grad_two)
    grad_middle = own_cot.reshape(-1, width).astype(F32) + grad_mid_part

    grad_middle_low = grad_middle.astype(BF)
    grad_attn = dot_back(grad_middle_low, wo_full).astype(BF)
    grad_attn = jnp.stack(
        [grad_attn[:, slot * q_width : (slot + 1) * q_width] for slot in range(slots)]
    )
    grad_attn, grad_middle_low = together(grad_attn, grad_middle_low)
    grad_output = dot_outer(attn_wide, grad_middle_low)
    grad_output = grad_output.astype(BF).reshape(slots, -1, width)
    grad_attn = columns_out_async(grad_attn).reshape(query.shape)
    grad_two, middle, grad_attn = together(grad_two, middle, grad_attn)
    ffn_gain_part = jnp.sum(grad_two * middle * rms_inverse(middle), axis=0)
    first_sum = GroupSum(grad_output)
    state, moving = (), None
    for turn in range(1, his + 1):
        step = his - turn
        *dkv, state_out = attend_back(
            codes[step],
            bases[step],
            query,
            grad_attn,
            exact,
            lse,
            kv_steps[step],
            info_rows,
            first_pos[:, None],
            state,
            turn == his,
            head_size,
        )
        if turn > 1:
            *dkv, moving = together(*dkv, moving)
        if turn == 1:
            dkv = first_sum.second(*dkv)
        if turn == min(2, his):
            dkv = first_sum.hold(*dkv)
            output_part = first_sum.done().astype(BF)
            row_grads = jnp.concatenate(
                [
                    output_part.reshape(his * los, out_rows, width),
                    grad_down.reshape(his * los, down_rows, width),
                ],
                axis=1,
            )
            row_sum = scatter_data(row_grads)
            out_part, *dkv = together(out_part, *dkv)
            second_sum = GroupSum(out_part)
        if turn == min(3, his):
            dkv = second_sum.second(*dkv)
        if turn == min(4, his):
            dkv = second_sum.hold(*dkv)
        if turn == his:
            *dkv, gate_up_sum = together(*dkv, gate_up_sum)
            if fast:
                gate_up_back = exchange_blocks([gate_up_sum[slot] for slot in range(4)])
            else:
                gate_up_back = [columns_out(gate_up_sum)]
        parts = [dkv[0]] + ([other_low(dkv[1])] if los == 2 else [])
        parts += [moving] if turn > 1 else []
        if turn < his:
            low, state_out = together(low_sum(*parts), state_out)
            moving = lax.ppermute(low, "hi", [(i, i - 1) for i in range(his - turn, his)])
        state = (state_out,)
    out_sum = second_sum.done()
    dkv_mine = sum(part.astype(F32) for part in parts)
    dq = state[0]
    grad_raw, head_gains = unproject(
        raw,
        dq.reshape(-1, q_width),
        dkv_mine.reshape(raw.shape[0], -1),
        cos,
        sin,
        q_gain,
        k_gain,
        head_size,
    )
    block_out = (middle + out_sum).astype(BF)
    grad_raw, row_sum, *gate_up_back = together(grad_raw, row_sum, *gate_up_back)
    grad_qkv = dot_outer(normed, grad_raw).astype(BF)
    head_sums = jnp.sum(head_gains, axis=0).reshape(2, 2, head_size).sum(axis=1)
    in_wide = in_all.reshape(-1, width).astype(F32)
    normed_back = lambda grads: dot_back(grads, w_qkv).astype(BF)
    gain_vector = lambda low: jnp.concatenate(
        [
            jnp.sum(low.astype(F32) * in_wide * rms_inverse(in_wide), axis=0),
            ffn_gain_part,
            head_sums[0],
            head_sums[1],
        ]
    )
    into_slots = lambda low: low.reshape(slots, batches * rows, width)
    if fast:
        own_part, other_part = unplaced(grad_qkv, w_rows, True)
        own_part, other_part, grad_raw = together(own_part, other_part, grad_raw)
        other_part = other_low(other_part)
        grad_normed_low = normed_back(grad_raw)
        gains = gain_vector(grad_normed_low)
        other_part, grad_normed_low, gains = together(other_part, grad_normed_low, gains)
        summed = low_sum(own_part, other_part)
        normed_sum = GroupSum(into_slots(grad_normed_low))
        stages = sum_stages()
        moving = None
        for step in range(1, his):
            moving = ring(summed[step] if moving is None else low_sum(summed[step], moving), 1)
            gains = gains + stages.pop(0)(gains)
            moving, gains = together(moving, gains)
            if step == 1:
                moving, gains = normed_sum.second(moving, gains)
        qkv_sum = low_sum(summed[0], moving) if his > 1 else summed[0]
        qkv_cols = columns_out(qkv_sum)
        gains = gains + stages.pop(0)(gains)
        qkv_cols, gains = together(qkv_cols, gains)
        for stage in stages:
            gains = gains + stage(gains)
    else:
        grad_qkv = scatter_order(grad_qkv, w_rows)
        qkv_cols = columns_out(scatter_data(grad_qkv).reshape(slots, w_rows, -1))
        grad_normed_low = normed_back(grad_raw)
        gains = all_sum(gain_vector(grad_normed_low))
        normed_sum = GroupSum(into_slots(grad_normed_low))
        normed_sum.second()
    grad_normed = normed_sum.done()
    row_back = rows_back(row_sum).astype(F32)
    grad_in_part, _ = norm_back(own_in.reshape(-1, width).astype(F32), attn_gain, grad_normed)
    grad_inputs = grad_middle + grad_in_part

    qkv_cols = qkv_cols.transpose(1, 0, 2).astype(F32)
    if fast:
        gate_cols, up_cols = gate_up_merge(gate_up_back)
    else:
        gate_cols, up_cols = jnp.split(gate_up_back[0].transpose(1, 0, 2).astype(F32), 2, axis=2)
    kv_sums = qkv_cols[:, :, q_width:].reshape(w_rows, slots, pairs, 2, head_size)
    return (
        block_out.reshape(batches, 1, rows, width),
        grad_inputs.reshape(batches, 1, rows, width),
        gains[:width],
        qkv_cols[:, :, :q_width].reshape(w_rows, -1),
        kv_sums[:, :, :, 0].reshape(w_rows, -1),
        kv_sums[:, :, :, 1].reshape(w_rows, -1),
        row_back[:out_rows],
        gains[2 * width : 2 * width + head_size],
        gains[2 * width + head_size :],
        gains[width : 2 * width],
        gate_cols.reshape(w_rows, -1),
        up_cols.reshape(w_rows, -1),
        row_back[out_rows:],
    )


def solution(mesh):
    heads, seq = mesh.shape["heads"], mesh.shape["seq"]
    rows_spec = P(None, SEQ, "heads", None)
    weight_spec = P(ALL, None)

    def run(*args):
        kv_heads = args[4].shape[1] // args[7].shape[0]
        low = 2 if seq % 2 == 0 else 1
        mid = 2 if seq % (2 * low) == 0 and kv_heads % (2 * heads) == 0 else 1
        split = Mesh(
            mesh.devices.reshape(heads, seq // (mid * low), mid, low), ("heads",) + SEQ
        )
        return jax.shard_map(
            per_device,
            mesh=split,
            in_specs=(
                (rows_spec, rows_spec, P())
                + (weight_spec,) * 4
                + (P(), P(), P())
                + (weight_spec,) * 3
                + (P(),)
            ),
            out_specs=(
                (rows_spec, rows_spec, P())
                + (weight_spec,) * 4
                + (P(), P(), P())
                + (weight_spec,) * 3
            ),
            check_vma=False,
        )(*args)

    return run
```

```python
import functools
import math

import jax
import jax.numpy as jnp
from jax import lax
from jax.experimental import pallas as pl
from jax.experimental.pallas import tpu as pltpu
from jax.sharding import Mesh, PartitionSpec as P

EPS = 1e-05
THETA = 1000000.0
LANES = 128
LOG2E = math.log2(math.e)
GROUP = ("heads", "mid")
DATA = ("hi", "lo")
SEQ = ("hi", "mid", "lo")
ALL = ("heads",) + SEQ
BF = jnp.bfloat16
F32 = jnp.float32
MIB = 1024 * 1024
VMEM_LIMIT = 48 * MIB
CHEAP = pl.CostEstimate(flops=1, bytes_accessed=1, transcendentals=0)
STEP = pl.CostEstimate(flops=1, bytes_accessed=1, transcendentals=0)


def dot_plain(left_side, right_side):
    return jnp.dot(left_side, right_side, preferred_element_type=F32)


def dot_back(left_side, right_side):
    return lax.dot_general(
        left_side, right_side, (((1,), (1,)), ((), ())), preferred_element_type=F32
    )


def dot_outer(left_side, right_side):
    return lax.dot_general(
        left_side, right_side, (((0,), (0,)), ((), ())), preferred_element_type=F32
    )


def together(*values):
    return lax.optimization_barrier(values)


def rms_inverse(values):
    return lax.rsqrt(jnp.mean(values * values, axis=-1, keepdims=True) + EPS)


def norm_back(values, gain_vec, upstream):
    inverse = rms_inverse(values)
    scaled = upstream * gain_vec
    inner_mean = jnp.mean(scaled * values, axis=-1, keepdims=True)
    grad_values = inverse * scaled - values * inverse * inverse * inverse * inner_mean
    return (grad_values, upstream * values * inverse)


def is_quad():
    return lax.axis_size("heads") == 2 and lax.axis_size("mid") == 2


def swap(part, axis):
    return lax.ppermute(part, axis, [(0, 1), (1, 0)])


def group_rank():
    return lax.axis_index("heads") * lax.axis_size("mid") + lax.axis_index("mid")


def block_at(parts, index):
    return lax.dynamic_index_in_dim(parts, index, axis=0, keepdims=False)


def in_order(blocks):
    rank = group_rank()
    total = jnp.zeros((4,) + blocks[0].shape, blocks[0].dtype)
    for slot, block in enumerate(blocks):
        total = lax.dynamic_update_index_in_dim(total, block, rank ^ slot, axis=0)
    return total


def group_near(part):
    return swap(part, "mid"), swap(part, "heads")


def group_far(by_mid, by_heads):
    half = by_mid.shape[0] // 2
    return swap(by_mid[:half], "heads"), swap(by_heads[half:], "mid")


def join_kernel(rank_ref, gain_ref, own_ref, mid_ref, head_ref, low_ref, high_ref, out_ref, *normed_ref):
    source = pl.program_id(0) ^ rank_ref[0]
    half = low_ref.shape[0]
    for slot, ref in enumerate((own_ref, mid_ref, head_ref)):

        @pl.when(source == slot)
        def _(ref=ref):
            out_ref[0] = ref[...]

    @pl.when(source == 3)
    def _():
        out_ref[0, :half] = low_ref[...]
        out_ref[0, half:] = high_ref[...]

    if normed_ref:
        values = out_ref[0].astype(F32)
        normed_ref[0][0] = (values * rms_inverse(values) * gain_ref[...]).astype(BF)


def group_joined(part, near, far, gain=None):
    width = part.shape[-1]
    flat = [block.reshape(-1, width) for block in (part, *near, *far)]
    whole = lambda i, rank: (0, 0)
    shape = (4,) + flat[0].shape
    outs = 1 if gain is None else 2
    out_spec = pl.BlockSpec((1,) + flat[0].shape, lambda i, rank: (i, 0, 0))
    gain_vec = jnp.zeros((1, width), F32) if gain is None else gain[None]
    result = pl.pallas_call(
        join_kernel,
        grid_spec=pltpu.PrefetchScalarGridSpec(
            num_scalar_prefetch=1,
            grid=(4,),
            in_specs=[pl.BlockSpec((1, width), whole)]
            + [pl.BlockSpec(block.shape, whole) for block in flat],
            out_specs=[out_spec] * outs,
        ),
        out_shape=[jax.ShapeDtypeStruct(shape, part.dtype)] * outs,
        compiler_params=pltpu.CompilerParams(vmem_limit_bytes=10 * MIB),
        cost_estimate=CHEAP,
    )(group_rank()[None].astype(jnp.int32), gain_vec, *flat)
    total = result[0].reshape((4,) + part.shape)
    return total if gain is None else (total, result[1].reshape(total.shape))


def group_gather(part):
    if not is_quad():
        return lax.all_gather(part, GROUP, axis=0, tiled=False)
    near = group_near(part)
    return group_joined(part, near, group_far(*near))


def group_gather_plain(part):
    return lax.all_gather(part, GROUP, axis=0, tiled=False)


def group_sum_plain(parts):
    flat = parts.reshape((-1,) + parts.shape[2:])
    return lax.psum_scatter(flat, GROUP, scatter_dimension=0, tiled=True)


class GroupSum:
    def __init__(self, parts):
        if is_quad():
            rank = group_rank()
            self.parts = [block_at(parts, rank ^ slot) for slot in range(4)]
            half = parts.shape[1] // 2
            far = self.parts[3]
            self.far = (swap(far[:half], "mid"), swap(far[half:], "heads"))
        else:
            self.total = group_sum_plain(parts)

    def second(self, *between):
        if is_quad():
            _, mid, head, _ = self.parts
            half = mid.shape[0] // 2
            far_low, far_high = self.far
            if between:
                far_low, far_high, *between = together(far_low, far_high, *between)
            for_mid = jnp.concatenate([mid[:half], low_sum(mid[half:], far_high)], axis=0)
            for_heads = jnp.concatenate([low_sum(head[:half], far_low), head[half:]], axis=0)
            self.near = (swap(for_mid, "mid"), swap(for_heads, "heads"))
        return between

    def hold(self, *later):
        if is_quad():
            near_mid, near_heads, *later = together(*self.near, *later)
            self.near = (near_mid, near_heads)
        return later

    def done(self):
        if not is_quad():
            return self.total.astype(F32)
        return self.parts[0].astype(F32) + self.near[0].astype(F32) + self.near[1].astype(F32)


def slot_places():
    mids = lax.axis_size("mid")
    slots = jnp.arange(lax.axis_size("heads") * mids, dtype=jnp.int32)
    return (slots // mids, slots % mids)


def sum_stages():
    def along_hi(vector):
        size = lax.axis_size("hi")
        parts = [vector]
        for shift in range(1, size):
            parts.append(lax.ppermute(vector, "hi", [(i, (i + shift) % size) for i in range(size)]))
        return sum(parts[1:], parts[0])

    def along_low(vector):
        return vector + swap(vector, "lo")

    def along_group(vector):
        far = [(0, 3), (1, 2), (2, 1), (3, 0)]
        near = swap(vector, "mid") + swap(vector, "heads")
        return vector + near + lax.ppermute(vector, GROUP, far)

    return [along_hi, along_low, along_group]


def all_sum(vector):
    for axis in ("lo", "mid", "heads", "hi"):
        size = lax.axis_size(axis)
        if size & (size - 1):
            vector = lax.psum(vector, axis)
            continue
        step = 1
        while step < size:
            vector = vector + lax.ppermute(vector, axis, [(i, i ^ step) for i in range(size)])
            step *= 2
    return vector


def columns_out(parts):
    return lax.all_to_all(parts, GROUP, split_axis=0, concat_axis=0, tiled=True)


def columns_out_async(parts):
    if not is_quad():
        return columns_out(parts)
    rank = group_rank()
    far = [(0, 3), (1, 2), (2, 1), (3, 0)]
    return in_order(
        [
            block_at(parts, rank),
            swap(block_at(parts, rank ^ 1), "mid"),
            swap(block_at(parts, rank ^ 2), "heads"),
            lax.ppermute(block_at(parts, rank ^ 3), GROUP, far),
        ]
    )


def ring(part, shift):
    size = lax.axis_size("hi")
    return lax.ppermute(part, "hi", [(i, (i + shift) % size) for i in range(size)])


def other_low(part):
    return swap(part, "lo")


def fast_rows(rows):
    return lax.axis_size("lo") == 2 and rows % 16 == 0


def data_ring(part):
    own = [part]
    for _ in range(lax.axis_size("hi") - 1):
        own.append(ring(own[-1], 1))
    return own, [other_low(piece) for piece in own]


def place_index():
    return jnp.stack(
        [lax.axis_index("hi"), lax.axis_index("lo"), lax.axis_index("heads"), lax.axis_index("mid")]
    ).astype(jnp.int32)


def block_row(at_ref, sizes, step, other, source):
    his, los, heads, mids = sizes
    hi = lax.rem(at_ref[0] - step + his, his)
    low = 1 - at_ref[1] if other else at_ref[1]
    if source is None:
        return hi * los + low
    return ((source // mids * his + hi) * mids + source % mids) * los + low


def split_sizes():
    return tuple(lax.axis_size(name) for name in ("hi", "lo", "heads", "mid"))


def place_kernel(sizes, sources, rows, at_ref, *refs):
    his = sizes[0]
    pieces, out_ref, sems = refs[: 2 * his], refs[2 * his], refs[2 * his + 1]
    copies = []
    for step in range(his):
        for other in range(2):
            for source in sources:
                first = block_row(at_ref, sizes, step, other, source) * rows
                piece = pieces[step + other * his]
                copies.append(
                    pltpu.make_async_copy(
                        piece if source is None else piece.at[source],
                        out_ref.at[pl.ds(pl.multiple_of(first, rows), rows)],
                        sems.at[len(copies)],
                    )
                )
    for copy in copies:
        copy.start()
    for copy in copies:
        copy.wait()


def placed(own, other):
    sizes = split_sizes()
    first = own[0]
    rows, cols = first.shape[-2:]
    sources = range(first.shape[0]) if first.ndim == 3 else (None,)
    total = rows * sizes[0] * sizes[1] * len(sources)
    anywhere = pl.BlockSpec(memory_space=pl.ANY)
    return pl.pallas_call(
        functools.partial(place_kernel, sizes, sources, rows),
        in_specs=[pl.BlockSpec(memory_space=pltpu.SMEM)] + [anywhere] * (2 * sizes[0]),
        out_specs=pl.BlockSpec(memory_space=pltpu.VMEM),
        out_shape=jax.ShapeDtypeStruct((total, cols), first.dtype),
        scratch_shapes=[pltpu.SemaphoreType.DMA((2 * sizes[0] * len(sources),))],
        compiler_params=pltpu.CompilerParams(vmem_limit_bytes=8 * MIB),
        cost_estimate=CHEAP,
    )(place_index(), *own, *other)


def unplace_kernel(sizes, sources, rows, at_ref, full_ref, own_ref, other_ref, sems):
    his = sizes[0]
    copies = []
    for step in range(his):
        for other in range(2):
            for source in sources:
                first = block_row(at_ref, sizes, step, other, source) * rows
                target = (other_ref if other else own_ref).at[step]
                copies.append(
                    pltpu.make_async_copy(
                        full_ref.at[pl.ds(pl.multiple_of(first, rows), rows)],
                        target if source is None else target.at[source],
                        sems.at[len(copies)],
                    )
                )
    for copy in copies:
        copy.start()
    for copy in copies:
        copy.wait()


def unplaced(full, rows, by_source):
    sizes = split_sizes()
    cols = full.shape[1]
    slots = sizes[2] * sizes[3]
    sources = range(slots) if by_source else (None,)
    shape = (sizes[0],) + ((slots,) if by_source else ()) + (rows, cols)
    anywhere = pl.BlockSpec(memory_space=pl.ANY)
    return pl.pallas_call(
        functools.partial(unplace_kernel, sizes, sources, rows),
        in_specs=[pl.BlockSpec(memory_space=pltpu.SMEM), pl.BlockSpec(memory_space=pltpu.VMEM)],
        out_specs=[anywhere, anywhere],
        out_shape=[jax.ShapeDtypeStruct(shape, full.dtype)] * 2,
        scratch_shapes=[pltpu.SemaphoreType.DMA((2 * sizes[0] * len(sources),))],
        compiler_params=pltpu.CompilerParams(vmem_limit_bytes=8 * MIB),
        cost_estimate=CHEAP,
    )(place_index(), full)


def natural_rows(gathered):
    his, los, heads, mids = split_sizes()
    rows, cols = gathered.shape[2:]
    parts = gathered.reshape(his, los, heads, mids, rows, cols)
    return parts.transpose(2, 0, 3, 1, 4, 5).reshape(-1, cols)


def gather_data(part):
    return lax.all_gather(part, DATA, axis=0, tiled=False)


def gather_rows(part):
    if fast_rows(part.shape[-2]):
        return placed(*data_ring(part))
    return natural_rows(gather_data(part))


def low_sum(*parts):
    total = parts[0].astype(F32)
    for part in parts[1:]:
        total = total + part.astype(F32)
    return total.astype(BF)


def scatter_data(parts):
    return lax.psum_scatter(parts, DATA, scatter_dimension=0, tiled=False)


def scatter_order(grads, rows):
    his, los, heads, mids = split_sizes()
    cols = grads.shape[1]
    parts = grads.reshape(heads, his, mids, los, rows, cols).transpose(1, 3, 0, 2, 4, 5)
    return parts.reshape(his * los, heads * mids * rows, cols)


def scatter_ring(summed):
    moving = None
    for step in range(1, lax.axis_size("hi")):
        part = summed[step]
        moving = ring(part if moving is None else low_sum(part, moving), 1)
    return summed[0] if moving is None else low_sum(summed[0], moving)


def row_moves():
    mids, los = lax.axis_size("mid"), lax.axis_size("lo")
    count = lax.axis_size("hi") * mids * los
    share = count // mids
    moves = []
    for source in range(count):
        owner, rest = source // share, source % share
        moves.append((source, ((rest // los) * mids + owner) * los + rest % los))
    return moves


def rows_out(part):
    return lax.ppermute(part, SEQ, row_moves())


def rows_back(part):
    return lax.ppermute(part, SEQ, [(there, here) for here, there in row_moves()])


def lane_index(shape):
    return lax.broadcasted_iota(jnp.int32, shape, len(shape) - 1)


def half_sums(values, lane, head_size):
    first = jnp.sum(jnp.where(lane < head_size, values, 0.0), axis=-1, keepdims=True)
    second = jnp.sum(jnp.where(lane < head_size, 0.0, values), axis=-1, keepdims=True)
    return jnp.where(lane < head_size, first, second)


def partner(values, lane, head_size):
    quarter = head_size // 2
    return jnp.where(
        lane % head_size < quarter,
        pltpu.roll(values, LANES - quarter, 1),
        pltpu.roll(values, quarter, 1),
    )


def project_kernel(
    head_size, normed_ref, w_ref, cos_ref, sin_ref, qgain_ref, kgain_ref, raw_ref, q_ref, kv_ref
):
    raw = dot_plain(normed_ref[...], w_ref[...])
    raw_ref[...] = raw
    cos, sin = cos_ref[...], sin_ref[...]
    lane = lane_index(cos.shape)
    q_width = q_ref.shape[1]
    for at in range(0, raw.shape[1], LANES):
        part = raw[:, at : at + LANES]
        is_query = at < q_width
        inverse = lax.rsqrt(half_sums(part * part, lane, head_size) / head_size + EPS)
        scaled = part * inverse * (qgain_ref[...] if is_query else kgain_ref[...])
        turned = scaled * cos + partner(scaled, lane, head_size) * sin
        if is_query:
            q_ref[:, at : at + LANES] = turned.astype(BF)
        else:
            out_at = at - q_width
            kv_ref[:, out_at : out_at + LANES] = jnp.where(lane < head_size, turned, part).astype(BF)


def project(normed, w_qkv, cos, sin, query_gain, key_gain, q_width, head_size):
    rows, width = normed.shape
    cols = w_qkv.shape[1]
    tile = 256
    whole = lambda i: (0, 0)
    step = lambda i: (i, 0)
    return pl.pallas_call(
        functools.partial(project_kernel, head_size),
        grid=(rows // tile,),
        in_specs=[
            pl.BlockSpec((tile, width), step),
            pl.BlockSpec((width, cols), whole),
            pl.BlockSpec((tile, LANES), step),
            pl.BlockSpec((tile, LANES), step),
            pl.BlockSpec((1, LANES), whole),
            pl.BlockSpec((1, LANES), whole),
        ],
        out_specs=[
            pl.BlockSpec((tile, cols), step),
            pl.BlockSpec((tile, q_width), step),
            pl.BlockSpec((tile, cols - q_width), step),
        ],
        out_shape=[
            jax.ShapeDtypeStruct((rows, cols), F32),
            jax.ShapeDtypeStruct((rows, q_width), BF),
            jax.ShapeDtypeStruct((rows, cols - q_width), BF),
        ],
        compiler_params=pltpu.CompilerParams(vmem_limit_bytes=12 * MIB),
        cost_estimate=CHEAP,
    )(normed, w_qkv, cos, sin, query_gain, key_gain)


def unproject_kernel(
    head_size, raw_ref, dq_ref, dkv_ref, cos_ref, sin_ref, qgain_ref, kgain_ref, out_ref, gain_ref
):
    cos, sin = cos_ref[...], sin_ref[...]
    lane = lane_index(cos.shape)
    q_width = dq_ref.shape[1]
    totals = [jnp.zeros((1, LANES), F32), jnp.zeros((1, LANES), F32)]
    for at in range(0, raw_ref.shape[1], LANES):
        part = raw_ref[:, at : at + LANES]
        is_query = at < q_width
        if is_query:
            upstream = dq_ref[:, at : at + LANES]
            gain = qgain_ref[...]
        else:
            upstream = dkv_ref[:, at - q_width : at - q_width + LANES].astype(F32)
            gain = kgain_ref[...]
        turned = upstream * cos - partner(upstream, lane, head_size) * sin
        inverse = lax.rsqrt(half_sums(part * part, lane, head_size) / head_size + EPS)
        scaled = turned * gain
        inner = half_sums(scaled * part, lane, head_size) / head_size
        grad = inverse * scaled - part * inverse * inverse * inverse * inner
        gain_part = jnp.sum(turned * part * inverse, axis=0, keepdims=True)
        if not is_query:
            grad = jnp.where(lane < head_size, grad, upstream)
            gain_part = jnp.where(lane[:1] < head_size, gain_part, 0.0)
        totals[0 if is_query else 1] += gain_part
        out_ref[:, at : at + LANES] = grad.astype(BF)
    gain_ref[0] = jnp.concatenate(totals, axis=0)


def unproject(raw, dq, dkv, cos, sin, query_gain, key_gain, head_size):
    rows, cols = raw.shape
    q_width = dq.shape[1]
    tile = 256
    whole = lambda i: (0, 0)
    step = lambda i: (i, 0)
    return pl.pallas_call(
        functools.partial(unproject_kernel, head_size),
        grid=(rows // tile,),
        in_specs=[
            pl.BlockSpec((tile, cols), step),
            pl.BlockSpec((tile, q_width), step),
            pl.BlockSpec((tile, cols - q_width), step),
            pl.BlockSpec((tile, LANES), step),
            pl.BlockSpec((tile, LANES), step),
            pl.BlockSpec((1, LANES), whole),
            pl.BlockSpec((1, LANES), whole),
        ],
        out_specs=[
            pl.BlockSpec((tile, cols), step),
            pl.BlockSpec((1, 2, LANES), lambda i: (i, 0, 0)),
        ],
        out_shape=[
            jax.ShapeDtypeStruct((rows, cols), BF),
            jax.ShapeDtypeStruct((rows // tile, 2, LANES), F32),
        ],
        compiler_params=pltpu.CompilerParams(vmem_limit_bytes=12 * MIB),
        cost_estimate=CHEAP,
    )(raw, dq, dkv, cos, sin, query_gain, key_gain)


def head_parts(pair, lane, head_size):
    return (
        jnp.where(lane < head_size, pair, 0.0).astype(BF),
        jnp.where(lane < head_size, pltpu.roll(pair, head_size, 1), 0.0).astype(BF),
    )


def attend_kernel(head_size, lows, first, last, code_ref, base_ref, q_ref, row_ref, key_ref, *refs):
    kv_refs, refs = refs[:lows], refs[lows:]
    if not first:
        (acc_in, sum_in), refs = refs[:2], refs[2:]
    if last:
        exact_ref, low_ref, lse_ref, qs_ref, acc_ref, sum_ref = refs
    else:
        acc_out, sum_out, qs_ref, acc_ref, sum_ref = refs
    batch = pl.program_id(0)
    count = row_ref.shape[1]
    factor = LOG2E * head_size**-0.5
    lane = lane_index((count, LANES))
    some = functools.reduce(jnp.maximum, [code_ref[batch, low] for low in range(lows)]) > 0

    @pl.when(some)
    def _():
        both = q_ref[:, 0].reshape(count, LANES).astype(F32)
        qs_ref[0], qs_ref[1] = head_parts(both, lane, head_size)

    if first:
        acc_ref[...] = jnp.zeros_like(acc_ref)
        sum_ref[...] = jnp.zeros_like(sum_ref)
    else:
        acc_ref[...] = acc_in[0, 0]
        sum_ref[...] = sum_in[0, 0]

    def one(low, masked):
        keys = kv_refs[low][:, 0].reshape(count, LANES)
        if masked:
            key_pos = key_ref[...] + base_ref[low]
            allowed = (key_pos <= row_ref[0, :, 0:1]) & (key_pos >= row_ref[0, :, 1:2])
        for head in range(2):
            exps = jnp.exp2(dot_back(qs_ref[head], keys) * factor)
            if masked:
                exps = jnp.where(allowed, exps, 0.0)
            partial = exps[:, :LANES]
            for lane_at in range(LANES, count, LANES):
                partial = partial + exps[:, lane_at : lane_at + LANES]
            sum_ref[head] += partial
            acc_ref[head] += dot_plain(exps.astype(BF), keys)

    for low in range(lows):
        code = code_ref[batch, low]
        pl.when(code == 1)(functools.partial(one, low, False))
        pl.when(code == 2)(functools.partial(one, low, True))

    if not last:
        acc_out[0, 0] = acc_ref[...]
        sum_out[0, 0] = sum_ref[...]
        return
    results = []
    for head in range(2):
        total = jnp.sum(sum_ref[head], axis=-1, keepdims=True)
        results.append(acc_ref[head] / total)
        wide = jnp.broadcast_to(jnp.log2(total), (count, LANES))
        lse_ref[0, 0, head] = wide.T[:8]
    joined = jnp.where(lane < head_size, pltpu.roll(results[0], head_size, 1), results[1])
    joined = joined.reshape(exact_ref.shape[0], -1, LANES)
    exact_ref[:, 0] = joined
    low_ref[:, 0] = joined.astype(BF)


def attend(codes, bases, query, kvs, row_info, key_pos, state, last, head_size):
    slots, batches, rows, q_width = query.shape
    count = slots * rows
    pairs = q_width // LANES
    pick = lambda b, p, *_: (0, b, 0, p)
    by_pair = lambda b, p, *_: (b, p, 0, 0, 0)
    slab = pl.BlockSpec((slots, 1, rows, LANES), pick)
    wide = pl.BlockSpec((1, 1, 2, count, LANES), by_pair)
    wide_shape = jax.ShapeDtypeStruct((batches, pairs, 2, count, LANES), F32)
    if last:
        out_specs = [slab, slab, pl.BlockSpec((1, 1, 2, 8, count), by_pair)]
        out_shape = [
            jax.ShapeDtypeStruct(query.shape, F32),
            jax.ShapeDtypeStruct(query.shape, BF),
            jax.ShapeDtypeStruct((batches, pairs, 2, 8, count), F32),
        ]
    else:
        out_specs, out_shape = [wide, wide], [wide_shape, wide_shape]
    return pl.pallas_call(
        functools.partial(attend_kernel, head_size, len(kvs), not state, last),
        grid_spec=pltpu.PrefetchScalarGridSpec(
            num_scalar_prefetch=2,
            grid=(batches, pairs),
            in_specs=[
                slab,
                pl.BlockSpec((1, count, 2), lambda b, p, *_: (b, 0, 0)),
                pl.BlockSpec((1, count), lambda b, p, *_: (0, 0)),
            ]
            + [slab] * len(kvs)
            + [wide] * len(state),
            out_specs=out_specs,
            scratch_shapes=[
                pltpu.VMEM((2, count, LANES), BF),
                pltpu.VMEM((2, count, LANES), F32),
                pltpu.VMEM((2, count, LANES), F32),
            ],
        ),
        out_shape=out_shape,
        compiler_params=pltpu.CompilerParams(vmem_limit_bytes=VMEM_LIMIT if count > 512 else 16 * MIB),
        cost_estimate=STEP,
    )(codes, bases, query, row_info, key_pos, *kvs, *state)


def attend_back_kernel(
    head_size,
    lows,
    first,
    last,
    code_ref,
    base_ref,
    q_ref,
    up_ref,
    exact_ref,
    lse_ref,
    row_ref,
    key_ref,
    *refs,
):
    kv_refs, refs = refs[:lows], refs[lows:]
    if not first:
        acc_in, refs = refs[0], refs[1:]
    dkv_refs, refs = refs[:lows], refs[lows:]
    out_ref, qs_ref, us_ref, acc_ref, delta_ref = refs
    batch = pl.program_id(0)
    count = row_ref.shape[2]
    scale = head_size**-0.5
    factor = LOG2E * scale
    lane = lane_index((count, LANES))
    some = functools.reduce(jnp.maximum, [code_ref[batch, low] for low in range(lows)]) > 0

    @pl.when(some)
    def _():
        both = q_ref[:, 0].reshape(count, LANES).astype(F32)
        qs_ref[0], qs_ref[1] = head_parts(both, lane, head_size)
        upper = up_ref[:, 0].reshape(count, LANES).astype(F32)
        us_ref[0] = jnp.where(lane < head_size, 0.0, pltpu.roll(upper, head_size, 1)).astype(BF)
        us_ref[1] = jnp.where(lane < head_size, 0.0, upper).astype(BF)
        products = upper * exact_ref[:, 0].reshape(count, LANES)
        for head in range(2):
            inside = (lane < head_size) if head == 0 else (lane >= head_size)
            total = jnp.sum(jnp.where(inside, products, 0.0), axis=-1, keepdims=True)
            delta_ref[head] = jnp.broadcast_to(total, (count, LANES)).T[:8]

    acc_ref[...] = jnp.zeros_like(acc_ref) if first else acc_in[0, 0]

    def none(low):
        dkv_refs[low][:, 0] = jnp.zeros((kv_refs[low].shape[0],) + kv_refs[low].shape[2:], BF)

    def one(low, masked):
        keys = kv_refs[low][:, 0].reshape(count, LANES)
        if masked:
            key_pos = key_ref[...] + base_ref[low]
            allowed = (key_pos <= row_ref[0, 0:1]) & (key_pos >= row_ref[0, 1:2])
        grad_kv = jnp.zeros((count, LANES), F32)
        for head in range(2):
            scores = dot_back(keys, qs_ref[head]) * factor
            probs = jnp.exp2(scores - lse_ref[0, 0, head, 0:1])
            if masked:
                probs = jnp.where(allowed, probs, 0.0)
            grads = dot_back(keys, us_ref[head])
            grads = (probs * (grads - delta_ref[head, 0:1])).astype(BF)
            grad_kv += dot_plain(probs.astype(BF), us_ref[head])
            grad_kv += dot_plain(grads, qs_ref[head]) * scale
            acc_ref[head] += dot_outer(grads, keys)
        dkv_refs[low][:, 0] = grad_kv.astype(BF).reshape(kv_refs[low].shape[0], -1, LANES)

    for low in range(lows):
        code = code_ref[batch, low]
        pl.when(code == 0)(functools.partial(none, low))
        pl.when(code == 1)(functools.partial(one, low, False))
        pl.when(code == 2)(functools.partial(one, low, True))

    if not last:
        out_ref[0, 0] = acc_ref[...]
        return
    joined = jnp.where(lane < head_size, acc_ref[0], pltpu.roll(acc_ref[1], head_size, 1))
    out_ref[:, 0] = (joined * scale).reshape(out_ref.shape[0], -1, LANES)


def attend_back(codes, bases, query, upstream, exact, lse, kvs, row_info, key_pos, state, last, head_size):
    slots, batches, rows, q_width = query.shape
    count = slots * rows
    pairs = q_width // LANES
    pick = lambda b, p, *_: (0, b, 0, p)
    by_pair = lambda b, p, *_: (b, p, 0, 0, 0)
    slab = pl.BlockSpec((slots, 1, rows, LANES), pick)
    wide = pl.BlockSpec((1, 1, 2, count, LANES), by_pair)
    wide_shape = jax.ShapeDtypeStruct((batches, pairs, 2, count, LANES), F32)
    return pl.pallas_call(
        functools.partial(attend_back_kernel, head_size, len(kvs), not state, last),
        grid_spec=pltpu.PrefetchScalarGridSpec(
            num_scalar_prefetch=2,
            grid=(batches, pairs),
            in_specs=[
                slab,
                slab,
                slab,
                pl.BlockSpec((1, 1, 2, 8, count), by_pair),
                pl.BlockSpec((1, 2, count), lambda b, p, *_: (b, 0, 0)),
                pl.BlockSpec((count, 1), lambda b, p, *_: (0, 0)),
            ]
            + [slab] * len(kvs)
            + [wide] * len(state),
            out_specs=[slab] * len(kvs) + [slab if last else wide],
            scratch_shapes=[
                pltpu.VMEM((2, count, LANES), BF),
                pltpu.VMEM((2, count, LANES), BF),
                pltpu.VMEM((2, count, LANES), F32),
                pltpu.VMEM((2, 8, count), F32),
            ],
        ),
        out_shape=[jax.ShapeDtypeStruct(kvs[0].shape, BF)] * len(kvs)
        + [jax.ShapeDtypeStruct(query.shape, F32) if last else wide_shape],
        compiler_params=pltpu.CompilerParams(vmem_limit_bytes=VMEM_LIMIT if count > 512 else 22 * MIB),
        cost_estimate=STEP,
    )(codes, bases, query, upstream, exact, lse, row_info, key_pos, *kvs, *state)


TILE = 384


def block_order():
    his, los, heads, mids = split_sizes()
    return tuple(
        (hi * los + lo, head * mids + mid)
        for head in range(heads)
        for hi in range(his)
        for mid in range(mids)
        for lo in range(los)
    )


def split_kernel(rank_ref, *refs):
    for slot in range(4):
        gate_ref, up_ref, out_ref = refs[slot], refs[4 + slot], refs[8 + slot]
        for at in range(0, gate_ref.shape[1], TILE):
            out_ref[:, 2 * at : 2 * at + TILE] = gate_ref[:, at : at + TILE]
            out_ref[:, 2 * at + TILE : 2 * at + 2 * TILE] = up_ref[:, at : at + TILE]


def rank_scalar():
    return group_rank()[None].astype(jnp.int32)


def gate_up_blocks(w_gate, w_up):
    rows, cols = w_gate.shape
    part = cols // 4
    picks = [
        pl.BlockSpec((rows, part), lambda i, rank, slot=slot: (0, rank[0] ^ slot)) for slot in range(4)
    ]
    return pl.pallas_call(
        split_kernel,
        grid_spec=pltpu.PrefetchScalarGridSpec(
            num_scalar_prefetch=1,
            grid=(1,),
            in_specs=picks + picks,
            out_specs=[pl.BlockSpec((rows, 2 * part), lambda i, rank: (0, 0))] * 4,
        ),
        out_shape=[jax.ShapeDtypeStruct((rows, 2 * part), w_gate.dtype)] * 4,
        compiler_params=pltpu.CompilerParams(vmem_limit_bytes=6 * MIB),
        cost_estimate=CHEAP,
    )(rank_scalar(), *[w_gate] * 4, *[w_up] * 4)


def merge_kernel(rank_ref, *refs):
    source = pl.program_id(0) ^ rank_ref[0]
    gate_ref, up_ref = refs[4:]
    for slot in range(4):

        @pl.when(source == slot)
        def _(ref=refs[slot]):
            for at in range(0, gate_ref.shape[1], TILE):
                gate_ref[:, at : at + TILE] = ref[:, 2 * at : 2 * at + TILE].astype(F32)
                up_ref[:, at : at + TILE] = ref[:, 2 * at + TILE : 2 * at + 2 * TILE].astype(F32)


def gate_up_merge(blocks):
    rows, both = blocks[0].shape
    column = pl.BlockSpec((rows, both // 2), lambda i, rank: (0, i))
    return pl.pallas_call(
        merge_kernel,
        grid_spec=pltpu.PrefetchScalarGridSpec(
            num_scalar_prefetch=1,
            grid=(4,),
            in_specs=[pl.BlockSpec((rows, both), lambda i, rank: (0, 0))] * 4,
            out_specs=[column, column],
        ),
        out_shape=[jax.ShapeDtypeStruct((rows, 2 * both), F32)] * 2,
        compiler_params=pltpu.CompilerParams(vmem_limit_bytes=6 * MIB),
        cost_estimate=CHEAP,
    )(rank_scalar(), *blocks)


def exchange_blocks(blocks):
    far = [(0, 3), (1, 2), (2, 1), (3, 0)]
    return [
        blocks[0],
        swap(blocks[1], "mid"),
        swap(blocks[2], "heads"),
        lax.ppermute(blocks[3], GROUP, far),
    ]


def feed_kernel(order, rank_ref, x_ref, cot_ref, w_ref, wd_ref, hid_ref, grad_ref, two_ref, w_all, acc_ref):
    rows = w_ref.shape[2]
    for index, (data, source) in enumerate(order):
        w_all[pl.ds(index * rows, rows)] = w_ref[data, source ^ rank_ref[0]]
    step = pl.program_id(0)
    count = x_ref.shape[0]
    part = math.gcd(count, 512)

    @pl.when(step == 0)
    def _():
        acc_ref[...] = jnp.zeros_like(acc_ref)

    for first in range(0, count, part):
        at = pl.ds(first, part)
        both = dot_plain(x_ref[at], w_all[...])
        gate, upper = both[:, :TILE], both[:, TILE:]
        grad_hidden = dot_back(cot_ref[at], wd_ref[...])
        sigmoid = jax.nn.sigmoid(gate)
        silu = gate * sigmoid
        hid_ref[at] = (silu * upper).astype(BF)
        grad_gate = (grad_hidden * upper * sigmoid * (1.0 + gate * (1.0 - sigmoid))).astype(BF)
        grad_upper = (grad_hidden * silu).astype(BF)
        grads = jnp.concatenate([grad_gate, grad_upper], axis=1)
        grad_ref[at] = grads
        acc_ref[at] += dot_back(grads, w_all[...])

    @pl.when(step == pl.num_programs(0) - 1)
    def _():
        two_ref[...] = acc_ref[...].astype(BF)


def feed(x, cot, w_both, wd):
    count, width = x.shape
    cols = wd.shape[0]
    whole = lambda i, rank: (0, 0)
    column = lambda i, rank: (0, i)
    return pl.pallas_call(
        functools.partial(feed_kernel, block_order()),
        grid_spec=pltpu.PrefetchScalarGridSpec(
            num_scalar_prefetch=1,
            grid=(cols // TILE,),
            in_specs=[
                pl.BlockSpec((count, width), whole),
                pl.BlockSpec((count, width), whole),
                pl.BlockSpec(w_both.shape[:3] + (2 * TILE,), lambda i, rank: (0, 0, 0, i)),
                pl.BlockSpec((TILE, width), lambda i, rank: (i, 0)),
            ],
            out_specs=[
                pl.BlockSpec((count, TILE), column),
                pl.BlockSpec((count, 2 * TILE), column),
                pl.BlockSpec((count, width), whole),
            ],
            scratch_shapes=[pltpu.VMEM((width, 2 * TILE), BF), pltpu.VMEM((count, width), F32)],
        ),
        out_shape=[
            jax.ShapeDtypeStruct((count, cols), BF),
            jax.ShapeDtypeStruct((count, 2 * cols), BF),
            jax.ShapeDtypeStruct((count, width), BF),
        ],
        compiler_params=pltpu.CompilerParams(vmem_limit_bytes=44 * MIB),
        cost_estimate=CHEAP,
    )(rank_scalar(), x, cot, w_both, wd)


def gate_grad_kernel(order, rank_ref, x_ref, grad_ref, out_ref, xt_ref):
    rows = out_ref.shape[2]

    @pl.when(pl.program_id(0) == 0)
    def _():
        xt_ref[...] = x_ref[...].T

    result = dot_plain(xt_ref[...], grad_ref[...]).astype(BF)
    for index, (data, source) in enumerate(order):
        out_ref[data, source ^ rank_ref[0]] = result[index * rows : (index + 1) * rows]


def gate_grads(x, grads, shape):
    count, width = x.shape
    return pl.pallas_call(
        functools.partial(gate_grad_kernel, block_order()),
        grid_spec=pltpu.PrefetchScalarGridSpec(
            num_scalar_prefetch=1,
            grid=(grads.shape[1] // (2 * TILE),),
            in_specs=[
                pl.BlockSpec((count, width), lambda i, rank: (0, 0)),
                pl.BlockSpec((count, 2 * TILE), lambda i, rank: (0, i)),
            ],
            out_specs=pl.BlockSpec(shape[:3] + (2 * TILE,), lambda i, rank: (0, 0, 0, i)),
            scratch_shapes=[pltpu.VMEM((width, count), BF)],
        ),
        out_shape=jax.ShapeDtypeStruct(shape, BF),
        compiler_params=pltpu.CompilerParams(vmem_limit_bytes=22 * MIB),
        cost_estimate=CHEAP,
    )(rank_scalar(), x, grads)


def down_kernel(hid_ref, cot_ref, wd_ref, grad_ref, out_ref, acc_ref):
    step = pl.program_id(0)
    hidden = hid_ref[...]
    grad_ref[...] = dot_outer(hidden, cot_ref[...]).astype(BF)
    part = dot_plain(hidden, wd_ref[...])

    @pl.when(step == 0)
    def _():
        acc_ref[...] = part

    @pl.when(step > 0)
    def _():
        acc_ref[...] += part

    @pl.when(step == pl.num_programs(0) - 1)
    def _():
        out_ref[...] = acc_ref[...].astype(BF)


def down_grads(hidden, cot, wd):
    count, cols = hidden.shape
    width = wd.shape[1]
    tile = TILE
    whole = lambda i: (0, 0)
    return pl.pallas_call(
        down_kernel,
        grid=(cols // tile,),
        in_specs=[
            pl.BlockSpec((count, tile), lambda i: (0, i)),
            pl.BlockSpec((count, width), whole),
            pl.BlockSpec((tile, width), lambda i: (i, 0)),
        ],
        out_specs=[
            pl.BlockSpec((tile, width), lambda i: (i, 0)),
            pl.BlockSpec((count, width), whole),
        ],
        out_shape=[
            jax.ShapeDtypeStruct((cols, width), BF),
            jax.ShapeDtypeStruct((count, width), BF),
        ],
        scratch_shapes=[pltpu.VMEM((count, width), F32)],
        compiler_params=pltpu.CompilerParams(vmem_limit_bytes=30 * MIB),
        cost_estimate=CHEAP,
    )(hidden, cot, wd)


def per_device(
    inputs,
    cotangent,
    attn_gain,
    w_query,
    w_key,
    w_value,
    w_output,
    query_gain,
    key_gain,
    ffn_gain,
    w_gate,
    w_up,
    w_down,
    doc_starts,
):
    heads, mids = lax.axis_size("heads"), lax.axis_size("mid")
    his, los = lax.axis_size("hi"), lax.axis_size("lo")
    slots = heads * mids
    batches, _, rows, width = inputs.shape
    block = rows * heads
    count = slots * rows
    head_size = query_gain.shape[0]
    w_rows = w_query.shape[0]
    q_width = w_query.shape[1] // slots
    pairs = w_key.shape[1] // head_size // slots
    ff_width = w_gate.shape[1] // slots

    by_slot = lambda w: w.reshape(w_rows, slots, -1)
    kv_cols = jnp.stack(
        [
            w_key.reshape(w_rows, slots, pairs, head_size),
            w_value.reshape(w_rows, slots, pairs, head_size),
        ],
        axis=3,
    )
    qkv_parts = jnp.concatenate([by_slot(w_query), kv_cols.reshape(w_rows, slots, -1)], axis=2)
    qkv_mine = columns_out(qkv_parts.transpose(1, 0, 2))
    out_rows, down_rows = w_output.shape[0], w_down.shape[0]
    own_in, own_cot = inputs[:, 0], cotangent[:, 0]
    row_part = jnp.concatenate([w_output, w_down], axis=0)
    if is_quad():
        qkv_mine, own_in, row_part, doc_starts = together(qkv_mine, own_in, row_part, doc_starts)
        in_near = group_near(own_in)
    row_part = rows_out(row_part)
    qkv_all = gather_data(qkv_mine)
    fast = is_quad() and fast_rows(w_rows) and ff_width % TILE == 0

    head_at, mid_at = slot_places()
    row_at = jnp.arange(rows, dtype=jnp.int32)
    hi_at, lo_at = lax.axis_index("hi"), lax.axis_index("lo")
    first_pos = ((mid_at * los * block + head_at * rows)[:, None] + row_at[None, :]).reshape(count)
    row_pos = first_pos + hi_at * (mids * los * block) + lo_at * block
    lows = [lo_at] if los == 1 else [lo_at, 1 - lo_at]
    starts = doc_starts[:, None, :]
    row_begin = jnp.max(jnp.where(starts <= row_pos[None, :, None], starts, 0), axis=2)
    row_both = jnp.broadcast_to(row_pos[None], (batches, count))
    begin_low, begin_high = (
        jnp.min(row_begin, axis=1)[:, None],
        jnp.max(row_begin, axis=1)[:, None],
    )

    back = hi_at - jnp.arange(his, dtype=jnp.int32)[:, None]
    bases = back * (mids * los * block) + jnp.stack(lows)[None] * block
    key_low, key_high = (bases + jnp.min(first_pos))[:, None], (bases + jnp.max(first_pos))[:, None]
    none = (key_low > jnp.max(row_pos)) | (key_high < begin_low) | (back < 0)[:, None]
    full = (key_high <= jnp.min(row_pos)) & (key_low >= begin_high)
    codes = jnp.where(none, 0, jnp.where(full, 1, 2)).astype(jnp.int32)
    bases = bases.astype(jnp.int32)
    info_cols = jnp.stack([row_both, row_begin], axis=2)
    info_rows = jnp.stack([row_both, row_begin], axis=1)

    half = head_size // 2
    frequency = THETA ** (-(jnp.arange(half, dtype=F32) * 2.0 / head_size))
    turn_pos = (row_both - row_begin).reshape(batches, slots, rows).transpose(1, 0, 2)
    angles = turn_pos.reshape(-1).astype(F32)[:, None] * frequency[None, :]
    cos, sin = jnp.cos(angles), jnp.sin(angles)
    cos = jnp.concatenate([cos] * 4, axis=1)
    sin = jnp.concatenate([-sin, sin, -sin, sin], axis=1)
    q_gain = jnp.concatenate([query_gain, query_gain])[None]
    k_gain = jnp.concatenate([key_gain, key_gain])[None]

    if is_quad():
        *in_near, cos, sin, info_cols, info_rows, codes, bases = together(
            *in_near, cos, sin, info_cols, info_rows, codes, bases
        )
        in_far = group_far(*in_near)
        *in_far, qkv_all, row_part = together(*in_far, qkv_all, row_part)
        in_all, normed = group_joined(own_in, in_near, in_far, attn_gain)
    else:
        in_all = group_gather(own_in)
        in_wide = in_all.astype(F32)
        normed = (in_wide * rms_inverse(in_wide) * attn_gain).astype(BF)
    row_all = gather_data(row_part)
    w_qkv = natural_rows(qkv_all)
    normed = normed.reshape(-1, width)
    raw, query, kv = project(normed, w_qkv, cos, sin, q_gain, k_gain, q_width, head_size)
    query, w_gate, w_up = together(query, w_gate, w_up)
    if fast:
        gate_up_mine = jnp.stack(exchange_blocks(gate_up_blocks(w_gate, w_up)))
    else:
        gate_up_parts = jnp.concatenate([by_slot(w_gate), by_slot(w_up)], axis=2)
        gate_up_mine = columns_out(gate_up_parts.transpose(1, 0, 2))
    query = query.reshape(slots, batches, rows, q_width)
    moving = kv.reshape(slots, batches, rows, -1)
    kv_steps, state = [], ()
    for step in range(his):
        if step:
            moving = lax.ppermute(moving, "hi", [(i, i + 1) for i in range(step - 1, his - 1)])
            moving, *state = together(moving, *state)
        if step == his - 1:
            moving, gate_up_mine = together(moving, gate_up_mine)
            gate_up_all = gather_data(gate_up_mine)
        kv_steps.append([moving] if los == 1 else [moving, other_low(moving)])
        state = attend(
            codes[step],
            bases[step],
            query,
            kv_steps[step],
            info_cols,
            first_pos[None],
            tuple(state),
            step == his - 1,
            head_size,
        )
        state = list(state)
        if not is_quad():
            continue
        if step == 0:
            gate_up_mine, state[0], cot_own = together(gate_up_mine, state[0], own_cot)
            cot_near = group_near(cot_own)
        if step == 1:
            *cot_near, row_all, state[0] = together(*cot_near, row_all, state[0])
            cot_far = group_far(*cot_near)
            wo_part = row_all[:, :out_rows].reshape(-1, width)
            wd_use = row_all[:, out_rows:].reshape(-1, width)
            wo_near = group_near(wo_part)
        if step == 2:
            *cot_far, state[0] = together(*cot_far, state[0])
            *wo_near, wd_use, state[0] = together(*wo_near, wd_use, state[0])
            wo_far = group_far(*wo_near)
            cot_all = group_joined(cot_own, cot_near, cot_far)
        if step == 3:
            *wo_far, cot_all, state[1] = together(*wo_far, cot_all, state[1])
            wo_full = group_joined(wo_part, wo_near, wo_far)
    exact, attn, lse = state
    if not is_quad():
        cot_all = group_gather(own_cot)
        wo_full = group_gather(row_all[:, :out_rows].reshape(-1, width))
        wd_use = row_all[:, out_rows:].reshape(-1, width)
    wo_full = wo_full.reshape(-1, width)
    attn_wide = columns_out_async(attn.reshape(slots, batches * rows, q_width))
    attn_wide = jnp.concatenate([attn_wide[slot] for slot in range(slots)], axis=1)
    middle = own_in.reshape(-1, width).astype(F32) + dot_plain(attn_wide, wo_full)

    normed_two = (middle * rms_inverse(middle) * ffn_gain).astype(BF)
    normed_two_all = group_gather(normed_two).reshape(-1, width)
    normed_two_all, gate_up_all = together(normed_two_all, gate_up_all)
    cot_rows = cot_all.reshape(-1, width)
    if fast:
        hidden, grads, grad_two = feed(normed_two_all, cot_rows, gate_up_all, wd_use)
        grad_two, grads, hidden = together(grad_two, grads, hidden)
        grad_gate_up = gate_grads(normed_two_all, grads, gate_up_all.shape)
        grad_gate_up = grad_gate_up.reshape(his * los, slots * w_rows, -1)
        grad_down, out_part = down_grads(hidden, cot_rows, wd_use)
    else:
        w_both = natural_rows(gate_up_all)
        both = dot_plain(normed_two_all, w_both)
        gate, upper = both[:, :ff_width], both[:, ff_width:]
        grad_hidden = dot_back(cot_rows, wd_use)
        sigmoid = jax.nn.sigmoid(gate)
        silu = gate * sigmoid
        hidden = (silu * upper).astype(BF)
        grad_gate = grad_hidden * upper * sigmoid * (1.0 + gate * (1.0 - sigmoid))
        grads = jnp.concatenate([grad_gate, grad_hidden * silu], axis=1).astype(BF)
        grad_two = dot_back(grads, w_both).astype(BF)
        grad_gate_up = scatter_order(dot_outer(normed_two_all, grads).astype(BF), w_rows)
        grad_down = dot_outer(hidden, cot_rows).astype(BF)
        out_part = dot_plain(hidden, wd_use).astype(BF)
    in_slots = lambda total: total.reshape(slots, batches * rows, width)
    out_part = in_slots(out_part)
    two_sum = GroupSum(in_slots(grad_two))
    (grad_gate_up,) = two_sum.second(grad_gate_up)
    grad_down, out_part = two_sum.hold(grad_down, out_part)
    grad_two = two_sum.done()
    gate_up_sum = scatter_data(grad_gate_up).reshape(slots, w_rows, -1)
    grad_mid_part, _ = norm_back(middle, ffn_gain, grad_two)
    grad_middle = own_cot.reshape(-1, width).astype(F32) + grad_mid_part

    grad_middle_low = grad_middle.astype(BF)
    grad_attn = dot_back(grad_middle_low, wo_full).astype(BF)
    grad_attn = jnp.stack(
        [grad_attn[:, slot * q_width : (slot + 1) * q_width] for slot in range(slots)]
    )
    grad_attn, grad_middle_low = together(grad_attn, grad_middle_low)
    grad_output = dot_outer(attn_wide, grad_middle_low)
    grad_output = grad_output.astype(BF).reshape(slots, -1, width)
    grad_attn = columns_out_async(grad_attn).reshape(query.shape)
    first_sum = GroupSum(grad_output)
    state, moving = (), None
    for turn in range(1, his + 1):
        step = his - turn
        *dkv, state_out = attend_back(
            codes[step],
            bases[step],
            query,
            grad_attn,
            exact,
            lse,
            kv_steps[step],
            info_rows,
            first_pos[:, None],
            state,
            turn == his,
            head_size,
        )
        if turn > 1:
            *dkv, moving = together(*dkv, moving)
        if turn == 1:
            dkv = first_sum.second(*dkv)
        if turn == min(2, his):
            dkv = first_sum.hold(*dkv)
            out_part, *dkv = together(out_part, *dkv)
            second_sum = GroupSum(out_part)
        if turn == min(3, his):
            dkv = second_sum.second(*dkv)
            dkv = first_sum.hold(*dkv)
            output_part, gate_up_sum = together(first_sum.done().astype(BF), gate_up_sum)
            row_grads = jnp.concatenate(
                [
                    output_part.reshape(his * los, out_rows, width),
                    grad_down.reshape(his * los, down_rows, width),
                ],
                axis=1,
            )
        if turn == min(4, his):
            dkv = second_sum.hold(*dkv)
            row_sum = scatter_data(row_grads)
        parts = [dkv[0]] + ([other_low(dkv[1])] if los == 2 else [])
        parts += [moving] if turn > 1 else []
        if turn < his:
            low, state_out = together(low_sum(*parts), state_out)
            moving = lax.ppermute(low, "hi", [(i, i - 1) for i in range(his - turn, his)])
        state = (state_out,)
    out_sum = second_sum.done()
    dkv_mine = sum(part.astype(F32) for part in parts)
    dq = state[0]
    grad_raw, head_gains = unproject(
        raw,
        dq.reshape(-1, q_width),
        dkv_mine.reshape(raw.shape[0], -1),
        cos,
        sin,
        q_gain,
        k_gain,
        head_size,
    )
    block_out = (middle + out_sum).astype(BF)
    grad_qkv = dot_outer(normed, grad_raw).astype(BF)
    head_sums = jnp.sum(head_gains, axis=0).reshape(2, 2, head_size).sum(axis=1)
    in_wide = in_all.reshape(-1, width).astype(F32)
    normed_back = lambda grads: dot_back(grads, w_qkv).astype(BF)
    gain_vector = lambda low, grad_two, middle: jnp.concatenate(
        [
            jnp.sum(low.astype(F32) * in_wide * rms_inverse(in_wide), axis=0),
            jnp.sum(grad_two * middle * rms_inverse(middle), axis=0),
            head_sums[0],
            head_sums[1],
        ]
    )
    into_slots = lambda low: low.reshape(slots, batches * rows, width)
    if fast:
        own_part, other_part = unplaced(grad_qkv, w_rows, True)
        own_part, other_part, grad_raw = together(own_part, other_part, grad_raw)
        other_part = other_low(other_part)
        grad_normed_low = normed_back(grad_raw)
        other_part, grad_normed_low, gate_up_sum, grad_two, middle = together(
            other_part, grad_normed_low, gate_up_sum, grad_two, middle
        )
        summed = low_sum(own_part, other_part)
        normed_sum = GroupSum(into_slots(grad_normed_low))
        gains = gain_vector(grad_normed_low, grad_two, middle)
        stages = sum_stages()
        moving = None
        for step in range(1, his):
            moving = ring(summed[step] if moving is None else low_sum(summed[step], moving), 1)
            if step == 1:
                moving, gains = normed_sum.second(moving, gains)
                gate_up_back = exchange_blocks([gate_up_sum[slot] for slot in range(4)])
            else:
                gains = stages.pop(0)(gains)
                moving, gains = together(moving, gains)
            if step == his - 1:
                moving, gains = normed_sum.hold(moving, gains)
                held = together(moving, *gate_up_back)
                moving, gate_up_back = held[0], held[1:]
        qkv_sum = low_sum(summed[0], moving) if his > 1 else summed[0]
        qkv_cols = columns_out(qkv_sum)
        for stage in stages:
            gains = stage(gains)
    else:
        gate_up_back = [columns_out(gate_up_sum)]
        grad_qkv = scatter_order(grad_qkv, w_rows)
        qkv_cols = columns_out(scatter_data(grad_qkv).reshape(slots, w_rows, -1))
        grad_normed_low = normed_back(grad_raw)
        gains = all_sum(gain_vector(grad_normed_low, grad_two, middle))
        normed_sum = GroupSum(into_slots(grad_normed_low))
        normed_sum.second()
    grad_normed = normed_sum.done()
    row_back = rows_back(row_sum).astype(F32)
    grad_in_part, _ = norm_back(own_in.reshape(-1, width).astype(F32), attn_gain, grad_normed)
    grad_inputs = grad_middle + grad_in_part

    qkv_cols = qkv_cols.transpose(1, 0, 2).astype(F32)
    if fast:
        gate_cols, up_cols = gate_up_merge(gate_up_back)
    else:
        gate_cols, up_cols = jnp.split(gate_up_back[0].transpose(1, 0, 2).astype(F32), 2, axis=2)
    kv_sums = qkv_cols[:, :, q_width:].reshape(w_rows, slots, pairs, 2, head_size)
    return (
        block_out.reshape(batches, 1, rows, width),
        grad_inputs.reshape(batches, 1, rows, width),
        gains[:width],
        qkv_cols[:, :, :q_width].reshape(w_rows, -1),
        kv_sums[:, :, :, 0].reshape(w_rows, -1),
        kv_sums[:, :, :, 1].reshape(w_rows, -1),
        row_back[:out_rows],
        gains[2 * width : 2 * width + head_size],
        gains[2 * width + head_size :],
        gains[width : 2 * width],
        gate_cols.reshape(w_rows, -1),
        up_cols.reshape(w_rows, -1),
        row_back[out_rows:],
    )


def solution(mesh):
    heads, seq = mesh.shape["heads"], mesh.shape["seq"]
    rows_spec = P(None, SEQ, "heads", None)
    weight_spec = P(ALL, None)

    def run(*args):
        kv_heads = args[4].shape[1] // args[7].shape[0]
        low = 2 if seq % 2 == 0 else 1
        mid = 2 if seq % (2 * low) == 0 and kv_heads % (2 * heads) == 0 else 1
        split = Mesh(
            mesh.devices.reshape(heads, seq // (mid * low), mid, low), ("heads",) + SEQ
        )
        return jax.shard_map(
            per_device,
            mesh=split,
            in_specs=(
                (rows_spec, rows_spec, P())
                + (weight_spec,) * 4
                + (P(), P(), P())
                + (weight_spec,) * 3
                + (P(),)
            ),
            out_specs=(
                (rows_spec, rows_spec, P())
                + (weight_spec,) * 4
                + (P(), P(), P())
                + (weight_spec,) * 3
            ),
            check_vma=False,
        )(*args)

    return run
```

```python
import functools
import math

import jax
import jax.numpy as jnp
from jax import lax
from jax.experimental import pallas as pl
from jax.experimental.pallas import tpu as pltpu
from jax.sharding import Mesh, PartitionSpec as P

EPS = 1e-05
THETA = 1000000.0
LANES = 128
LOG2E = math.log2(math.e)
GROUP = ("heads", "mid")
DATA = ("hi", "lo")
SEQ = ("hi", "mid", "lo")
ALL = ("heads",) + SEQ
BF = jnp.bfloat16
F32 = jnp.float32
MIB = 1024 * 1024
VMEM_LIMIT = 48 * MIB
CHEAP = pl.CostEstimate(flops=1, bytes_accessed=1, transcendentals=0)
STEP = pl.CostEstimate(flops=1, bytes_accessed=1, transcendentals=0)


def dot_plain(left_side, right_side):
    return jnp.dot(left_side, right_side, preferred_element_type=F32)


def dot_back(left_side, right_side):
    return lax.dot_general(
        left_side, right_side, (((1,), (1,)), ((), ())), preferred_element_type=F32
    )


def dot_outer(left_side, right_side):
    return lax.dot_general(
        left_side, right_side, (((0,), (0,)), ((), ())), preferred_element_type=F32
    )


def together(*values):
    return lax.optimization_barrier(values)


def rms_inverse(values):
    return lax.rsqrt(jnp.mean(values * values, axis=-1, keepdims=True) + EPS)


def norm_back(values, gain_vec, upstream):
    inverse = rms_inverse(values)
    scaled = upstream * gain_vec
    inner_mean = jnp.mean(scaled * values, axis=-1, keepdims=True)
    grad_values = inverse * scaled - values * inverse * inverse * inverse * inner_mean
    return (grad_values, upstream * values * inverse)


def is_quad():
    return lax.axis_size("heads") == 2 and lax.axis_size("mid") == 2


def swap(part, axis):
    return lax.ppermute(part, axis, [(0, 1), (1, 0)])


def group_rank():
    return lax.axis_index("heads") * lax.axis_size("mid") + lax.axis_index("mid")


def block_at(parts, index):
    return lax.dynamic_index_in_dim(parts, index, axis=0, keepdims=False)


def in_order(blocks):
    rank = group_rank()
    total = jnp.zeros((4,) + blocks[0].shape, blocks[0].dtype)
    for slot, block in enumerate(blocks):
        total = lax.dynamic_update_index_in_dim(total, block, rank ^ slot, axis=0)
    return total


def group_near(part):
    return swap(part, "mid"), swap(part, "heads")


def group_far(by_mid, by_heads):
    half = by_mid.shape[0] // 2
    return swap(by_mid[:half], "heads"), swap(by_heads[half:], "mid")


def join_kernel(rank_ref, gain_ref, own_ref, mid_ref, head_ref, low_ref, high_ref, out_ref, *normed_ref):
    source = pl.program_id(0) ^ rank_ref[0]
    half = low_ref.shape[0]
    for slot, ref in enumerate((own_ref, mid_ref, head_ref)):

        @pl.when(source == slot)
        def _(ref=ref):
            out_ref[0] = ref[...]

    @pl.when(source == 3)
    def _():
        out_ref[0, :half] = low_ref[...]
        out_ref[0, half:] = high_ref[...]

    if normed_ref:
        values = out_ref[0].astype(F32)
        normed_ref[0][0] = (values * rms_inverse(values) * gain_ref[...]).astype(BF)


def group_joined(part, near, far, gain=None):
    width = part.shape[-1]
    flat = [block.reshape(-1, width) for block in (part, *near, *far)]
    whole = lambda i, rank: (0, 0)
    shape = (4,) + flat[0].shape
    outs = 1 if gain is None else 2
    out_spec = pl.BlockSpec((1,) + flat[0].shape, lambda i, rank: (i, 0, 0))
    gain_vec = jnp.zeros((1, width), F32) if gain is None else gain[None]
    result = pl.pallas_call(
        join_kernel,
        grid_spec=pltpu.PrefetchScalarGridSpec(
            num_scalar_prefetch=1,
            grid=(4,),
            in_specs=[pl.BlockSpec((1, width), whole)]
            + [pl.BlockSpec(block.shape, whole) for block in flat],
            out_specs=[out_spec] * outs,
        ),
        out_shape=[jax.ShapeDtypeStruct(shape, part.dtype)] * outs,
        compiler_params=pltpu.CompilerParams(vmem_limit_bytes=10 * MIB),
        cost_estimate=CHEAP,
    )(group_rank()[None].astype(jnp.int32), gain_vec, *flat)
    total = result[0].reshape((4,) + part.shape)
    return total if gain is None else (total, result[1].reshape(total.shape))


def group_gather(part):
    if not is_quad():
        return lax.all_gather(part, GROUP, axis=0, tiled=False)
    near = group_near(part)
    return group_joined(part, near, group_far(*near))


def group_gather_plain(part):
    return lax.all_gather(part, GROUP, axis=0, tiled=False)


def group_sum_plain(parts):
    flat = parts.reshape((-1,) + parts.shape[2:])
    return lax.psum_scatter(flat, GROUP, scatter_dimension=0, tiled=True)


class GroupSum:
    def __init__(self, parts):
        if is_quad():
            rank = group_rank()
            self.parts = [block_at(parts, rank ^ slot) for slot in range(4)]
            half = parts.shape[1] // 2
            far = self.parts[3]
            self.far = (swap(far[:half], "mid"), swap(far[half:], "heads"))
        else:
            self.total = group_sum_plain(parts)

    def second(self, *between):
        if is_quad():
            _, mid, head, _ = self.parts
            half = mid.shape[0] // 2
            far_low, far_high = self.far
            if between:
                far_low, far_high, *between = together(far_low, far_high, *between)
            for_mid = jnp.concatenate([mid[:half], low_sum(mid[half:], far_high)], axis=0)
            for_heads = jnp.concatenate([low_sum(head[:half], far_low), head[half:]], axis=0)
            self.near = (swap(for_mid, "mid"), swap(for_heads, "heads"))
        return between

    def hold(self, *later):
        if is_quad():
            near_mid, near_heads, *later = together(*self.near, *later)
            self.near = (near_mid, near_heads)
        return later

    def done(self):
        if not is_quad():
            return self.total.astype(F32)
        return self.parts[0].astype(F32) + self.near[0].astype(F32) + self.near[1].astype(F32)


def slot_places():
    mids = lax.axis_size("mid")
    slots = jnp.arange(lax.axis_size("heads") * mids, dtype=jnp.int32)
    return (slots // mids, slots % mids)


def sum_stages():
    def along_hi(vector):
        size = lax.axis_size("hi")
        parts = [vector]
        for shift in range(1, size):
            parts.append(lax.ppermute(vector, "hi", [(i, (i + shift) % size) for i in range(size)]))
        return sum(parts[1:], parts[0])

    def along_low(vector):
        return vector + swap(vector, "lo")

    def along_group(vector):
        far = [(0, 3), (1, 2), (2, 1), (3, 0)]
        near = swap(vector, "mid") + swap(vector, "heads")
        return vector + near + lax.ppermute(vector, GROUP, far)

    return [along_hi, along_low, along_group]


def all_sum(vector):
    for axis in ("lo", "mid", "heads", "hi"):
        size = lax.axis_size(axis)
        if size & (size - 1):
            vector = lax.psum(vector, axis)
            continue
        step = 1
        while step < size:
            vector = vector + lax.ppermute(vector, axis, [(i, i ^ step) for i in range(size)])
            step *= 2
    return vector


def columns_out(parts):
    return lax.all_to_all(parts, GROUP, split_axis=0, concat_axis=0, tiled=True)


def columns_out_async(parts):
    if not is_quad():
        return columns_out(parts)
    rank = group_rank()
    far = [(0, 3), (1, 2), (2, 1), (3, 0)]
    return in_order(
        [
            block_at(parts, rank),
            swap(block_at(parts, rank ^ 1), "mid"),
            swap(block_at(parts, rank ^ 2), "heads"),
            lax.ppermute(block_at(parts, rank ^ 3), GROUP, far),
        ]
    )


def ring(part, shift):
    size = lax.axis_size("hi")
    return lax.ppermute(part, "hi", [(i, (i + shift) % size) for i in range(size)])


def other_low(part):
    return swap(part, "lo")


def fast_rows(rows):
    return lax.axis_size("lo") == 2 and rows % 16 == 0


def data_ring(part):
    own = [part]
    for _ in range(lax.axis_size("hi") - 1):
        own.append(ring(own[-1], 1))
    return own, [other_low(piece) for piece in own]


def place_index():
    return jnp.stack(
        [lax.axis_index("hi"), lax.axis_index("lo"), lax.axis_index("heads"), lax.axis_index("mid")]
    ).astype(jnp.int32)


def block_row(at_ref, sizes, step, other, source):
    his, los, heads, mids = sizes
    hi = lax.rem(at_ref[0] - step + his, his)
    low = 1 - at_ref[1] if other else at_ref[1]
    if source is None:
        return hi * los + low
    return ((source // mids * his + hi) * mids + source % mids) * los + low


def split_sizes():
    return tuple(lax.axis_size(name) for name in ("hi", "lo", "heads", "mid"))


def place_kernel(sizes, sources, rows, at_ref, *refs):
    his = sizes[0]
    pieces, out_ref, sems = refs[: 2 * his], refs[2 * his], refs[2 * his + 1]
    copies = []
    for step in range(his):
        for other in range(2):
            for source in sources:
                first = block_row(at_ref, sizes, step, other, source) * rows
                piece = pieces[step + other * his]
                copies.append(
                    pltpu.make_async_copy(
                        piece if source is None else piece.at[source],
                        out_ref.at[pl.ds(pl.multiple_of(first, rows), rows)],
                        sems.at[len(copies)],
                    )
                )
    for copy in copies:
        copy.start()
    for copy in copies:
        copy.wait()


def placed(own, other):
    sizes = split_sizes()
    first = own[0]
    rows, cols = first.shape[-2:]
    sources = range(first.shape[0]) if first.ndim == 3 else (None,)
    total = rows * sizes[0] * sizes[1] * len(sources)
    anywhere = pl.BlockSpec(memory_space=pl.ANY)
    return pl.pallas_call(
        functools.partial(place_kernel, sizes, sources, rows),
        in_specs=[pl.BlockSpec(memory_space=pltpu.SMEM)] + [anywhere] * (2 * sizes[0]),
        out_specs=pl.BlockSpec(memory_space=pltpu.VMEM),
        out_shape=jax.ShapeDtypeStruct((total, cols), first.dtype),
        scratch_shapes=[pltpu.SemaphoreType.DMA((2 * sizes[0] * len(sources),))],
        compiler_params=pltpu.CompilerParams(vmem_limit_bytes=8 * MIB),
        cost_estimate=CHEAP,
    )(place_index(), *own, *other)


def unplace_kernel(sizes, sources, rows, at_ref, full_ref, own_ref, other_ref, sems):
    his = sizes[0]
    copies = []
    for step in range(his):
        for other in range(2):
            for source in sources:
                first = block_row(at_ref, sizes, step, other, source) * rows
                target = (other_ref if other else own_ref).at[step]
                copies.append(
                    pltpu.make_async_copy(
                        full_ref.at[pl.ds(pl.multiple_of(first, rows), rows)],
                        target if source is None else target.at[source],
                        sems.at[len(copies)],
                    )
                )
    for copy in copies:
        copy.start()
    for copy in copies:
        copy.wait()


def unplaced(full, rows, by_source):
    sizes = split_sizes()
    cols = full.shape[1]
    slots = sizes[2] * sizes[3]
    sources = range(slots) if by_source else (None,)
    shape = (sizes[0],) + ((slots,) if by_source else ()) + (rows, cols)
    anywhere = pl.BlockSpec(memory_space=pl.ANY)
    return pl.pallas_call(
        functools.partial(unplace_kernel, sizes, sources, rows),
        in_specs=[pl.BlockSpec(memory_space=pltpu.SMEM), pl.BlockSpec(memory_space=pltpu.VMEM)],
        out_specs=[anywhere, anywhere],
        out_shape=[jax.ShapeDtypeStruct(shape, full.dtype)] * 2,
        scratch_shapes=[pltpu.SemaphoreType.DMA((2 * sizes[0] * len(sources),))],
        compiler_params=pltpu.CompilerParams(vmem_limit_bytes=8 * MIB),
        cost_estimate=CHEAP,
    )(place_index(), full)


def natural_rows(gathered):
    his, los, heads, mids = split_sizes()
    rows, cols = gathered.shape[2:]
    parts = gathered.reshape(his, los, heads, mids, rows, cols)
    return parts.transpose(2, 0, 3, 1, 4, 5).reshape(-1, cols)


def gather_data(part):
    return lax.all_gather(part, DATA, axis=0, tiled=False)


def gather_rows(part):
    if fast_rows(part.shape[-2]):
        return placed(*data_ring(part))
    return natural_rows(gather_data(part))


def low_sum(*parts):
    total = parts[0].astype(F32)
    for part in parts[1:]:
        total = total + part.astype(F32)
    return total.astype(BF)


def scatter_data(parts):
    return lax.psum_scatter(parts, DATA, scatter_dimension=0, tiled=False)


def scatter_order(grads, rows):
    his, los, heads, mids = split_sizes()
    cols = grads.shape[1]
    parts = grads.reshape(heads, his, mids, los, rows, cols).transpose(1, 3, 0, 2, 4, 5)
    return parts.reshape(his * los, heads * mids * rows, cols)


def scatter_ring(summed):
    moving = None
    for step in range(1, lax.axis_size("hi")):
        part = summed[step]
        moving = ring(part if moving is None else low_sum(part, moving), 1)
    return summed[0] if moving is None else low_sum(summed[0], moving)


def row_moves():
    mids, los = lax.axis_size("mid"), lax.axis_size("lo")
    count = lax.axis_size("hi") * mids * los
    share = count // mids
    moves = []
    for source in range(count):
        owner, rest = source // share, source % share
        moves.append((source, ((rest // los) * mids + owner) * los + rest % los))
    return moves


def rows_out(part):
    return lax.ppermute(part, SEQ, row_moves())


def rows_back(part):
    return lax.ppermute(part, SEQ, [(there, here) for here, there in row_moves()])


def lane_index(shape):
    return lax.broadcasted_iota(jnp.int32, shape, len(shape) - 1)


def half_sums(values, lane, head_size):
    first = jnp.sum(jnp.where(lane < head_size, values, 0.0), axis=-1, keepdims=True)
    second = jnp.sum(jnp.where(lane < head_size, 0.0, values), axis=-1, keepdims=True)
    return jnp.where(lane < head_size, first, second)


def partner(values, lane, head_size):
    quarter = head_size // 2
    return jnp.where(
        lane % head_size < quarter,
        pltpu.roll(values, LANES - quarter, 1),
        pltpu.roll(values, quarter, 1),
    )


def project_kernel(
    head_size, normed_ref, w_ref, cos_ref, sin_ref, qgain_ref, kgain_ref, raw_ref, q_ref, kv_ref
):
    raw = dot_plain(normed_ref[...], w_ref[...])
    raw_ref[...] = raw
    cos, sin = cos_ref[...], sin_ref[...]
    lane = lane_index(cos.shape)
    q_width = q_ref.shape[1]
    for at in range(0, raw.shape[1], LANES):
        part = raw[:, at : at + LANES]
        is_query = at < q_width
        inverse = lax.rsqrt(half_sums(part * part, lane, head_size) / head_size + EPS)
        scaled = part * inverse * (qgain_ref[...] if is_query else kgain_ref[...])
        turned = scaled * cos + partner(scaled, lane, head_size) * sin
        if is_query:
            q_ref[:, at : at + LANES] = turned.astype(BF)
        else:
            out_at = at - q_width
            kv_ref[:, out_at : out_at + LANES] = jnp.where(lane < head_size, turned, part).astype(BF)


def project(normed, w_qkv, cos, sin, query_gain, key_gain, q_width, head_size):
    rows, width = normed.shape
    cols = w_qkv.shape[1]
    tile = 256
    whole = lambda i: (0, 0)
    step = lambda i: (i, 0)
    return pl.pallas_call(
        functools.partial(project_kernel, head_size),
        grid=(rows // tile,),
        in_specs=[
            pl.BlockSpec((tile, width), step),
            pl.BlockSpec((width, cols), whole),
            pl.BlockSpec((tile, LANES), step),
            pl.BlockSpec((tile, LANES), step),
            pl.BlockSpec((1, LANES), whole),
            pl.BlockSpec((1, LANES), whole),
        ],
        out_specs=[
            pl.BlockSpec((tile, cols), step),
            pl.BlockSpec((tile, q_width), step),
            pl.BlockSpec((tile, cols - q_width), step),
        ],
        out_shape=[
            jax.ShapeDtypeStruct((rows, cols), F32),
            jax.ShapeDtypeStruct((rows, q_width), BF),
            jax.ShapeDtypeStruct((rows, cols - q_width), BF),
        ],
        compiler_params=pltpu.CompilerParams(vmem_limit_bytes=12 * MIB),
        cost_estimate=CHEAP,
    )(normed, w_qkv, cos, sin, query_gain, key_gain)


def unproject_kernel(
    head_size, raw_ref, dq_ref, dkv_ref, cos_ref, sin_ref, qgain_ref, kgain_ref, out_ref, gain_ref
):
    cos, sin = cos_ref[...], sin_ref[...]
    lane = lane_index(cos.shape)
    q_width = dq_ref.shape[1]
    totals = [jnp.zeros((1, LANES), F32), jnp.zeros((1, LANES), F32)]
    for at in range(0, raw_ref.shape[1], LANES):
        part = raw_ref[:, at : at + LANES]
        is_query = at < q_width
        if is_query:
            upstream = dq_ref[:, at : at + LANES]
            gain = qgain_ref[...]
        else:
            upstream = dkv_ref[:, at - q_width : at - q_width + LANES].astype(F32)
            gain = kgain_ref[...]
        turned = upstream * cos - partner(upstream, lane, head_size) * sin
        inverse = lax.rsqrt(half_sums(part * part, lane, head_size) / head_size + EPS)
        scaled = turned * gain
        inner = half_sums(scaled * part, lane, head_size) / head_size
        grad = inverse * scaled - part * inverse * inverse * inverse * inner
        gain_part = jnp.sum(turned * part * inverse, axis=0, keepdims=True)
        if not is_query:
            grad = jnp.where(lane < head_size, grad, upstream)
            gain_part = jnp.where(lane[:1] < head_size, gain_part, 0.0)
        totals[0 if is_query else 1] += gain_part
        out_ref[:, at : at + LANES] = grad.astype(BF)
    gain_ref[0] = jnp.concatenate(totals, axis=0)


def unproject(raw, dq, dkv, cos, sin, query_gain, key_gain, head_size):
    rows, cols = raw.shape
    q_width = dq.shape[1]
    tile = 256
    whole = lambda i: (0, 0)
    step = lambda i: (i, 0)
    return pl.pallas_call(
        functools.partial(unproject_kernel, head_size),
        grid=(rows // tile,),
        in_specs=[
            pl.BlockSpec((tile, cols), step),
            pl.BlockSpec((tile, q_width), step),
            pl.BlockSpec((tile, cols - q_width), step),
            pl.BlockSpec((tile, LANES), step),
            pl.BlockSpec((tile, LANES), step),
            pl.BlockSpec((1, LANES), whole),
            pl.BlockSpec((1, LANES), whole),
        ],
        out_specs=[
            pl.BlockSpec((tile, cols), step),
            pl.BlockSpec((1, 2, LANES), lambda i: (i, 0, 0)),
        ],
        out_shape=[
            jax.ShapeDtypeStruct((rows, cols), BF),
            jax.ShapeDtypeStruct((rows // tile, 2, LANES), F32),
        ],
        compiler_params=pltpu.CompilerParams(vmem_limit_bytes=12 * MIB),
        cost_estimate=CHEAP,
    )(raw, dq, dkv, cos, sin, query_gain, key_gain)


def head_parts(pair, lane, head_size):
    return (
        jnp.where(lane < head_size, pair, 0.0).astype(BF),
        jnp.where(lane < head_size, pltpu.roll(pair, head_size, 1), 0.0).astype(BF),
    )


def attend_kernel(head_size, lows, first, last, code_ref, base_ref, q_ref, row_ref, key_ref, *refs):
    kv_refs, refs = refs[:lows], refs[lows:]
    if not first:
        (acc_in, sum_in), refs = refs[:2], refs[2:]
    if last:
        exact_ref, low_ref, lse_ref, qs_ref, acc_ref, sum_ref = refs
    else:
        acc_out, sum_out, qs_ref, acc_ref, sum_ref = refs
    batch = pl.program_id(0)
    count = row_ref.shape[1]
    factor = LOG2E * head_size**-0.5
    lane = lane_index((count, LANES))
    some = functools.reduce(jnp.maximum, [code_ref[batch, low] for low in range(lows)]) > 0

    @pl.when(some)
    def _():
        both = q_ref[:, 0].reshape(count, LANES).astype(F32)
        qs_ref[0], qs_ref[1] = head_parts(both, lane, head_size)

    if first:
        acc_ref[...] = jnp.zeros_like(acc_ref)
        sum_ref[...] = jnp.zeros_like(sum_ref)
    else:
        acc_ref[...] = acc_in[0, 0]
        sum_ref[...] = sum_in[0, 0]

    def one(low, masked):
        keys = kv_refs[low][:, 0].reshape(count, LANES)
        if masked:
            key_pos = key_ref[...] + base_ref[low]
            allowed = (key_pos <= row_ref[0, :, 0:1]) & (key_pos >= row_ref[0, :, 1:2])
        for head in range(2):
            exps = jnp.exp2(dot_back(qs_ref[head], keys) * factor)
            if masked:
                exps = jnp.where(allowed, exps, 0.0)
            partial = exps[:, :LANES]
            for lane_at in range(LANES, count, LANES):
                partial = partial + exps[:, lane_at : lane_at + LANES]
            sum_ref[head] += partial
            acc_ref[head] += dot_plain(exps.astype(BF), keys)

    for low in range(lows):
        code = code_ref[batch, low]
        pl.when(code == 1)(functools.partial(one, low, False))
        pl.when(code == 2)(functools.partial(one, low, True))

    if not last:
        acc_out[0, 0] = acc_ref[...]
        sum_out[0, 0] = sum_ref[...]
        return
    results = []
    for head in range(2):
        total = jnp.sum(sum_ref[head], axis=-1, keepdims=True)
        results.append(acc_ref[head] / total)
        wide = jnp.broadcast_to(jnp.log2(total), (count, LANES))
        lse_ref[0, 0, head] = wide.T[:8]
    joined = jnp.where(lane < head_size, pltpu.roll(results[0], head_size, 1), results[1])
    joined = joined.reshape(exact_ref.shape[0], -1, LANES)
    exact_ref[:, 0] = joined
    low_ref[:, 0] = joined.astype(BF)


def attend(codes, bases, query, kvs, row_info, key_pos, state, last, head_size):
    slots, batches, rows, q_width = query.shape
    count = slots * rows
    pairs = q_width // LANES
    pick = lambda b, p, *_: (0, b, 0, p)
    by_pair = lambda b, p, *_: (b, p, 0, 0, 0)
    slab = pl.BlockSpec((slots, 1, rows, LANES), pick)
    wide = pl.BlockSpec((1, 1, 2, count, LANES), by_pair)
    wide_shape = jax.ShapeDtypeStruct((batches, pairs, 2, count, LANES), F32)
    if last:
        out_specs = [slab, slab, pl.BlockSpec((1, 1, 2, 8, count), by_pair)]
        out_shape = [
            jax.ShapeDtypeStruct(query.shape, F32),
            jax.ShapeDtypeStruct(query.shape, BF),
            jax.ShapeDtypeStruct((batches, pairs, 2, 8, count), F32),
        ]
    else:
        out_specs, out_shape = [wide, wide], [wide_shape, wide_shape]
    return pl.pallas_call(
        functools.partial(attend_kernel, head_size, len(kvs), not state, last),
        grid_spec=pltpu.PrefetchScalarGridSpec(
            num_scalar_prefetch=2,
            grid=(batches, pairs),
            in_specs=[
                slab,
                pl.BlockSpec((1, count, 2), lambda b, p, *_: (b, 0, 0)),
                pl.BlockSpec((1, count), lambda b, p, *_: (0, 0)),
            ]
            + [slab] * len(kvs)
            + [wide] * len(state),
            out_specs=out_specs,
            scratch_shapes=[
                pltpu.VMEM((2, count, LANES), BF),
                pltpu.VMEM((2, count, LANES), F32),
                pltpu.VMEM((2, count, LANES), F32),
            ],
        ),
        out_shape=out_shape,
        compiler_params=pltpu.CompilerParams(vmem_limit_bytes=VMEM_LIMIT if count > 512 else 32 * MIB),
        cost_estimate=STEP,
    )(codes, bases, query, row_info, key_pos, *kvs, *state)


def attend_back_kernel(
    head_size,
    lows,
    first,
    last,
    code_ref,
    base_ref,
    q_ref,
    up_ref,
    exact_ref,
    lse_ref,
    row_ref,
    key_ref,
    *refs,
):
    kv_refs, refs = refs[:lows], refs[lows:]
    if not first:
        acc_in, refs = refs[0], refs[1:]
    dkv_refs, refs = refs[:lows], refs[lows:]
    out_ref, qs_ref, us_ref, acc_ref, delta_ref = refs
    batch = pl.program_id(0)
    count = row_ref.shape[2]
    scale = head_size**-0.5
    factor = LOG2E * scale
    lane = lane_index((count, LANES))
    some = functools.reduce(jnp.maximum, [code_ref[batch, low] for low in range(lows)]) > 0

    @pl.when(some)
    def _():
        both = q_ref[:, 0].reshape(count, LANES).astype(F32)
        qs_ref[0], qs_ref[1] = head_parts(both, lane, head_size)
        upper = up_ref[:, 0].reshape(count, LANES).astype(F32)
        us_ref[0] = jnp.where(lane < head_size, 0.0, pltpu.roll(upper, head_size, 1)).astype(BF)
        us_ref[1] = jnp.where(lane < head_size, 0.0, upper).astype(BF)
        products = upper * exact_ref[:, 0].reshape(count, LANES)
        for head in range(2):
            inside = (lane < head_size) if head == 0 else (lane >= head_size)
            total = jnp.sum(jnp.where(inside, products, 0.0), axis=-1, keepdims=True)
            delta_ref[head] = jnp.broadcast_to(total, (count, LANES)).T[:8]

    acc_ref[...] = jnp.zeros_like(acc_ref) if first else acc_in[0, 0]

    def none(low):
        dkv_refs[low][:, 0] = jnp.zeros((kv_refs[low].shape[0],) + kv_refs[low].shape[2:], BF)

    def one(low, masked):
        keys = kv_refs[low][:, 0].reshape(count, LANES)
        if masked:
            key_pos = key_ref[...] + base_ref[low]
            allowed = (key_pos <= row_ref[0, 0:1]) & (key_pos >= row_ref[0, 1:2])
        grad_kv = jnp.zeros((count, LANES), F32)
        for head in range(2):
            scores = dot_back(keys, qs_ref[head]) * factor
            probs = jnp.exp2(scores - lse_ref[0, 0, head, 0:1])
            if masked:
                probs = jnp.where(allowed, probs, 0.0)
            grads = dot_back(keys, us_ref[head])
            grads = (probs * (grads - delta_ref[head, 0:1])).astype(BF)
            grad_kv += dot_plain(probs.astype(BF), us_ref[head])
            grad_kv += dot_plain(grads, qs_ref[head]) * scale
            acc_ref[head] += dot_outer(grads, keys)
        dkv_refs[low][:, 0] = grad_kv.astype(BF).reshape(kv_refs[low].shape[0], -1, LANES)

    for low in range(lows):
        code = code_ref[batch, low]
        pl.when(code == 0)(functools.partial(none, low))
        pl.when(code == 1)(functools.partial(one, low, False))
        pl.when(code == 2)(functools.partial(one, low, True))

    if not last:
        out_ref[0, 0] = acc_ref[...]
        return
    joined = jnp.where(lane < head_size, acc_ref[0], pltpu.roll(acc_ref[1], head_size, 1))
    out_ref[:, 0] = (joined * scale).reshape(out_ref.shape[0], -1, LANES)


def attend_back(codes, bases, query, upstream, exact, lse, kvs, row_info, key_pos, state, last, head_size):
    slots, batches, rows, q_width = query.shape
    count = slots * rows
    pairs = q_width // LANES
    pick = lambda b, p, *_: (0, b, 0, p)
    by_pair = lambda b, p, *_: (b, p, 0, 0, 0)
    slab = pl.BlockSpec((slots, 1, rows, LANES), pick)
    wide = pl.BlockSpec((1, 1, 2, count, LANES), by_pair)
    wide_shape = jax.ShapeDtypeStruct((batches, pairs, 2, count, LANES), F32)
    return pl.pallas_call(
        functools.partial(attend_back_kernel, head_size, len(kvs), not state, last),
        grid_spec=pltpu.PrefetchScalarGridSpec(
            num_scalar_prefetch=2,
            grid=(batches, pairs),
            in_specs=[
                slab,
                slab,
                slab,
                pl.BlockSpec((1, 1, 2, 8, count), by_pair),
                pl.BlockSpec((1, 2, count), lambda b, p, *_: (b, 0, 0)),
                pl.BlockSpec((count, 1), lambda b, p, *_: (0, 0)),
            ]
            + [slab] * len(kvs)
            + [wide] * len(state),
            out_specs=[slab] * len(kvs) + [slab if last else wide],
            scratch_shapes=[
                pltpu.VMEM((2, count, LANES), BF),
                pltpu.VMEM((2, count, LANES), BF),
                pltpu.VMEM((2, count, LANES), F32),
                pltpu.VMEM((2, 8, count), F32),
            ],
        ),
        out_shape=[jax.ShapeDtypeStruct(kvs[0].shape, BF)] * len(kvs)
        + [jax.ShapeDtypeStruct(query.shape, F32) if last else wide_shape],
        compiler_params=pltpu.CompilerParams(vmem_limit_bytes=VMEM_LIMIT if count > 512 else 22 * MIB),
        cost_estimate=STEP,
    )(codes, bases, query, upstream, exact, lse, row_info, key_pos, *kvs, *state)


TILE = 384


def block_order():
    his, los, heads, mids = split_sizes()
    return tuple(
        (hi * los + lo, head * mids + mid)
        for head in range(heads)
        for hi in range(his)
        for mid in range(mids)
        for lo in range(los)
    )


def split_kernel(rank_ref, *refs):
    for slot in range(4):
        gate_ref, up_ref, out_ref = refs[slot], refs[4 + slot], refs[8 + slot]
        for at in range(0, gate_ref.shape[1], TILE):
            out_ref[:, 2 * at : 2 * at + TILE] = gate_ref[:, at : at + TILE]
            out_ref[:, 2 * at + TILE : 2 * at + 2 * TILE] = up_ref[:, at : at + TILE]


def rank_scalar():
    return group_rank()[None].astype(jnp.int32)


def gate_up_blocks(w_gate, w_up):
    rows, cols = w_gate.shape
    part = cols // 4
    picks = [
        pl.BlockSpec((rows, part), lambda i, rank, slot=slot: (0, rank[0] ^ slot)) for slot in range(4)
    ]
    return pl.pallas_call(
        split_kernel,
        grid_spec=pltpu.PrefetchScalarGridSpec(
            num_scalar_prefetch=1,
            grid=(1,),
            in_specs=picks + picks,
            out_specs=[pl.BlockSpec((rows, 2 * part), lambda i, rank: (0, 0))] * 4,
        ),
        out_shape=[jax.ShapeDtypeStruct((rows, 2 * part), w_gate.dtype)] * 4,
        compiler_params=pltpu.CompilerParams(vmem_limit_bytes=6 * MIB),
        cost_estimate=CHEAP,
    )(rank_scalar(), *[w_gate] * 4, *[w_up] * 4)


def merge_kernel(rank_ref, *refs):
    source = pl.program_id(0) ^ rank_ref[0]
    gate_ref, up_ref = refs[4:]
    for slot in range(4):

        @pl.when(source == slot)
        def _(ref=refs[slot]):
            for at in range(0, gate_ref.shape[1], TILE):
                gate_ref[:, at : at + TILE] = ref[:, 2 * at : 2 * at + TILE].astype(F32)
                up_ref[:, at : at + TILE] = ref[:, 2 * at + TILE : 2 * at + 2 * TILE].astype(F32)


def gate_up_merge(blocks):
    rows, both = blocks[0].shape
    column = pl.BlockSpec((rows, both // 2), lambda i, rank: (0, i))
    return pl.pallas_call(
        merge_kernel,
        grid_spec=pltpu.PrefetchScalarGridSpec(
            num_scalar_prefetch=1,
            grid=(4,),
            in_specs=[pl.BlockSpec((rows, both), lambda i, rank: (0, 0))] * 4,
            out_specs=[column, column],
        ),
        out_shape=[jax.ShapeDtypeStruct((rows, 2 * both), F32)] * 2,
        compiler_params=pltpu.CompilerParams(vmem_limit_bytes=6 * MIB),
        cost_estimate=CHEAP,
    )(rank_scalar(), *blocks)


def exchange_blocks(blocks):
    far = [(0, 3), (1, 2), (2, 1), (3, 0)]
    return [
        blocks[0],
        swap(blocks[1], "mid"),
        swap(blocks[2], "heads"),
        lax.ppermute(blocks[3], GROUP, far),
    ]


def feed_kernel(order, rank_ref, x_ref, cot_ref, w_ref, wd_ref, hid_ref, grad_ref, two_ref, w_all, acc_ref):
    rows = w_ref.shape[2]
    for index, (data, source) in enumerate(order):
        w_all[pl.ds(index * rows, rows)] = w_ref[data, source ^ rank_ref[0]]
    step = pl.program_id(0)
    count = x_ref.shape[0]
    part = math.gcd(count, 512)

    @pl.when(step == 0)
    def _():
        acc_ref[...] = jnp.zeros_like(acc_ref)

    for first in range(0, count, part):
        at = pl.ds(first, part)
        both = dot_plain(x_ref[at], w_all[...])
        gate, upper = both[:, :TILE], both[:, TILE:]
        grad_hidden = dot_back(cot_ref[at], wd_ref[...])
        sigmoid = jax.nn.sigmoid(gate)
        silu = gate * sigmoid
        hid_ref[at] = (silu * upper).astype(BF)
        grad_gate = (grad_hidden * upper * sigmoid * (1.0 + gate * (1.0 - sigmoid))).astype(BF)
        grad_upper = (grad_hidden * silu).astype(BF)
        grads = jnp.concatenate([grad_gate, grad_upper], axis=1)
        grad_ref[at] = grads
        acc_ref[at] += dot_back(grads, w_all[...])

    @pl.when(step == pl.num_programs(0) - 1)
    def _():
        two_ref[...] = acc_ref[...].astype(BF)


def feed(x, cot, w_both, wd):
    count, width = x.shape
    cols = wd.shape[0]
    whole = lambda i, rank: (0, 0)
    column = lambda i, rank: (0, i)
    return pl.pallas_call(
        functools.partial(feed_kernel, block_order()),
        grid_spec=pltpu.PrefetchScalarGridSpec(
            num_scalar_prefetch=1,
            grid=(cols // TILE,),
            in_specs=[
                pl.BlockSpec((count, width), whole),
                pl.BlockSpec((count, width), whole),
                pl.BlockSpec(w_both.shape[:3] + (2 * TILE,), lambda i, rank: (0, 0, 0, i)),
                pl.BlockSpec((TILE, width), lambda i, rank: (i, 0)),
            ],
            out_specs=[
                pl.BlockSpec((count, TILE), column),
                pl.BlockSpec((count, 2 * TILE), column),
                pl.BlockSpec((count, width), whole),
            ],
            scratch_shapes=[pltpu.VMEM((width, 2 * TILE), BF), pltpu.VMEM((count, width), F32)],
        ),
        out_shape=[
            jax.ShapeDtypeStruct((count, cols), BF),
            jax.ShapeDtypeStruct((count, 2 * cols), BF),
            jax.ShapeDtypeStruct((count, width), BF),
        ],
        compiler_params=pltpu.CompilerParams(vmem_limit_bytes=44 * MIB),
        cost_estimate=CHEAP,
    )(rank_scalar(), x, cot, w_both, wd)


def gate_grad_kernel(order, rank_ref, x_ref, grad_ref, out_ref, xt_ref):
    rows = out_ref.shape[2]

    @pl.when(pl.program_id(0) == 0)
    def _():
        xt_ref[...] = x_ref[...].T

    result = dot_plain(xt_ref[...], grad_ref[...]).astype(BF)
    for index, (data, source) in enumerate(order):
        out_ref[data, source ^ rank_ref[0]] = result[index * rows : (index + 1) * rows]


def gate_grads(x, grads, shape):
    count, width = x.shape
    return pl.pallas_call(
        functools.partial(gate_grad_kernel, block_order()),
        grid_spec=pltpu.PrefetchScalarGridSpec(
            num_scalar_prefetch=1,
            grid=(grads.shape[1] // (2 * TILE),),
            in_specs=[
                pl.BlockSpec((count, width), lambda i, rank: (0, 0)),
                pl.BlockSpec((count, 2 * TILE), lambda i, rank: (0, i)),
            ],
            out_specs=pl.BlockSpec(shape[:3] + (2 * TILE,), lambda i, rank: (0, 0, 0, i)),
            scratch_shapes=[pltpu.VMEM((width, count), BF)],
        ),
        out_shape=jax.ShapeDtypeStruct(shape, BF),
        compiler_params=pltpu.CompilerParams(vmem_limit_bytes=VMEM_LIMIT),
        cost_estimate=CHEAP,
    )(rank_scalar(), x, grads)


def down_kernel(hid_ref, cot_ref, wd_ref, grad_ref, out_ref, acc_ref):
    step = pl.program_id(0)
    hidden = hid_ref[...]
    grad_ref[...] = dot_outer(hidden, cot_ref[...]).astype(BF)
    part = dot_plain(hidden, wd_ref[...])

    @pl.when(step == 0)
    def _():
        acc_ref[...] = part

    @pl.when(step > 0)
    def _():
        acc_ref[...] += part

    @pl.when(step == pl.num_programs(0) - 1)
    def _():
        out_ref[...] = acc_ref[...].astype(BF)


def down_grads(hidden, cot, wd):
    count, cols = hidden.shape
    width = wd.shape[1]
    tile = TILE
    whole = lambda i: (0, 0)
    return pl.pallas_call(
        down_kernel,
        grid=(cols // tile,),
        in_specs=[
            pl.BlockSpec((count, tile), lambda i: (0, i)),
            pl.BlockSpec((count, width), whole),
            pl.BlockSpec((tile, width), lambda i: (i, 0)),
        ],
        out_specs=[
            pl.BlockSpec((tile, width), lambda i: (i, 0)),
            pl.BlockSpec((count, width), whole),
        ],
        out_shape=[
            jax.ShapeDtypeStruct((cols, width), BF),
            jax.ShapeDtypeStruct((count, width), BF),
        ],
        scratch_shapes=[pltpu.VMEM((count, width), F32)],
        compiler_params=pltpu.CompilerParams(vmem_limit_bytes=VMEM_LIMIT),
        cost_estimate=CHEAP,
    )(hidden, cot, wd)


def per_device(
    inputs,
    cotangent,
    attn_gain,
    w_query,
    w_key,
    w_value,
    w_output,
    query_gain,
    key_gain,
    ffn_gain,
    w_gate,
    w_up,
    w_down,
    doc_starts,
):
    heads, mids = lax.axis_size("heads"), lax.axis_size("mid")
    his, los = lax.axis_size("hi"), lax.axis_size("lo")
    slots = heads * mids
    batches, _, rows, width = inputs.shape
    block = rows * heads
    count = slots * rows
    head_size = query_gain.shape[0]
    w_rows = w_query.shape[0]
    q_width = w_query.shape[1] // slots
    pairs = w_key.shape[1] // head_size // slots
    ff_width = w_gate.shape[1] // slots

    by_slot = lambda w: w.reshape(w_rows, slots, -1)
    kv_cols = jnp.stack(
        [
            w_key.reshape(w_rows, slots, pairs, head_size),
            w_value.reshape(w_rows, slots, pairs, head_size),
        ],
        axis=3,
    )
    qkv_parts = jnp.concatenate([by_slot(w_query), kv_cols.reshape(w_rows, slots, -1)], axis=2)
    qkv_mine = columns_out(qkv_parts.transpose(1, 0, 2))
    out_rows, down_rows = w_output.shape[0], w_down.shape[0]
    own_in, own_cot = inputs[:, 0], cotangent[:, 0]
    row_part = jnp.concatenate([w_output, w_down], axis=0)
    if is_quad():
        qkv_mine, own_in, row_part, doc_starts = together(qkv_mine, own_in, row_part, doc_starts)
        in_near = group_near(own_in)
    row_part = rows_out(row_part)
    qkv_all = gather_data(qkv_mine)
    fast = is_quad() and fast_rows(w_rows) and ff_width % TILE == 0

    head_at, mid_at = slot_places()
    row_at = jnp.arange(rows, dtype=jnp.int32)
    hi_at, lo_at = lax.axis_index("hi"), lax.axis_index("lo")
    first_pos = ((mid_at * los * block + head_at * rows)[:, None] + row_at[None, :]).reshape(count)
    row_pos = first_pos + hi_at * (mids * los * block) + lo_at * block
    lows = [lo_at] if los == 1 else [lo_at, 1 - lo_at]
    starts = doc_starts[:, None, :]
    row_begin = jnp.max(jnp.where(starts <= row_pos[None, :, None], starts, 0), axis=2)
    row_both = jnp.broadcast_to(row_pos[None], (batches, count))
    begin_low, begin_high = (
        jnp.min(row_begin, axis=1)[:, None],
        jnp.max(row_begin, axis=1)[:, None],
    )

    back = hi_at - jnp.arange(his, dtype=jnp.int32)[:, None]
    bases = back * (mids * los * block) + jnp.stack(lows)[None] * block
    key_low, key_high = (bases + jnp.min(first_pos))[:, None], (bases + jnp.max(first_pos))[:, None]
    none = (key_low > jnp.max(row_pos)) | (key_high < begin_low) | (back < 0)[:, None]
    full = (key_high <= jnp.min(row_pos)) & (key_low >= begin_high)
    codes = jnp.where(none, 0, jnp.where(full, 1, 2)).astype(jnp.int32)
    bases = bases.astype(jnp.int32)
    info_cols = jnp.stack([row_both, row_begin], axis=2)
    info_rows = jnp.stack([row_both, row_begin], axis=1)

    half = head_size // 2
    frequency = THETA ** (-(jnp.arange(half, dtype=F32) * 2.0 / head_size))
    turn_pos = (row_both - row_begin).reshape(batches, slots, rows).transpose(1, 0, 2)
    angles = turn_pos.reshape(-1).astype(F32)[:, None] * frequency[None, :]
    cos, sin = jnp.cos(angles), jnp.sin(angles)
    cos = jnp.concatenate([cos] * 4, axis=1)
    sin = jnp.concatenate([-sin, sin, -sin, sin], axis=1)
    q_gain = jnp.concatenate([query_gain, query_gain])[None]
    k_gain = jnp.concatenate([key_gain, key_gain])[None]

    if is_quad():
        *in_near, cos, sin, info_cols, info_rows, codes, bases = together(
            *in_near, cos, sin, info_cols, info_rows, codes, bases
        )
        in_far = group_far(*in_near)
        *in_far, qkv_all, row_part = together(*in_far, qkv_all, row_part)
        in_all, normed = group_joined(own_in, in_near, in_far, attn_gain)
    else:
        in_all = group_gather(own_in)
        in_wide = in_all.astype(F32)
        normed = (in_wide * rms_inverse(in_wide) * attn_gain).astype(BF)
    row_all = gather_data(row_part)
    w_qkv = natural_rows(qkv_all)
    normed = normed.reshape(-1, width)
    raw, query, kv = project(normed, w_qkv, cos, sin, q_gain, k_gain, q_width, head_size)
    query, w_gate, w_up = together(query, w_gate, w_up)
    if fast:
        gate_up_mine = jnp.stack(exchange_blocks(gate_up_blocks(w_gate, w_up)))
    else:
        gate_up_parts = jnp.concatenate([by_slot(w_gate), by_slot(w_up)], axis=2)
        gate_up_mine = columns_out(gate_up_parts.transpose(1, 0, 2))
    query = query.reshape(slots, batches, rows, q_width)
    moving = kv.reshape(slots, batches, rows, -1)
    kv_steps, state = [], ()
    for step in range(his):
        if step:
            moving = lax.ppermute(moving, "hi", [(i, i + 1) for i in range(step - 1, his - 1)])
            moving, *state = together(moving, *state)
        if step == his - 1:
            moving, gate_up_mine = together(moving, gate_up_mine)
            gate_up_all = gather_data(gate_up_mine)
        kv_steps.append([moving] if los == 1 else [moving, other_low(moving)])
        state = attend(
            codes[step],
            bases[step],
            query,
            kv_steps[step],
            info_cols,
            first_pos[None],
            tuple(state),
            step == his - 1,
            head_size,
        )
        state = list(state)
        if not is_quad():
            continue
        if step == 0:
            gate_up_mine, state[0], cot_own = together(gate_up_mine, state[0], own_cot)
            cot_near = group_near(cot_own)
        if step == 1:
            *cot_near, row_all, state[0] = together(*cot_near, row_all, state[0])
            cot_far = group_far(*cot_near)
            wo_part = row_all[:, :out_rows].reshape(-1, width)
            wd_use = row_all[:, out_rows:].reshape(-1, width)
            wo_near = group_near(wo_part)
        if step == 2:
            *cot_far, state[0] = together(*cot_far, state[0])
            *wo_near, wd_use, state[0] = together(*wo_near, wd_use, state[0])
            wo_far = group_far(*wo_near)
            cot_all = group_joined(cot_own, cot_near, cot_far)
        if step == 3:
            *wo_far, cot_all, state[1] = together(*wo_far, cot_all, state[1])
            wo_full = group_joined(wo_part, wo_near, wo_far)
    exact, attn, lse = state
    if not is_quad():
        cot_all = group_gather(own_cot)
        wo_full = group_gather(row_all[:, :out_rows].reshape(-1, width))
        wd_use = row_all[:, out_rows:].reshape(-1, width)
    wo_full = wo_full.reshape(-1, width)
    attn_wide = columns_out_async(attn.reshape(slots, batches * rows, q_width))
    attn_wide = jnp.concatenate([attn_wide[slot] for slot in range(slots)], axis=1)
    middle = own_in.reshape(-1, width).astype(F32) + dot_plain(attn_wide, wo_full)

    normed_two = (middle * rms_inverse(middle) * ffn_gain).astype(BF)
    normed_two_all = group_gather(normed_two).reshape(-1, width)
    normed_two_all, gate_up_all = together(normed_two_all, gate_up_all)
    cot_rows = cot_all.reshape(-1, width)
    if fast:
        hidden, grads, grad_two = feed(normed_two_all, cot_rows, gate_up_all, wd_use)
        grad_two, grads, hidden = together(grad_two, grads, hidden)
        grad_gate_up = gate_grads(normed_two_all, grads, gate_up_all.shape)
        grad_gate_up = grad_gate_up.reshape(his * los, slots * w_rows, -1)
        grad_down, out_part = down_grads(hidden, cot_rows, wd_use)
    else:
        w_both = natural_rows(gate_up_all)
        both = dot_plain(normed_two_all, w_both)
        gate, upper = both[:, :ff_width], both[:, ff_width:]
        grad_hidden = dot_back(cot_rows, wd_use)
        sigmoid = jax.nn.sigmoid(gate)
        silu = gate * sigmoid
        hidden = (silu * upper).astype(BF)
        grad_gate = grad_hidden * upper * sigmoid * (1.0 + gate * (1.0 - sigmoid))
        grads = jnp.concatenate([grad_gate, grad_hidden * silu], axis=1).astype(BF)
        grad_two = dot_back(grads, w_both).astype(BF)
        grad_gate_up = scatter_order(dot_outer(normed_two_all, grads).astype(BF), w_rows)
        grad_down = dot_outer(hidden, cot_rows).astype(BF)
        out_part = dot_plain(hidden, wd_use).astype(BF)
    in_slots = lambda total: total.reshape(slots, batches * rows, width)
    out_part = in_slots(out_part)
    two_sum = GroupSum(in_slots(grad_two))
    (grad_gate_up,) = two_sum.second(grad_gate_up)
    grad_down, out_part = two_sum.hold(grad_down, out_part)
    grad_two = two_sum.done()
    gate_up_sum = scatter_data(grad_gate_up).reshape(slots, w_rows, -1)
    grad_mid_part, _ = norm_back(middle, ffn_gain, grad_two)
    grad_middle = own_cot.reshape(-1, width).astype(F32) + grad_mid_part

    grad_middle_low = grad_middle.astype(BF)
    grad_attn = dot_back(grad_middle_low, wo_full).astype(BF)
    grad_attn = jnp.stack(
        [grad_attn[:, slot * q_width : (slot + 1) * q_width] for slot in range(slots)]
    )
    grad_attn, grad_middle_low = together(grad_attn, grad_middle_low)
    grad_output = dot_outer(attn_wide, grad_middle_low)
    grad_output = grad_output.astype(BF).reshape(slots, -1, width)
    grad_attn = columns_out_async(grad_attn).reshape(query.shape)
    first_sum = GroupSum(grad_output)
    state, moving = (), None
    for turn in range(1, his + 1):
        step = his - turn
        *dkv, state_out = attend_back(
            codes[step],
            bases[step],
            query,
            grad_attn,
            exact,
            lse,
            kv_steps[step],
            info_rows,
            first_pos[:, None],
            state,
            turn == his,
            head_size,
        )
        if turn > 1:
            *dkv, moving = together(*dkv, moving)
        if turn == 1:
            dkv = first_sum.second(*dkv)
        if turn == min(2, his):
            dkv = first_sum.hold(*dkv)
            out_part, *dkv = together(out_part, *dkv)
            second_sum = GroupSum(out_part)
        if turn == min(3, his):
            dkv = second_sum.second(*dkv)
            dkv = first_sum.hold(*dkv)
            output_part, gate_up_sum = together(first_sum.done().astype(BF), gate_up_sum)
            row_grads = jnp.concatenate(
                [
                    output_part.reshape(his * los, out_rows, width),
                    grad_down.reshape(his * los, down_rows, width),
                ],
                axis=1,
            )
        if turn == min(4, his):
            dkv = second_sum.hold(*dkv)
            row_sum = scatter_data(row_grads)
        parts = [dkv[0]] + ([other_low(dkv[1])] if los == 2 else [])
        parts += [moving] if turn > 1 else []
        if turn < his:
            low, state_out = together(low_sum(*parts), state_out)
            moving = lax.ppermute(low, "hi", [(i, i - 1) for i in range(his - turn, his)])
        state = (state_out,)
    out_sum = second_sum.done()
    dkv_mine = sum(part.astype(F32) for part in parts)
    dq = state[0]
    grad_raw, head_gains = unproject(
        raw,
        dq.reshape(-1, q_width),
        dkv_mine.reshape(raw.shape[0], -1),
        cos,
        sin,
        q_gain,
        k_gain,
        head_size,
    )
    block_out = (middle + out_sum).astype(BF)
    grad_qkv = dot_outer(normed, grad_raw).astype(BF)
    head_sums = jnp.sum(head_gains, axis=0).reshape(2, 2, head_size).sum(axis=1)
    in_wide = in_all.reshape(-1, width).astype(F32)
    normed_back = lambda grads: dot_back(grads, w_qkv).astype(BF)
    gain_vector = lambda low, grad_two, middle: jnp.concatenate(
        [
            jnp.sum(low.astype(F32) * in_wide * rms_inverse(in_wide), axis=0),
            jnp.sum(grad_two * middle * rms_inverse(middle), axis=0),
            head_sums[0],
            head_sums[1],
        ]
    )
    into_slots = lambda low: low.reshape(slots, batches * rows, width)
    if fast:
        own_part, other_part = unplaced(grad_qkv, w_rows, True)
        own_part, other_part, grad_raw = together(own_part, other_part, grad_raw)
        other_part = other_low(other_part)
        grad_normed_low = normed_back(grad_raw)
        other_part, grad_normed_low, gate_up_sum, grad_two, middle = together(
            other_part, grad_normed_low, gate_up_sum, grad_two, middle
        )
        summed = low_sum(own_part, other_part)
        normed_sum = GroupSum(into_slots(grad_normed_low))
        gains = gain_vector(grad_normed_low, grad_two, middle)
        stages = sum_stages()
        moving = None
        for step in range(1, his):
            moving = ring(summed[step] if moving is None else low_sum(summed[step], moving), 1)
            if step == 1:
                moving, gains = normed_sum.second(moving, gains)
                gate_up_back = exchange_blocks([gate_up_sum[slot] for slot in range(4)])
            else:
                gains = stages.pop(0)(gains)
                moving, gains = together(moving, gains)
            if step == his - 1:
                moving, gains = normed_sum.hold(moving, gains)
                moving, row_sum, *gate_up_back = together(moving, row_sum, *gate_up_back)
        qkv_sum = low_sum(summed[0], moving) if his > 1 else summed[0]
        qkv_cols, row_back = columns_out(qkv_sum), rows_back(row_sum)
        for stage in stages:
            gains = stage(gains)
        qkv_cols, row_back = together(qkv_cols, row_back)
    else:
        gate_up_back = [columns_out(gate_up_sum)]
        grad_qkv = scatter_order(grad_qkv, w_rows)
        qkv_cols = columns_out(scatter_data(grad_qkv).reshape(slots, w_rows, -1))
        grad_normed_low = normed_back(grad_raw)
        gains = all_sum(gain_vector(grad_normed_low, grad_two, middle))
        normed_sum = GroupSum(into_slots(grad_normed_low))
        normed_sum.second()
        row_back = rows_back(row_sum)
    grad_normed = normed_sum.done()
    row_back = row_back.astype(F32)
    grad_in_part, _ = norm_back(own_in.reshape(-1, width).astype(F32), attn_gain, grad_normed)
    grad_inputs = grad_middle + grad_in_part

    qkv_cols = qkv_cols.transpose(1, 0, 2).astype(F32)
    if fast:
        gate_cols, up_cols = gate_up_merge(gate_up_back)
    else:
        gate_cols, up_cols = jnp.split(gate_up_back[0].transpose(1, 0, 2).astype(F32), 2, axis=2)
    kv_sums = qkv_cols[:, :, q_width:].reshape(w_rows, slots, pairs, 2, head_size)
    return (
        block_out.reshape(batches, 1, rows, width),
        grad_inputs.reshape(batches, 1, rows, width),
        gains[:width],
        qkv_cols[:, :, :q_width].reshape(w_rows, -1),
        kv_sums[:, :, :, 0].reshape(w_rows, -1),
        kv_sums[:, :, :, 1].reshape(w_rows, -1),
        row_back[:out_rows],
        gains[2 * width : 2 * width + head_size],
        gains[2 * width + head_size :],
        gains[width : 2 * width],
        gate_cols.reshape(w_rows, -1),
        up_cols.reshape(w_rows, -1),
        row_back[out_rows:],
    )


def solution(mesh):
    heads, seq = mesh.shape["heads"], mesh.shape["seq"]
    rows_spec = P(None, SEQ, "heads", None)
    weight_spec = P(ALL, None)

    def run(*args):
        kv_heads = args[4].shape[1] // args[7].shape[0]
        low = 2 if seq % 2 == 0 else 1
        mid = 2 if seq % (2 * low) == 0 and kv_heads % (2 * heads) == 0 else 1
        split = Mesh(
            mesh.devices.reshape(heads, seq // (mid * low), mid, low), ("heads",) + SEQ
        )
        return jax.shard_map(
            per_device,
            mesh=split,
            in_specs=(
                (rows_spec, rows_spec, P())
                + (weight_spec,) * 4
                + (P(), P(), P())
                + (weight_spec,) * 3
                + (P(),)
            ),
            out_specs=(
                (rows_spec, rows_spec, P())
                + (weight_spec,) * 4
                + (P(), P(), P())
                + (weight_spec,) * 3
            ),
            check_vma=False,
        )(*args)

    return run
```

```python
import functools
import math

import jax
import jax.numpy as jnp
from jax import lax
from jax.experimental import pallas as pl
from jax.experimental.pallas import tpu as pltpu
from jax.sharding import Mesh, PartitionSpec as P

EPS = 1e-05
THETA = 1000000.0
LANES = 128
LOG2E = math.log2(math.e)
GROUP = ("heads", "mid")
DATA = ("hi", "lo")
SEQ = ("hi", "mid", "lo")
ALL = ("heads",) + SEQ
BF = jnp.bfloat16
F32 = jnp.float32
MIB = 1024 * 1024
VMEM_LIMIT = 48 * MIB
CHEAP = pl.CostEstimate(flops=1, bytes_accessed=1, transcendentals=0)
STEP = pl.CostEstimate(flops=1, bytes_accessed=1, transcendentals=0)


def dot_plain(left_side, right_side):
    return jnp.dot(left_side, right_side, preferred_element_type=F32)


def dot_back(left_side, right_side):
    return lax.dot_general(
        left_side, right_side, (((1,), (1,)), ((), ())), preferred_element_type=F32
    )


def dot_outer(left_side, right_side):
    return lax.dot_general(
        left_side, right_side, (((0,), (0,)), ((), ())), preferred_element_type=F32
    )


def together(*values):
    return lax.optimization_barrier(values)


def rms_inverse(values):
    return lax.rsqrt(jnp.mean(values * values, axis=-1, keepdims=True) + EPS)


def norm_back(values, gain_vec, upstream):
    inverse = rms_inverse(values)
    scaled = upstream * gain_vec
    inner_mean = jnp.mean(scaled * values, axis=-1, keepdims=True)
    grad_values = inverse * scaled - values * inverse * inverse * inverse * inner_mean
    return (grad_values, upstream * values * inverse)


def is_quad():
    return lax.axis_size("heads") == 2 and lax.axis_size("mid") == 2


def swap(part, axis):
    return lax.ppermute(part, axis, [(0, 1), (1, 0)])


def group_rank():
    return lax.axis_index("heads") * lax.axis_size("mid") + lax.axis_index("mid")


def block_at(parts, index):
    return lax.dynamic_index_in_dim(parts, index, axis=0, keepdims=False)


def in_order(blocks):
    rank = group_rank()
    total = jnp.zeros((4,) + blocks[0].shape, blocks[0].dtype)
    for slot, block in enumerate(blocks):
        total = lax.dynamic_update_index_in_dim(total, block, rank ^ slot, axis=0)
    return total


def group_near(part):
    return swap(part, "mid"), swap(part, "heads")


def group_far(by_mid, by_heads):
    half = by_mid.shape[0] // 2
    return swap(by_mid[:half], "heads"), swap(by_heads[half:], "mid")


def join_kernel(rank_ref, gain_ref, own_ref, mid_ref, head_ref, low_ref, high_ref, out_ref, *normed_ref):
    source = pl.program_id(0) ^ rank_ref[0]
    half = low_ref.shape[0]
    for slot, ref in enumerate((own_ref, mid_ref, head_ref)):

        @pl.when(source == slot)
        def _(ref=ref):
            out_ref[0] = ref[...]

    @pl.when(source == 3)
    def _():
        out_ref[0, :half] = low_ref[...]
        out_ref[0, half:] = high_ref[...]

    if normed_ref:
        values = out_ref[0].astype(F32)
        normed_ref[0][0] = (values * rms_inverse(values) * gain_ref[...]).astype(BF)


def group_joined(part, near, far, gain=None):
    width = part.shape[-1]
    flat = [block.reshape(-1, width) for block in (part, *near, *far)]
    whole = lambda i, rank: (0, 0)
    shape = (4,) + flat[0].shape
    outs = 1 if gain is None else 2
    out_spec = pl.BlockSpec((1,) + flat[0].shape, lambda i, rank: (i, 0, 0))
    gain_vec = jnp.zeros((1, width), F32) if gain is None else gain[None]
    result = pl.pallas_call(
        join_kernel,
        grid_spec=pltpu.PrefetchScalarGridSpec(
            num_scalar_prefetch=1,
            grid=(4,),
            in_specs=[pl.BlockSpec((1, width), whole)]
            + [pl.BlockSpec(block.shape, whole) for block in flat],
            out_specs=[out_spec] * outs,
        ),
        out_shape=[jax.ShapeDtypeStruct(shape, part.dtype)] * outs,
        compiler_params=pltpu.CompilerParams(vmem_limit_bytes=10 * MIB),
        cost_estimate=CHEAP,
    )(group_rank()[None].astype(jnp.int32), gain_vec, *flat)
    total = result[0].reshape((4,) + part.shape)
    return total if gain is None else (total, result[1].reshape(total.shape))


def group_gather(part):
    if not is_quad():
        return lax.all_gather(part, GROUP, axis=0, tiled=False)
    near = group_near(part)
    return group_joined(part, near, group_far(*near))


def group_gather_plain(part):
    return lax.all_gather(part, GROUP, axis=0, tiled=False)


def group_sum_plain(parts):
    flat = parts.reshape((-1,) + parts.shape[2:])
    return lax.psum_scatter(flat, GROUP, scatter_dimension=0, tiled=True)


class GroupSum:
    def __init__(self, parts):
        if is_quad():
            rank = group_rank()
            self.parts = [block_at(parts, rank ^ slot) for slot in range(4)]
            half = parts.shape[1] // 2
            far = self.parts[3]
            self.far = (swap(far[:half], "mid"), swap(far[half:], "heads"))
        else:
            self.total = group_sum_plain(parts)

    def second(self, *between):
        if is_quad():
            _, mid, head, _ = self.parts
            half = mid.shape[0] // 2
            far_low, far_high = self.far
            if between:
                far_low, far_high, *between = together(far_low, far_high, *between)
            for_mid = jnp.concatenate([mid[:half], low_sum(mid[half:], far_high)], axis=0)
            for_heads = jnp.concatenate([low_sum(head[:half], far_low), head[half:]], axis=0)
            self.near = (swap(for_mid, "mid"), swap(for_heads, "heads"))
        return between

    def hold(self, *later):
        if is_quad():
            near_mid, near_heads, *later = together(*self.near, *later)
            self.near = (near_mid, near_heads)
        return later

    def done(self):
        if not is_quad():
            return self.total.astype(F32)
        return self.parts[0].astype(F32) + self.near[0].astype(F32) + self.near[1].astype(F32)


def slot_places():
    mids = lax.axis_size("mid")
    slots = jnp.arange(lax.axis_size("heads") * mids, dtype=jnp.int32)
    return (slots // mids, slots % mids)


def sum_stages():
    def along_hi(vector):
        size = lax.axis_size("hi")
        parts = [vector]
        for shift in range(1, size):
            parts.append(lax.ppermute(vector, "hi", [(i, (i + shift) % size) for i in range(size)]))
        return sum(parts[1:], parts[0])

    def along_low(vector):
        return vector + swap(vector, "lo")

    def along_group(vector):
        far = [(0, 3), (1, 2), (2, 1), (3, 0)]
        near = swap(vector, "mid") + swap(vector, "heads")
        return vector + near + lax.ppermute(vector, GROUP, far)

    return [along_hi, along_low, along_group]


def all_sum(vector):
    for axis in ("lo", "mid", "heads", "hi"):
        size = lax.axis_size(axis)
        if size & (size - 1):
            vector = lax.psum(vector, axis)
            continue
        step = 1
        while step < size:
            vector = vector + lax.ppermute(vector, axis, [(i, i ^ step) for i in range(size)])
            step *= 2
    return vector


def columns_out(parts):
    return lax.all_to_all(parts, GROUP, split_axis=0, concat_axis=0, tiled=True)


def columns_out_async(parts):
    if not is_quad():
        return columns_out(parts)
    rank = group_rank()
    far = [(0, 3), (1, 2), (2, 1), (3, 0)]
    return in_order(
        [
            block_at(parts, rank),
            swap(block_at(parts, rank ^ 1), "mid"),
            swap(block_at(parts, rank ^ 2), "heads"),
            lax.ppermute(block_at(parts, rank ^ 3), GROUP, far),
        ]
    )


def ring(part, shift):
    size = lax.axis_size("hi")
    return lax.ppermute(part, "hi", [(i, (i + shift) % size) for i in range(size)])


def other_low(part):
    return swap(part, "lo")


def fast_rows(rows):
    return lax.axis_size("lo") == 2 and rows % 16 == 0


def data_ring(part):
    own = [part]
    for _ in range(lax.axis_size("hi") - 1):
        own.append(ring(own[-1], 1))
    return own, [other_low(piece) for piece in own]


def place_index():
    return jnp.stack(
        [lax.axis_index("hi"), lax.axis_index("lo"), lax.axis_index("heads"), lax.axis_index("mid")]
    ).astype(jnp.int32)


def block_row(at_ref, sizes, step, other, source):
    his, los, heads, mids = sizes
    hi = lax.rem(at_ref[0] - step + his, his)
    low = 1 - at_ref[1] if other else at_ref[1]
    if source is None:
        return hi * los + low
    return ((source // mids * his + hi) * mids + source % mids) * los + low


def split_sizes():
    return tuple(lax.axis_size(name) for name in ("hi", "lo", "heads", "mid"))


def place_kernel(sizes, sources, rows, at_ref, *refs):
    his = sizes[0]
    pieces, out_ref, sems = refs[: 2 * his], refs[2 * his], refs[2 * his + 1]
    copies = []
    for step in range(his):
        for other in range(2):
            for source in sources:
                first = block_row(at_ref, sizes, step, other, source) * rows
                piece = pieces[step + other * his]
                copies.append(
                    pltpu.make_async_copy(
                        piece if source is None else piece.at[source],
                        out_ref.at[pl.ds(pl.multiple_of(first, rows), rows)],
                        sems.at[len(copies)],
                    )
                )
    for copy in copies:
        copy.start()
    for copy in copies:
        copy.wait()


def placed(own, other):
    sizes = split_sizes()
    first = own[0]
    rows, cols = first.shape[-2:]
    sources = range(first.shape[0]) if first.ndim == 3 else (None,)
    total = rows * sizes[0] * sizes[1] * len(sources)
    anywhere = pl.BlockSpec(memory_space=pl.ANY)
    return pl.pallas_call(
        functools.partial(place_kernel, sizes, sources, rows),
        in_specs=[pl.BlockSpec(memory_space=pltpu.SMEM)] + [anywhere] * (2 * sizes[0]),
        out_specs=pl.BlockSpec(memory_space=pltpu.VMEM),
        out_shape=jax.ShapeDtypeStruct((total, cols), first.dtype),
        scratch_shapes=[pltpu.SemaphoreType.DMA((2 * sizes[0] * len(sources),))],
        compiler_params=pltpu.CompilerParams(vmem_limit_bytes=8 * MIB),
        cost_estimate=CHEAP,
    )(place_index(), *own, *other)


def unplace_kernel(sizes, sources, rows, at_ref, full_ref, own_ref, other_ref, sems):
    his = sizes[0]
    copies = []
    for step in range(his):
        for other in range(2):
            for source in sources:
                first = block_row(at_ref, sizes, step, other, source) * rows
                target = (other_ref if other else own_ref).at[step]
                copies.append(
                    pltpu.make_async_copy(
                        full_ref.at[pl.ds(pl.multiple_of(first, rows), rows)],
                        target if source is None else target.at[source],
                        sems.at[len(copies)],
                    )
                )
    for copy in copies:
        copy.start()
    for copy in copies:
        copy.wait()


def unplaced(full, rows, by_source):
    sizes = split_sizes()
    cols = full.shape[1]
    slots = sizes[2] * sizes[3]
    sources = range(slots) if by_source else (None,)
    shape = (sizes[0],) + ((slots,) if by_source else ()) + (rows, cols)
    anywhere = pl.BlockSpec(memory_space=pl.ANY)
    return pl.pallas_call(
        functools.partial(unplace_kernel, sizes, sources, rows),
        in_specs=[pl.BlockSpec(memory_space=pltpu.SMEM), pl.BlockSpec(memory_space=pltpu.VMEM)],
        out_specs=[anywhere, anywhere],
        out_shape=[jax.ShapeDtypeStruct(shape, full.dtype)] * 2,
        scratch_shapes=[pltpu.SemaphoreType.DMA((2 * sizes[0] * len(sources),))],
        compiler_params=pltpu.CompilerParams(vmem_limit_bytes=8 * MIB),
        cost_estimate=CHEAP,
    )(place_index(), full)


def natural_rows(gathered):
    his, los, heads, mids = split_sizes()
    rows, cols = gathered.shape[2:]
    parts = gathered.reshape(his, los, heads, mids, rows, cols)
    return parts.transpose(2, 0, 3, 1, 4, 5).reshape(-1, cols)


def gather_data(part):
    return lax.all_gather(part, DATA, axis=0, tiled=False)


def gather_rows(part):
    if fast_rows(part.shape[-2]):
        return placed(*data_ring(part))
    return natural_rows(gather_data(part))


def low_sum(*parts):
    total = parts[0].astype(F32)
    for part in parts[1:]:
        total = total + part.astype(F32)
    return total.astype(BF)


def scatter_data(parts):
    return lax.psum_scatter(parts, DATA, scatter_dimension=0, tiled=False)


def scatter_order(grads, rows):
    his, los, heads, mids = split_sizes()
    cols = grads.shape[1]
    parts = grads.reshape(heads, his, mids, los, rows, cols).transpose(1, 3, 0, 2, 4, 5)
    return parts.reshape(his * los, heads * mids * rows, cols)


def scatter_ring(summed):
    moving = None
    for step in range(1, lax.axis_size("hi")):
        part = summed[step]
        moving = ring(part if moving is None else low_sum(part, moving), 1)
    return summed[0] if moving is None else low_sum(summed[0], moving)


def row_moves():
    mids, los = lax.axis_size("mid"), lax.axis_size("lo")
    count = lax.axis_size("hi") * mids * los
    share = count // mids
    moves = []
    for source in range(count):
        owner, rest = source // share, source % share
        moves.append((source, ((rest // los) * mids + owner) * los + rest % los))
    return moves


def rows_out(part):
    return lax.ppermute(part, SEQ, row_moves())


def rows_back(part):
    return lax.ppermute(part, SEQ, [(there, here) for here, there in row_moves()])


def lane_index(shape):
    return lax.broadcasted_iota(jnp.int32, shape, len(shape) - 1)


def half_sums(values, lane, head_size):
    first = jnp.sum(jnp.where(lane < head_size, values, 0.0), axis=-1, keepdims=True)
    second = jnp.sum(jnp.where(lane < head_size, 0.0, values), axis=-1, keepdims=True)
    return jnp.where(lane < head_size, first, second)


def partner(values, lane, head_size):
    quarter = head_size // 2
    return jnp.where(
        lane % head_size < quarter,
        pltpu.roll(values, LANES - quarter, 1),
        pltpu.roll(values, quarter, 1),
    )


def project_kernel(
    head_size, normed_ref, w_ref, cos_ref, sin_ref, qgain_ref, kgain_ref, raw_ref, q_ref, kv_ref
):
    raw = dot_plain(normed_ref[...], w_ref[...])
    raw_ref[...] = raw
    cos, sin = cos_ref[...], sin_ref[...]
    lane = lane_index(cos.shape)
    q_width = q_ref.shape[1]
    for at in range(0, raw.shape[1], LANES):
        part = raw[:, at : at + LANES]
        is_query = at < q_width
        inverse = lax.rsqrt(half_sums(part * part, lane, head_size) / head_size + EPS)
        scaled = part * inverse * (qgain_ref[...] if is_query else kgain_ref[...])
        turned = scaled * cos + partner(scaled, lane, head_size) * sin
        if is_query:
            q_ref[:, at : at + LANES] = turned.astype(BF)
        else:
            out_at = at - q_width
            kv_ref[:, out_at : out_at + LANES] = jnp.where(lane < head_size, turned, part).astype(BF)


def project(normed, w_qkv, cos, sin, query_gain, key_gain, q_width, head_size):
    rows, width = normed.shape
    cols = w_qkv.shape[1]
    tile = 512
    whole = lambda i: (0, 0)
    step = lambda i: (i, 0)
    return pl.pallas_call(
        functools.partial(project_kernel, head_size),
        grid=(rows // tile,),
        in_specs=[
            pl.BlockSpec((tile, width), step),
            pl.BlockSpec((width, cols), whole),
            pl.BlockSpec((tile, LANES), step),
            pl.BlockSpec((tile, LANES), step),
            pl.BlockSpec((1, LANES), whole),
            pl.BlockSpec((1, LANES), whole),
        ],
        out_specs=[
            pl.BlockSpec((tile, cols), step),
            pl.BlockSpec((tile, q_width), step),
            pl.BlockSpec((tile, cols - q_width), step),
        ],
        out_shape=[
            jax.ShapeDtypeStruct((rows, cols), F32),
            jax.ShapeDtypeStruct((rows, q_width), BF),
            jax.ShapeDtypeStruct((rows, cols - q_width), BF),
        ],
        compiler_params=pltpu.CompilerParams(vmem_limit_bytes=24 * MIB),
        cost_estimate=CHEAP,
    )(normed, w_qkv, cos, sin, query_gain, key_gain)


def unproject_kernel(
    head_size, raw_ref, dq_ref, dkv_ref, cos_ref, sin_ref, qgain_ref, kgain_ref, out_ref, gain_ref
):
    cos, sin = cos_ref[...], sin_ref[...]
    lane = lane_index(cos.shape)
    q_width = dq_ref.shape[1]
    totals = [jnp.zeros((1, LANES), F32), jnp.zeros((1, LANES), F32)]
    for at in range(0, raw_ref.shape[1], LANES):
        part = raw_ref[:, at : at + LANES]
        is_query = at < q_width
        if is_query:
            upstream = dq_ref[:, at : at + LANES]
            gain = qgain_ref[...]
        else:
            upstream = dkv_ref[:, at - q_width : at - q_width + LANES].astype(F32)
            gain = kgain_ref[...]
        turned = upstream * cos - partner(upstream, lane, head_size) * sin
        inverse = lax.rsqrt(half_sums(part * part, lane, head_size) / head_size + EPS)
        scaled = turned * gain
        inner = half_sums(scaled * part, lane, head_size) / head_size
        grad = inverse * scaled - part * inverse * inverse * inverse * inner
        gain_part = jnp.sum(turned * part * inverse, axis=0, keepdims=True)
        if not is_query:
            grad = jnp.where(lane < head_size, grad, upstream)
            gain_part = jnp.where(lane[:1] < head_size, gain_part, 0.0)
        totals[0 if is_query else 1] += gain_part
        out_ref[:, at : at + LANES] = grad.astype(BF)
    gain_ref[0] = jnp.concatenate(totals, axis=0)


def unproject(raw, dq, dkv, cos, sin, query_gain, key_gain, head_size):
    rows, cols = raw.shape
    q_width = dq.shape[1]
    tile = 512
    whole = lambda i: (0, 0)
    step = lambda i: (i, 0)
    return pl.pallas_call(
        functools.partial(unproject_kernel, head_size),
        grid=(rows // tile,),
        in_specs=[
            pl.BlockSpec((tile, cols), step),
            pl.BlockSpec((tile, q_width), step),
            pl.BlockSpec((tile, cols - q_width), step),
            pl.BlockSpec((tile, LANES), step),
            pl.BlockSpec((tile, LANES), step),
            pl.BlockSpec((1, LANES), whole),
            pl.BlockSpec((1, LANES), whole),
        ],
        out_specs=[
            pl.BlockSpec((tile, cols), step),
            pl.BlockSpec((1, 2, LANES), lambda i: (i, 0, 0)),
        ],
        out_shape=[
            jax.ShapeDtypeStruct((rows, cols), BF),
            jax.ShapeDtypeStruct((rows // tile, 2, LANES), F32),
        ],
        compiler_params=pltpu.CompilerParams(vmem_limit_bytes=24 * MIB),
        cost_estimate=CHEAP,
    )(raw, dq, dkv, cos, sin, query_gain, key_gain)


def head_parts(pair, lane, head_size):
    return (
        jnp.where(lane < head_size, pair, 0.0).astype(BF),
        jnp.where(lane < head_size, pltpu.roll(pair, head_size, 1), 0.0).astype(BF),
    )


def attend_kernel(head_size, lows, first, last, code_ref, base_ref, q_ref, row_ref, key_ref, *refs):
    kv_refs, refs = refs[:lows], refs[lows:]
    if not first:
        (acc_in, sum_in), refs = refs[:2], refs[2:]
    if last:
        exact_ref, low_ref, lse_ref, qs_ref, acc_ref, sum_ref = refs
    else:
        acc_out, sum_out, qs_ref, acc_ref, sum_ref = refs
    batch = pl.program_id(0)
    count = row_ref.shape[1]
    factor = LOG2E * head_size**-0.5
    lane = lane_index((count, LANES))
    some = functools.reduce(jnp.maximum, [code_ref[batch, low] for low in range(lows)]) > 0

    @pl.when(some)
    def _():
        both = q_ref[:, 0].reshape(count, LANES).astype(F32)
        qs_ref[0], qs_ref[1] = head_parts(both, lane, head_size)

    if first:
        acc_ref[...] = jnp.zeros_like(acc_ref)
        sum_ref[...] = jnp.zeros_like(sum_ref)
    else:
        acc_ref[...] = acc_in[0, 0]
        sum_ref[...] = sum_in[0, 0]

    def one(low, masked):
        keys = kv_refs[low][:, 0].reshape(count, LANES)
        if masked:
            key_pos = key_ref[...] + base_ref[low]
            allowed = (key_pos <= row_ref[0, :, 0:1]) & (key_pos >= row_ref[0, :, 1:2])
        for head in range(2):
            exps = jnp.exp2(dot_back(qs_ref[head], keys) * factor)
            if masked:
                exps = jnp.where(allowed, exps, 0.0)
            partial = exps[:, :LANES]
            for lane_at in range(LANES, count, LANES):
                partial = partial + exps[:, lane_at : lane_at + LANES]
            sum_ref[head] += partial
            acc_ref[head] += dot_plain(exps.astype(BF), keys)

    for low in range(lows):
        code = code_ref[batch, low]
        pl.when(code == 1)(functools.partial(one, low, False))
        pl.when(code == 2)(functools.partial(one, low, True))

    if not last:
        acc_out[0, 0] = acc_ref[...]
        sum_out[0, 0] = sum_ref[...]
        return
    results = []
    for head in range(2):
        total = jnp.sum(sum_ref[head], axis=-1, keepdims=True)
        results.append(acc_ref[head] / total)
        wide = jnp.broadcast_to(jnp.log2(total), (count, LANES))
        lse_ref[0, 0, head] = wide.T[:8]
    joined = jnp.where(lane < head_size, pltpu.roll(results[0], head_size, 1), results[1])
    joined = joined.reshape(exact_ref.shape[0], -1, LANES)
    exact_ref[:, 0] = joined
    low_ref[:, 0] = joined.astype(BF)


def attend(codes, bases, query, kvs, row_info, key_pos, state, last, head_size):
    slots, batches, rows, q_width = query.shape
    count = slots * rows
    pairs = q_width // LANES
    pick = lambda b, p, *_: (0, b, 0, p)
    by_pair = lambda b, p, *_: (b, p, 0, 0, 0)
    slab = pl.BlockSpec((slots, 1, rows, LANES), pick)
    wide = pl.BlockSpec((1, 1, 2, count, LANES), by_pair)
    wide_shape = jax.ShapeDtypeStruct((batches, pairs, 2, count, LANES), F32)
    if last:
        out_specs = [slab, slab, pl.BlockSpec((1, 1, 2, 8, count), by_pair)]
        out_shape = [
            jax.ShapeDtypeStruct(query.shape, F32),
            jax.ShapeDtypeStruct(query.shape, BF),
            jax.ShapeDtypeStruct((batches, pairs, 2, 8, count), F32),
        ]
    else:
        out_specs, out_shape = [wide, wide], [wide_shape, wide_shape]
    return pl.pallas_call(
        functools.partial(attend_kernel, head_size, len(kvs), not state, last),
        grid_spec=pltpu.PrefetchScalarGridSpec(
            num_scalar_prefetch=2,
            grid=(batches, pairs),
            in_specs=[
                slab,
                pl.BlockSpec((1, count, 2), lambda b, p, *_: (b, 0, 0)),
                pl.BlockSpec((1, count), lambda b, p, *_: (0, 0)),
            ]
            + [slab] * len(kvs)
            + [wide] * len(state),
            out_specs=out_specs,
            scratch_shapes=[
                pltpu.VMEM((2, count, LANES), BF),
                pltpu.VMEM((2, count, LANES), F32),
                pltpu.VMEM((2, count, LANES), F32),
            ],
        ),
        out_shape=out_shape,
        compiler_params=pltpu.CompilerParams(vmem_limit_bytes=VMEM_LIMIT if count > 512 else 32 * MIB),
        cost_estimate=STEP,
    )(codes, bases, query, row_info, key_pos, *kvs, *state)


def attend_back_kernel(
    head_size,
    lows,
    first,
    last,
    code_ref,
    base_ref,
    q_ref,
    up_ref,
    exact_ref,
    lse_ref,
    row_ref,
    key_ref,
    *refs,
):
    kv_refs, refs = refs[:lows], refs[lows:]
    if not first:
        acc_in, refs = refs[0], refs[1:]
    dkv_refs, refs = refs[:lows], refs[lows:]
    out_ref, qs_ref, us_ref, acc_ref, delta_ref = refs
    batch = pl.program_id(0)
    count = row_ref.shape[2]
    scale = head_size**-0.5
    factor = LOG2E * scale
    lane = lane_index((count, LANES))
    some = functools.reduce(jnp.maximum, [code_ref[batch, low] for low in range(lows)]) > 0

    @pl.when(some)
    def _():
        both = q_ref[:, 0].reshape(count, LANES).astype(F32)
        qs_ref[0], qs_ref[1] = head_parts(both, lane, head_size)
        upper = up_ref[:, 0].reshape(count, LANES).astype(F32)
        us_ref[0] = jnp.where(lane < head_size, 0.0, pltpu.roll(upper, head_size, 1)).astype(BF)
        us_ref[1] = jnp.where(lane < head_size, 0.0, upper).astype(BF)
        products = upper * exact_ref[:, 0].reshape(count, LANES)
        for head in range(2):
            inside = (lane < head_size) if head == 0 else (lane >= head_size)
            total = jnp.sum(jnp.where(inside, products, 0.0), axis=-1, keepdims=True)
            delta_ref[head] = jnp.broadcast_to(total, (count, LANES)).T[:8]

    acc_ref[...] = jnp.zeros_like(acc_ref) if first else acc_in[0, 0]

    def none(low):
        dkv_refs[low][:, 0] = jnp.zeros((kv_refs[low].shape[0],) + kv_refs[low].shape[2:], BF)

    def one(low, masked):
        keys = kv_refs[low][:, 0].reshape(count, LANES)
        if masked:
            key_pos = key_ref[...] + base_ref[low]
            allowed = (key_pos <= row_ref[0, 0:1]) & (key_pos >= row_ref[0, 1:2])
        grad_kv = jnp.zeros((count, LANES), F32)
        for head in range(2):
            scores = dot_back(keys, qs_ref[head]) * factor
            probs = jnp.exp2(scores - lse_ref[0, 0, head, 0:1])
            if masked:
                probs = jnp.where(allowed, probs, 0.0)
            grads = dot_back(keys, us_ref[head])
            grads = (probs * (grads - delta_ref[head, 0:1])).astype(BF)
            grad_kv += dot_plain(probs.astype(BF), us_ref[head])
            grad_kv += dot_plain(grads, qs_ref[head]) * scale
            acc_ref[head] += dot_outer(grads, keys)
        dkv_refs[low][:, 0] = grad_kv.astype(BF).reshape(kv_refs[low].shape[0], -1, LANES)

    for low in range(lows):
        code = code_ref[batch, low]
        pl.when(code == 0)(functools.partial(none, low))
        pl.when(code == 1)(functools.partial(one, low, False))
        pl.when(code == 2)(functools.partial(one, low, True))

    if not last:
        out_ref[0, 0] = acc_ref[...]
        return
    joined = jnp.where(lane < head_size, acc_ref[0], pltpu.roll(acc_ref[1], head_size, 1))
    out_ref[:, 0] = (joined * scale).reshape(out_ref.shape[0], -1, LANES)


def attend_back(codes, bases, query, upstream, exact, lse, kvs, row_info, key_pos, state, last, head_size):
    slots, batches, rows, q_width = query.shape
    count = slots * rows
    pairs = q_width // LANES
    pick = lambda b, p, *_: (0, b, 0, p)
    by_pair = lambda b, p, *_: (b, p, 0, 0, 0)
    slab = pl.BlockSpec((slots, 1, rows, LANES), pick)
    wide = pl.BlockSpec((1, 1, 2, count, LANES), by_pair)
    wide_shape = jax.ShapeDtypeStruct((batches, pairs, 2, count, LANES), F32)
    return pl.pallas_call(
        functools.partial(attend_back_kernel, head_size, len(kvs), not state, last),
        grid_spec=pltpu.PrefetchScalarGridSpec(
            num_scalar_prefetch=2,
            grid=(batches, pairs),
            in_specs=[
                slab,
                slab,
                slab,
                pl.BlockSpec((1, 1, 2, 8, count), by_pair),
                pl.BlockSpec((1, 2, count), lambda b, p, *_: (b, 0, 0)),
                pl.BlockSpec((count, 1), lambda b, p, *_: (0, 0)),
            ]
            + [slab] * len(kvs)
            + [wide] * len(state),
            out_specs=[slab] * len(kvs) + [slab if last else wide],
            scratch_shapes=[
                pltpu.VMEM((2, count, LANES), BF),
                pltpu.VMEM((2, count, LANES), BF),
                pltpu.VMEM((2, count, LANES), F32),
                pltpu.VMEM((2, 8, count), F32),
            ],
        ),
        out_shape=[jax.ShapeDtypeStruct(kvs[0].shape, BF)] * len(kvs)
        + [jax.ShapeDtypeStruct(query.shape, F32) if last else wide_shape],
        compiler_params=pltpu.CompilerParams(vmem_limit_bytes=VMEM_LIMIT if count > 512 else 22 * MIB),
        cost_estimate=STEP,
    )(codes, bases, query, upstream, exact, lse, row_info, key_pos, *kvs, *state)


TILE = 384


def block_order():
    his, los, heads, mids = split_sizes()
    return tuple(
        (hi * los + lo, head * mids + mid)
        for head in range(heads)
        for hi in range(his)
        for mid in range(mids)
        for lo in range(los)
    )


def split_kernel(rank_ref, *refs):
    for slot in range(4):
        gate_ref, up_ref, out_ref = refs[slot], refs[4 + slot], refs[8 + slot]
        for at in range(0, gate_ref.shape[1], TILE):
            out_ref[:, 2 * at : 2 * at + TILE] = gate_ref[:, at : at + TILE]
            out_ref[:, 2 * at + TILE : 2 * at + 2 * TILE] = up_ref[:, at : at + TILE]


def rank_scalar():
    return group_rank()[None].astype(jnp.int32)


def gate_up_blocks(w_gate, w_up):
    rows, cols = w_gate.shape
    part = cols // 4
    picks = [
        pl.BlockSpec((rows, part), lambda i, rank, slot=slot: (0, rank[0] ^ slot)) for slot in range(4)
    ]
    return pl.pallas_call(
        split_kernel,
        grid_spec=pltpu.PrefetchScalarGridSpec(
            num_scalar_prefetch=1,
            grid=(1,),
            in_specs=picks + picks,
            out_specs=[pl.BlockSpec((rows, 2 * part), lambda i, rank: (0, 0))] * 4,
        ),
        out_shape=[jax.ShapeDtypeStruct((rows, 2 * part), w_gate.dtype)] * 4,
        compiler_params=pltpu.CompilerParams(vmem_limit_bytes=6 * MIB),
        cost_estimate=CHEAP,
    )(rank_scalar(), *[w_gate] * 4, *[w_up] * 4)


def merge_kernel(rank_ref, *refs):
    source = pl.program_id(0) ^ rank_ref[0]
    gate_ref, up_ref = refs[4:]
    for slot in range(4):

        @pl.when(source == slot)
        def _(ref=refs[slot]):
            for at in range(0, gate_ref.shape[1], TILE):
                gate_ref[:, at : at + TILE] = ref[:, 2 * at : 2 * at + TILE].astype(F32)
                up_ref[:, at : at + TILE] = ref[:, 2 * at + TILE : 2 * at + 2 * TILE].astype(F32)


def gate_up_merge(blocks):
    rows, both = blocks[0].shape
    column = pl.BlockSpec((rows, both // 2), lambda i, rank: (0, i))
    return pl.pallas_call(
        merge_kernel,
        grid_spec=pltpu.PrefetchScalarGridSpec(
            num_scalar_prefetch=1,
            grid=(4,),
            in_specs=[pl.BlockSpec((rows, both), lambda i, rank: (0, 0))] * 4,
            out_specs=[column, column],
        ),
        out_shape=[jax.ShapeDtypeStruct((rows, 2 * both), F32)] * 2,
        compiler_params=pltpu.CompilerParams(vmem_limit_bytes=6 * MIB),
        cost_estimate=CHEAP,
    )(rank_scalar(), *blocks)


def exchange_blocks(blocks):
    far = [(0, 3), (1, 2), (2, 1), (3, 0)]
    return [
        blocks[0],
        swap(blocks[1], "mid"),
        swap(blocks[2], "heads"),
        lax.ppermute(blocks[3], GROUP, far),
    ]


def feed_kernel(order, rank_ref, x_ref, cot_ref, w_ref, wd_ref, hid_ref, grad_ref, two_ref, w_all, acc_ref):
    rows = w_ref.shape[2]
    for index, (data, source) in enumerate(order):
        w_all[pl.ds(index * rows, rows)] = w_ref[data, source ^ rank_ref[0]]
    step = pl.program_id(0)
    count = x_ref.shape[0]
    part = math.gcd(count, 512)

    @pl.when(step == 0)
    def _():
        acc_ref[...] = jnp.zeros_like(acc_ref)

    for first in range(0, count, part):
        at = pl.ds(first, part)
        both = dot_plain(x_ref[at], w_all[...])
        gate, upper = both[:, :TILE], both[:, TILE:]
        grad_hidden = dot_back(cot_ref[at], wd_ref[...])
        sigmoid = jax.nn.sigmoid(gate)
        silu = gate * sigmoid
        hid_ref[at] = (silu * upper).astype(BF)
        grad_gate = (grad_hidden * upper * sigmoid * (1.0 + gate * (1.0 - sigmoid))).astype(BF)
        grad_upper = (grad_hidden * silu).astype(BF)
        grads = jnp.concatenate([grad_gate, grad_upper], axis=1)
        grad_ref[at] = grads
        acc_ref[at] += dot_back(grads, w_all[...])

    @pl.when(step == pl.num_programs(0) - 1)
    def _():
        two_ref[...] = acc_ref[...].astype(BF)


def feed(x, cot, w_both, wd):
    count, width = x.shape
    cols = wd.shape[0]
    whole = lambda i, rank: (0, 0)
    column = lambda i, rank: (0, i)
    return pl.pallas_call(
        functools.partial(feed_kernel, block_order()),
        grid_spec=pltpu.PrefetchScalarGridSpec(
            num_scalar_prefetch=1,
            grid=(cols // TILE,),
            in_specs=[
                pl.BlockSpec((count, width), whole),
                pl.BlockSpec((count, width), whole),
                pl.BlockSpec(w_both.shape[:3] + (2 * TILE,), lambda i, rank: (0, 0, 0, i)),
                pl.BlockSpec((TILE, width), lambda i, rank: (i, 0)),
            ],
            out_specs=[
                pl.BlockSpec((count, TILE), column),
                pl.BlockSpec((count, 2 * TILE), column),
                pl.BlockSpec((count, width), whole),
            ],
            scratch_shapes=[pltpu.VMEM((width, 2 * TILE), BF), pltpu.VMEM((count, width), F32)],
        ),
        out_shape=[
            jax.ShapeDtypeStruct((count, cols), BF),
            jax.ShapeDtypeStruct((count, 2 * cols), BF),
            jax.ShapeDtypeStruct((count, width), BF),
        ],
        compiler_params=pltpu.CompilerParams(vmem_limit_bytes=44 * MIB),
        cost_estimate=CHEAP,
    )(rank_scalar(), x, cot, w_both, wd)


def gate_grad_kernel(order, rank_ref, x_ref, grad_ref, out_ref, xt_ref):
    rows = out_ref.shape[2]

    @pl.when(pl.program_id(0) == 0)
    def _():
        xt_ref[...] = x_ref[...].T

    result = dot_plain(xt_ref[...], grad_ref[...]).astype(BF)
    for index, (data, source) in enumerate(order):
        out_ref[data, source ^ rank_ref[0]] = result[index * rows : (index + 1) * rows]


def gate_grads(x, grads, shape):
    count, width = x.shape
    return pl.pallas_call(
        functools.partial(gate_grad_kernel, block_order()),
        grid_spec=pltpu.PrefetchScalarGridSpec(
            num_scalar_prefetch=1,
            grid=(grads.shape[1] // (2 * TILE),),
            in_specs=[
                pl.BlockSpec((count, width), lambda i, rank: (0, 0)),
                pl.BlockSpec((count, 2 * TILE), lambda i, rank: (0, i)),
            ],
            out_specs=pl.BlockSpec(shape[:3] + (2 * TILE,), lambda i, rank: (0, 0, 0, i)),
            scratch_shapes=[pltpu.VMEM((width, count), BF)],
        ),
        out_shape=jax.ShapeDtypeStruct(shape, BF),
        compiler_params=pltpu.CompilerParams(vmem_limit_bytes=VMEM_LIMIT),
        cost_estimate=CHEAP,
    )(rank_scalar(), x, grads)


def down_kernel(hid_ref, cot_ref, wd_ref, grad_ref, out_ref, acc_ref):
    step = pl.program_id(0)
    hidden = hid_ref[...]
    grad_ref[...] = dot_outer(hidden, cot_ref[...]).astype(BF)
    part = dot_plain(hidden, wd_ref[...])

    @pl.when(step == 0)
    def _():
        acc_ref[...] = part

    @pl.when(step > 0)
    def _():
        acc_ref[...] += part

    @pl.when(step == pl.num_programs(0) - 1)
    def _():
        out_ref[...] = acc_ref[...].astype(BF)


def down_grads(hidden, cot, wd):
    count, cols = hidden.shape
    width = wd.shape[1]
    tile = TILE
    whole = lambda i: (0, 0)
    return pl.pallas_call(
        down_kernel,
        grid=(cols // tile,),
        in_specs=[
            pl.BlockSpec((count, tile), lambda i: (0, i)),
            pl.BlockSpec((count, width), whole),
            pl.BlockSpec((tile, width), lambda i: (i, 0)),
        ],
        out_specs=[
            pl.BlockSpec((tile, width), lambda i: (i, 0)),
            pl.BlockSpec((count, width), whole),
        ],
        out_shape=[
            jax.ShapeDtypeStruct((cols, width), BF),
            jax.ShapeDtypeStruct((count, width), BF),
        ],
        scratch_shapes=[pltpu.VMEM((count, width), F32)],
        compiler_params=pltpu.CompilerParams(vmem_limit_bytes=VMEM_LIMIT),
        cost_estimate=CHEAP,
    )(hidden, cot, wd)


def per_device(
    inputs,
    cotangent,
    attn_gain,
    w_query,
    w_key,
    w_value,
    w_output,
    query_gain,
    key_gain,
    ffn_gain,
    w_gate,
    w_up,
    w_down,
    doc_starts,
):
    heads, mids = lax.axis_size("heads"), lax.axis_size("mid")
    his, los = lax.axis_size("hi"), lax.axis_size("lo")
    slots = heads * mids
    batches, _, rows, width = inputs.shape
    block = rows * heads
    count = slots * rows
    head_size = query_gain.shape[0]
    w_rows = w_query.shape[0]
    q_width = w_query.shape[1] // slots
    pairs = w_key.shape[1] // head_size // slots
    ff_width = w_gate.shape[1] // slots

    by_slot = lambda w: w.reshape(w_rows, slots, -1)
    kv_cols = jnp.stack(
        [
            w_key.reshape(w_rows, slots, pairs, head_size),
            w_value.reshape(w_rows, slots, pairs, head_size),
        ],
        axis=3,
    )
    qkv_parts = jnp.concatenate([by_slot(w_query), kv_cols.reshape(w_rows, slots, -1)], axis=2)
    qkv_mine = columns_out(qkv_parts.transpose(1, 0, 2))
    out_rows, down_rows = w_output.shape[0], w_down.shape[0]
    own_in, own_cot = inputs[:, 0], cotangent[:, 0]
    row_part = jnp.concatenate([w_output, w_down], axis=0)
    if is_quad():
        qkv_mine, own_in, row_part, doc_starts = together(qkv_mine, own_in, row_part, doc_starts)
        in_near = group_near(own_in)
    row_part = rows_out(row_part)
    qkv_all = gather_data(qkv_mine)
    fast = is_quad() and fast_rows(w_rows) and ff_width % TILE == 0

    head_at, mid_at = slot_places()
    row_at = jnp.arange(rows, dtype=jnp.int32)
    hi_at, lo_at = lax.axis_index("hi"), lax.axis_index("lo")
    first_pos = ((mid_at * los * block + head_at * rows)[:, None] + row_at[None, :]).reshape(count)
    row_pos = first_pos + hi_at * (mids * los * block) + lo_at * block
    lows = [lo_at] if los == 1 else [lo_at, 1 - lo_at]
    starts = doc_starts[:, None, :]
    row_begin = jnp.max(jnp.where(starts <= row_pos[None, :, None], starts, 0), axis=2)
    row_both = jnp.broadcast_to(row_pos[None], (batches, count))
    begin_low, begin_high = (
        jnp.min(row_begin, axis=1)[:, None],
        jnp.max(row_begin, axis=1)[:, None],
    )

    back = hi_at - jnp.arange(his, dtype=jnp.int32)[:, None]
    bases = back * (mids * los * block) + jnp.stack(lows)[None] * block
    key_low, key_high = (bases + jnp.min(first_pos))[:, None], (bases + jnp.max(first_pos))[:, None]
    none = (key_low > jnp.max(row_pos)) | (key_high < begin_low) | (back < 0)[:, None]
    full = (key_high <= jnp.min(row_pos)) & (key_low >= begin_high)
    codes = jnp.where(none, 0, jnp.where(full, 1, 2)).astype(jnp.int32)
    bases = bases.astype(jnp.int32)
    info_cols = jnp.stack([row_both, row_begin], axis=2)
    info_rows = jnp.stack([row_both, row_begin], axis=1)

    half = head_size // 2
    frequency = THETA ** (-(jnp.arange(half, dtype=F32) * 2.0 / head_size))
    turn_pos = (row_both - row_begin).reshape(batches, slots, rows).transpose(1, 0, 2)
    angles = turn_pos.reshape(-1).astype(F32)[:, None] * frequency[None, :]
    cos, sin = jnp.cos(angles), jnp.sin(angles)
    cos = jnp.concatenate([cos] * 4, axis=1)
    sin = jnp.concatenate([-sin, sin, -sin, sin], axis=1)
    q_gain = jnp.concatenate([query_gain, query_gain])[None]
    k_gain = jnp.concatenate([key_gain, key_gain])[None]

    if is_quad():
        *in_near, cos, sin, info_cols, info_rows, codes, bases = together(
            *in_near, cos, sin, info_cols, info_rows, codes, bases
        )
        in_far = group_far(*in_near)
        *in_far, qkv_all, row_part = together(*in_far, qkv_all, row_part)
        in_all, normed = group_joined(own_in, in_near, in_far, attn_gain)
    else:
        in_all = group_gather(own_in)
        in_wide = in_all.astype(F32)
        normed = (in_wide * rms_inverse(in_wide) * attn_gain).astype(BF)
    row_all = gather_data(row_part)
    w_qkv = natural_rows(qkv_all)
    normed = normed.reshape(-1, width)
    raw, query, kv = project(normed, w_qkv, cos, sin, q_gain, k_gain, q_width, head_size)
    query, w_gate, w_up = together(query, w_gate, w_up)
    if fast:
        gate_up_mine = jnp.stack(exchange_blocks(gate_up_blocks(w_gate, w_up)))
    else:
        gate_up_parts = jnp.concatenate([by_slot(w_gate), by_slot(w_up)], axis=2)
        gate_up_mine = columns_out(gate_up_parts.transpose(1, 0, 2))
    query = query.reshape(slots, batches, rows, q_width)
    moving = kv.reshape(slots, batches, rows, -1)
    kv_steps, state = [], ()
    for step in range(his):
        if step:
            moving = lax.ppermute(moving, "hi", [(i, i + 1) for i in range(step - 1, his - 1)])
            moving, *state = together(moving, *state)
        if step == his - 1:
            moving, gate_up_mine = together(moving, gate_up_mine)
            gate_up_all = gather_data(gate_up_mine)
        kv_steps.append([moving] if los == 1 else [moving, other_low(moving)])
        state = attend(
            codes[step],
            bases[step],
            query,
            kv_steps[step],
            info_cols,
            first_pos[None],
            tuple(state),
            step == his - 1,
            head_size,
        )
        state = list(state)
        if not is_quad():
            continue
        if step == 0:
            gate_up_mine, state[0], cot_own = together(gate_up_mine, state[0], own_cot)
            cot_near = group_near(cot_own)
        if step == 1:
            *cot_near, row_all, state[0] = together(*cot_near, row_all, state[0])
            cot_far = group_far(*cot_near)
            wo_part = row_all[:, :out_rows].reshape(-1, width)
            wd_use = row_all[:, out_rows:].reshape(-1, width)
            wo_near = group_near(wo_part)
        if step == 2:
            *cot_far, state[0] = together(*cot_far, state[0])
            *wo_near, wd_use, state[0] = together(*wo_near, wd_use, state[0])
            wo_far = group_far(*wo_near)
            cot_all = group_joined(cot_own, cot_near, cot_far)
        if step == 3:
            *wo_far, cot_all, state[1] = together(*wo_far, cot_all, state[1])
            wo_full = group_joined(wo_part, wo_near, wo_far)
    exact, attn, lse = state
    if not is_quad():
        cot_all = group_gather(own_cot)
        wo_full = group_gather(row_all[:, :out_rows].reshape(-1, width))
        wd_use = row_all[:, out_rows:].reshape(-1, width)
    wo_full = wo_full.reshape(-1, width)
    attn_wide = columns_out_async(attn.reshape(slots, batches * rows, q_width))
    attn_wide = jnp.concatenate([attn_wide[slot] for slot in range(slots)], axis=1)
    middle = own_in.reshape(-1, width).astype(F32) + dot_plain(attn_wide, wo_full)

    normed_two = (middle * rms_inverse(middle) * ffn_gain).astype(BF)
    normed_two_all = group_gather(normed_two).reshape(-1, width)
    normed_two_all, gate_up_all = together(normed_two_all, gate_up_all)
    cot_rows = cot_all.reshape(-1, width)
    if fast:
        hidden, grads, grad_two = feed(normed_two_all, cot_rows, gate_up_all, wd_use)
        grad_two, grads, hidden = together(grad_two, grads, hidden)
        grad_gate_up = gate_grads(normed_two_all, grads, gate_up_all.shape)
        grad_gate_up = grad_gate_up.reshape(his * los, slots * w_rows, -1)
        grad_down, out_part = down_grads(hidden, cot_rows, wd_use)
    else:
        w_both = natural_rows(gate_up_all)
        both = dot_plain(normed_two_all, w_both)
        gate, upper = both[:, :ff_width], both[:, ff_width:]
        grad_hidden = dot_back(cot_rows, wd_use)
        sigmoid = jax.nn.sigmoid(gate)
        silu = gate * sigmoid
        hidden = (silu * upper).astype(BF)
        grad_gate = grad_hidden * upper * sigmoid * (1.0 + gate * (1.0 - sigmoid))
        grads = jnp.concatenate([grad_gate, grad_hidden * silu], axis=1).astype(BF)
        grad_two = dot_back(grads, w_both).astype(BF)
        grad_gate_up = scatter_order(dot_outer(normed_two_all, grads).astype(BF), w_rows)
        grad_down = dot_outer(hidden, cot_rows).astype(BF)
        out_part = dot_plain(hidden, wd_use).astype(BF)
    in_slots = lambda total: total.reshape(slots, batches * rows, width)
    out_part = in_slots(out_part)
    two_sum = GroupSum(in_slots(grad_two))
    (grad_gate_up,) = two_sum.second(grad_gate_up)
    grad_down, out_part = two_sum.hold(grad_down, out_part)
    grad_two = two_sum.done()
    gate_up_sum = scatter_data(grad_gate_up).reshape(slots, w_rows, -1)
    grad_mid_part, _ = norm_back(middle, ffn_gain, grad_two)
    grad_middle = own_cot.reshape(-1, width).astype(F32) + grad_mid_part

    grad_middle_low = grad_middle.astype(BF)
    grad_attn = dot_back(grad_middle_low, wo_full).astype(BF)
    grad_attn = jnp.stack(
        [grad_attn[:, slot * q_width : (slot + 1) * q_width] for slot in range(slots)]
    )
    grad_attn, grad_middle_low = together(grad_attn, grad_middle_low)
    grad_output = dot_outer(attn_wide, grad_middle_low)
    grad_output = grad_output.astype(BF).reshape(slots, -1, width)
    grad_attn = columns_out_async(grad_attn).reshape(query.shape)
    first_sum = GroupSum(grad_output)
    state, moving = (), None
    for turn in range(1, his + 1):
        step = his - turn
        *dkv, state_out = attend_back(
            codes[step],
            bases[step],
            query,
            grad_attn,
            exact,
            lse,
            kv_steps[step],
            info_rows,
            first_pos[:, None],
            state,
            turn == his,
            head_size,
        )
        if turn > 1:
            *dkv, moving = together(*dkv, moving)
        if turn == 1:
            dkv = first_sum.second(*dkv)
        if turn == min(2, his):
            dkv = first_sum.hold(*dkv)
            out_part, *dkv = together(out_part, *dkv)
            second_sum = GroupSum(out_part)
        if turn == min(3, his):
            dkv = second_sum.second(*dkv)
            dkv = first_sum.hold(*dkv)
            output_part, gate_up_sum = together(first_sum.done().astype(BF), gate_up_sum)
            row_grads = jnp.concatenate(
                [
                    output_part.reshape(his * los, out_rows, width),
                    grad_down.reshape(his * los, down_rows, width),
                ],
                axis=1,
            )
        if turn == min(4, his):
            dkv = second_sum.hold(*dkv)
            row_sum = scatter_data(row_grads)
        parts = [dkv[0]] + ([other_low(dkv[1])] if los == 2 else [])
        parts += [moving] if turn > 1 else []
        if turn < his:
            low, state_out = together(low_sum(*parts), state_out)
            moving = lax.ppermute(low, "hi", [(i, i - 1) for i in range(his - turn, his)])
        state = (state_out,)
    out_sum = second_sum.done()
    dkv_mine = sum(part.astype(F32) for part in parts)
    dq = state[0]
    grad_raw, head_gains = unproject(
        raw,
        dq.reshape(-1, q_width),
        dkv_mine.reshape(raw.shape[0], -1),
        cos,
        sin,
        q_gain,
        k_gain,
        head_size,
    )
    block_out = (middle + out_sum).astype(BF)
    grad_qkv = dot_outer(normed, grad_raw).astype(BF)
    head_sums = jnp.sum(head_gains, axis=0).reshape(2, 2, head_size).sum(axis=1)
    in_wide = in_all.reshape(-1, width).astype(F32)
    normed_back = lambda grads: dot_back(grads, w_qkv).astype(BF)
    gain_vector = lambda low, grad_two, middle: jnp.concatenate(
        [
            jnp.sum(low.astype(F32) * in_wide * rms_inverse(in_wide), axis=0),
            jnp.sum(grad_two * middle * rms_inverse(middle), axis=0),
            head_sums[0],
            head_sums[1],
        ]
    )
    into_slots = lambda low: low.reshape(slots, batches * rows, width)
    if fast:
        own_part, other_part = unplaced(grad_qkv, w_rows, True)
        own_part, other_part, grad_raw = together(own_part, other_part, grad_raw)
        other_part = other_low(other_part)
        grad_normed_low = normed_back(grad_raw)
        other_part, grad_normed_low, gate_up_sum, grad_two, middle = together(
            other_part, grad_normed_low, gate_up_sum, grad_two, middle
        )
        summed = low_sum(own_part, other_part)
        normed_sum = GroupSum(into_slots(grad_normed_low))
        gains = gain_vector(grad_normed_low, grad_two, middle)
        stages = sum_stages()
        moving = None
        for step in range(1, his):
            moving = ring(summed[step] if moving is None else low_sum(summed[step], moving), 1)
            if step == 1:
                moving, gains = normed_sum.second(moving, gains)
                gate_up_back = exchange_blocks([gate_up_sum[slot] for slot in range(4)])
            else:
                gains = stages.pop(0)(gains)
                moving, gains = together(moving, gains)
            if step == his - 1:
                moving, gains = normed_sum.hold(moving, gains)
                moving, row_sum, *gate_up_back = together(moving, row_sum, *gate_up_back)
        qkv_sum = low_sum(summed[0], moving) if his > 1 else summed[0]
        qkv_cols, row_back = columns_out(qkv_sum), rows_back(row_sum)
        for stage in stages:
            gains = stage(gains)
        qkv_cols, row_back = together(qkv_cols, row_back)
    else:
        gate_up_back = [columns_out(gate_up_sum)]
        grad_qkv = scatter_order(grad_qkv, w_rows)
        qkv_cols = columns_out(scatter_data(grad_qkv).reshape(slots, w_rows, -1))
        grad_normed_low = normed_back(grad_raw)
        gains = all_sum(gain_vector(grad_normed_low, grad_two, middle))
        normed_sum = GroupSum(into_slots(grad_normed_low))
        normed_sum.second()
        row_back = rows_back(row_sum)
    grad_normed = normed_sum.done()
    row_back = row_back.astype(F32)
    grad_in_part, _ = norm_back(own_in.reshape(-1, width).astype(F32), attn_gain, grad_normed)
    grad_inputs = grad_middle + grad_in_part

    qkv_cols = qkv_cols.transpose(1, 0, 2).astype(F32)
    if fast:
        gate_cols, up_cols = gate_up_merge(gate_up_back)
    else:
        gate_cols, up_cols = jnp.split(gate_up_back[0].transpose(1, 0, 2).astype(F32), 2, axis=2)
    kv_sums = qkv_cols[:, :, q_width:].reshape(w_rows, slots, pairs, 2, head_size)
    return (
        block_out.reshape(batches, 1, rows, width),
        grad_inputs.reshape(batches, 1, rows, width),
        gains[:width],
        qkv_cols[:, :, :q_width].reshape(w_rows, -1),
        kv_sums[:, :, :, 0].reshape(w_rows, -1),
        kv_sums[:, :, :, 1].reshape(w_rows, -1),
        row_back[:out_rows],
        gains[2 * width : 2 * width + head_size],
        gains[2 * width + head_size :],
        gains[width : 2 * width],
        gate_cols.reshape(w_rows, -1),
        up_cols.reshape(w_rows, -1),
        row_back[out_rows:],
    )


def solution(mesh):
    heads, seq = mesh.shape["heads"], mesh.shape["seq"]
    rows_spec = P(None, SEQ, "heads", None)
    weight_spec = P(ALL, None)

    def run(*args):
        kv_heads = args[4].shape[1] // args[7].shape[0]
        low = 2 if seq % 2 == 0 else 1
        mid = 2 if seq % (2 * low) == 0 and kv_heads % (2 * heads) == 0 else 1
        split = Mesh(
            mesh.devices.reshape(heads, seq // (mid * low), mid, low), ("heads",) + SEQ
        )
        return jax.shard_map(
            per_device,
            mesh=split,
            in_specs=(
                (rows_spec, rows_spec, P())
                + (weight_spec,) * 4
                + (P(), P(), P())
                + (weight_spec,) * 3
                + (P(),)
            ),
            out_specs=(
                (rows_spec, rows_spec, P())
                + (weight_spec,) * 4
                + (P(), P(), P())
                + (weight_spec,) * 3
            ),
            check_vma=False,
        )(*args)

    return run
```
